32 devices in a mesh: dp: 8 (over z, y), head: 4 (over x, core).
Axes of the slice: x: 2, y: 2, z: 4, core: 2. Of those that a mesh axis runs over, the one named last changes fastest.
Arguments:
- inputs: bfloat16 [8192, 768], P('dp'), may hold values from -6 to 6
- seg_lengths: int32 [8, 4], P('dp'), may hold values from 1 to 512, 1024 in all within a row
- cotangent: bfloat16 [8192, 768], P('dp'), may hold values from -6 to 6
- qkv_weight: float32 [3, 768, 768], P(None, 'dp', 'head'), may hold values from -0.21875 to 0.21875
- qkv_moment: float32 [3, 768, 768], P(None, 'dp', 'head'), may hold values from -256 to 256
- qkv_average: float32 [3, 768, 768], P(None, 'dp', 'head'), may hold values from -0.21875 to 0.21875
- out_weight: float32 [768, 768], P('head', 'dp'), may hold values from -2 to 2
- out_moment: float32 [768, 768], P('head', 'dp'), may hold values from -32 to 32
- out_average: float32 [768, 768], P('head', 'dp'), may hold values from -2 to 2
- up_weight: float32 [768, 3072], P('dp', 'head'), may hold values from -0.21875 to 0.21875
- up_moment: float32 [768, 3072], P('dp', 'head'), may hold values from -192 to 192
- up_average: float32 [768, 3072], P('dp', 'head'), may hold values from -0.21875 to 0.21875
- down_weight: float32 [3072, 768], P('head', 'dp'), may hold values from -0.109375 to 0.109375
- down_moment: float32 [3072, 768], P('head', 'dp'), may hold values from -224 to 224
- down_average: float32 [3072, 768], P('head', 'dp'), may hold values from -0.109375 to 0.109375
- rel_table: float32 [512, 768], P(('dp', 'head')), may hold values from -6 to 6
- table_moment: float32 [512, 768], P(('dp', 'head')), may hold values from -16 to 16
- table_average: float32 [512, 768], P(('dp', 'head')), may hold values from -6 to 6
- vectors: float32 [11520], P(('dp', 'head')), may hold values from -1.5 to 1.75, as said below
- vector_moment: float32 [11520], P(('dp', 'head')), may hold values from -256 to 256
- vector_average: float32 [11520], P(('dp', 'head')), may hold values from -1.5 to 1.75
Outputs:
- output: bfloat16 [8192, 768], P(('dp', 'head'))
- input_grad: float32 [8192, 768], P(('dp', 'head'))
- qkv_new: float32 [3, 768, 768], P(None, 'dp', 'head')
- qkv_moment_new: float32 [3, 768, 768], P(None, 'dp', 'head')
- qkv_average_new: float32 [3, 768, 768], P(None, 'dp', 'head')
- out_new: float32 [768, 768], P('head', 'dp')
- out_moment_new: float32 [768, 768], P('head', 'dp')
- out_average_new: float32 [768, 768], P('head', 'dp')
- up_new: float32 [768, 3072], P('dp', 'head')
- up_moment_new: float32 [768, 3072], P('dp', 'head')
- up_average_new: float32 [768, 3072], P('dp', 'head')
- down_new: float32 [3072, 768], P('head', 'dp')
- down_moment_new: float32 [3072, 768], P('head', 'dp')
- down_average_new: float32 [3072, 768], P('head', 'dp')
- table_new: float32 [512, 768], P(('dp', 'head'))
- table_moment_new: float32 [512, 768], P(('dp', 'head'))
- table_average_new: float32 [512, 768], P(('dp', 'head'))
- vector_new: float32 [11520], P(('dp', 'head'))
- vector_moment_new: float32 [11520], P(('dp', 'head'))
- vector_average_new: float32 [11520], P(('dp', 'head'))
The draws below stay inside these ranges and needn't reach their ends.
Inputs may be any that keep to these rules, and one draw needn't show every extreme that they name: `seg_lengths`: each row sums to 1024; each row holds one sequence of exactly 512 tokens. `vectors`: the three gains lie in [0.25, 1.75].
All inputs are finite; a program needn't handle non-finite values.
Results may differ from the reference program's by a relative error of at most 0.02.
Values may be sent and summed in bfloat16 or wider, within the bound.
No kernel may reach another device: no remote copies, remote signals or barrier semaphores. Data moves between devices by JAX's collectives and lax.ppermute only.
A program may use at most 448 MiB of HBM per device.

```python
import math
import jax
import jax.numpy as jnp
import numpy as np
from jax import lax

D = 768
HEADS = 12
HD = 64
FF = 3072
BUCKETS = 256
MAXLEN = 512
TOK_DEV = 1024
SEGS = 4
TOKENS = 8192
TABLE = 512
VEC = 11520
N_DP = 8


def vector_values(key):
    position = jnp.arange(VEC)
    row_of = position // D
    is_gain = ((row_of == 0) | (row_of == 2) | (row_of == 4)) & (position < 11 * D)
    random_part = jax.random.truncated_normal(key, -5.0, 5.0, (VEC,), jnp.float32)
    return jnp.where(is_gain, 1.0 + 0.15 * random_part, 0.3 * random_part)


def draw_vectors(key, part):
    return vector_values(jax.random.fold_in(key, 11))


def draw_vector_average(key, part):
    return vector_values(jax.random.fold_in(key, 23))


def steps_of(key, shape, shards, low, largest):
    def one(dim, parts):
        heights = jax.random.uniform(jax.random.fold_in(jax.random.fold_in(key, 6), dim), (parts,), jnp.float32, low / len(shards), largest / len(shards))
        return jnp.repeat(jnp.exp(heights), shape[dim] // parts).reshape((-1,) + (1,) * (len(shape) - dim - 1))

    loudness = one(*shards[0])
    for cut in shards[1:]:
        loudness = loudness * one(*cut)
    return loudness


def length_profile(amount, total, bound, lean):
    weights = [(1 << 20) // math.isqrt(grade ** lean) + 1 for grade in range(2, amount + 1)]
    surplus, given = total - bound - (amount - 1), [1] * (amount - 1)
    while surplus > 0:
        free = [i for i in range(amount - 1) if given[i] < bound]
        whole, remaining = sum([weights[i] for i in free]), surplus
        for i in free:
            addition = min(bound - given[i], max(1, remaining * weights[i] // whole), surplus)
            given[i] = given[i] + addition
            surplus = surplus - addition
    return np.array([bound] + given)


def ragged(stream_key, amount, total, limit, skew):
    if amount == 2:
        one = jax.random.randint(stream_key, (), max(1, total - limit), min(limit, total - 1) + 1)
        return jnp.stack([one, total - one])
    sizes = jnp.asarray(length_profile(amount, total, limit, skew), jnp.int32)
    pairs = (amount - 1) // 2
    giver, sink = sizes[1:1 + 2 * pairs:2], sizes[2:2 + 2 * pairs:2]
    room = jnp.minimum(giver - 1, limit - sink)
    moved = jax.random.randint(jax.random.fold_in(stream_key, 1), (pairs,), 0, 1 << 20) % (room + 1)
    sizes = sizes.at[1:1 + 2 * pairs:2].set(giver - moved).at[2:2 + 2 * pairs:2].set(sink + moved)
    return sizes[jax.random.permutation(jax.random.fold_in(stream_key, 2), amount)]


def scatter_about(key, extent, width, most, cuts=(), kind=jnp.bfloat16):
    values = width * jax.random.normal(key, extent, jnp.float32)
    if cuts:
        values = values * steps_of(key, extent, cuts, -0.22, 0.18)
    return jnp.clip(values, -most, most).astype(kind)


def setup_inputs(seed: int = 0) -> dict:
    splits = jax.random.split(jax.random.key(seed), 22)
    return {
        "inputs": scatter_about(splits[0], (TOKENS, D), 1.0, 6.0, ((0, 8),)),
        "seg_lengths": jax.vmap(lambda own: ragged(own, SEGS, TOK_DEV, MAXLEN, 2))(jax.random.split(splits[1], N_DP)).reshape((N_DP, SEGS)).astype(jnp.int32),
        "cotangent": scatter_about(splits[2], (TOKENS, D), 1.0, 6.0, ((0, 8),)),
        "qkv_weight": scatter_about(splits[3], (3, D, D), D ** -0.5, 0.21875, ((1, 8), (2, 4)), jnp.float32),
        "qkv_moment": scatter_about(splits[4], (3, D, D), (0.5 * TOKENS ** 0.5), 256.0, ((1, 8), (2, 4)), jnp.float32),
        "qkv_average": scatter_about(splits[5], (3, D, D), D ** -0.5, 0.21875, ((1, 8), (2, 4)), jnp.float32),
        "out_weight": scatter_about(splits[6], (D, D), (6 * D // MAXLEN) ** -0.5, 2.0, ((0, 4), (1, 8)), jnp.float32),
        "out_moment": scatter_about(splits[7], (D, D), (1.3 * (TOKENS // MAXLEN) ** 0.5), 32.0, ((0, 4), (1, 8)), jnp.float32),
        "out_average": scatter_about(splits[8], (D, D), (6 * D // MAXLEN) ** -0.5, 2.0, ((0, 4), (1, 8)), jnp.float32),
        "up_weight": scatter_about(splits[9], (D, FF), D ** -0.5, 0.21875, ((0, 8), (1, 4)), jnp.float32),
        "up_moment": scatter_about(splits[10], (D, FF), (0.35 * TOKENS ** 0.5), 192.0, ((0, 8), (1, 4)), jnp.float32),
        "up_average": scatter_about(splits[11], (D, FF), D ** -0.5, 0.21875, ((0, 8), (1, 4)), jnp.float32),
        "down_weight": scatter_about(splits[12], (FF, D), FF ** -0.5, 0.109375, ((0, 4), (1, 8)), jnp.float32),
        "down_moment": scatter_about(splits[13], (FF, D), (0.4 * TOKENS ** 0.5), 224.0, ((0, 4), (1, 8)), jnp.float32),
        "down_average": scatter_about(splits[14], (FF, D), FF ** -0.5, 0.109375, ((0, 4), (1, 8)), jnp.float32),
        "rel_table": scatter_about(splits[15], (TABLE, D), 1.0, 6.0, ((0, 32),), jnp.float32),
        "table_moment": scatter_about(splits[16], (TABLE, D), (0.7 * (TOKENS // MAXLEN) ** 0.5), 16.0, ((0, 32),), jnp.float32),
        "table_average": scatter_about(splits[17], (TABLE, D), 1.0, 6.0, ((0, 32),), jnp.float32),
        "vectors": draw_vectors(jax.random.fold_in(splits[21], 71), 0),
        "vector_moment": scatter_about(splits[19], (VEC,), (0.5 * TOKENS ** 0.5), 256.0, ((0, 32),), jnp.float32),
        "vector_average": draw_vector_average(jax.random.fold_in(splits[21], 71), 0),
    }


EPSILON = 1e-07
MOMENTUM = 0.9
DECAY = 0.01
AVERAGE = 0.7
MASKED = -1e+30
HIGHEST = lax.Precision.HIGHEST

@jax.custom_vjp
def low(v):
    return lax.optimization_barrier(v.astype(jnp.bfloat16)).astype(jnp.float32)

@jax.custom_vjp
def low_back(v):
    return v

def low_keep(v):
    return (low(v), None)

def low_pass(kept, grad):
    return (grad,)

def back_keep(v):
    return (v, None)

def back_low(kept, grad):
    return (low(grad),)
low.defvjp(low_keep, low_pass)
low_back.defvjp(back_keep, back_low)

def bucket_of(offset, buckets, longest):
    middle = buckets // 2
    distance = middle - 1 if abs(offset) < middle else abs(offset)
    sign_of = 1 if offset > 0 else -1 if offset < 0 else 0
    far_bucket = math.ceil(math.log(distance / middle) / math.log((longest - 1) / middle) * (middle - 1)) + middle
    bucket = offset if distance <= middle else sign_of * far_bucket
    return min(max(bucket + buckets, 0), 2 * buckets - 1)

def bucket_table(token_count, buckets, longest):
    values = [bucket_of(offset, buckets, longest) for offset in range(-(token_count - 1), token_count)]
    return np.array(values, dtype=np.int32)

def pair_table(token_count, buckets, longest):
    relative = bucket_table(token_count, buckets, longest)
    places = np.arange(token_count)
    return relative[places[:, None] - places[None, :] + token_count - 1].astype(np.int32)

def layer_norm(values, gain_term, bias_term):
    center = values - lax.optimization_barrier(jnp.mean(values, axis=-1, keepdims=True))
    spread = lax.optimization_barrier(jnp.mean(center * center, axis=-1, keepdims=True))
    return center * lax.rsqrt(spread + EPSILON) * gain_term + bias_term

def nesterov(weight, moment, average, gradient, step_rate):
    decayed = gradient + DECAY * weight
    moment_new = MOMENTUM * moment + decayed
    weight_new = weight - step_rate * (decayed + MOMENTUM * moment_new)
    average_new = AVERAGE * average + (1.0 - AVERAGE) * weight_new
    return (weight_new, moment_new, average_new)

def product(left, right):
    return jnp.dot(left, right, precision=HIGHEST, preferred_element_type=jnp.float32)

def split_heads(matrix):
    return matrix.reshape(matrix.shape[0], HEADS, HD)

def layer_forward(inputs, seg_lengths, qkv_weight, out_weight, up_weight, down_weight, rel_table, vectors):
    vector_rows = vectors[:11 * D].reshape(11, D)
    bias_up = vectors[11 * D:]
    w_query = low(qkv_weight[0])
    w_key = low(qkv_weight[1])
    w_value = low(qkv_weight[2])
    w_output = low(out_weight)
    w_upward = low(up_weight)
    w_downward = low(down_weight)
    normed = low(layer_norm(rel_table, vector_rows[4], vector_rows[5]))
    key_table = split_heads(low_back(low(product(normed, w_key) + vector_rows[9])))
    query_table = split_heads(low_back(low(product(normed, w_query) + vector_rows[8])))
    pair_index = jnp.asarray(pair_table(TOK_DEV, BUCKETS, MAXLEN))
    block_rows = min(512, TOK_DEV)
    starts = jnp.arange(TOK_DEV // block_rows, dtype=jnp.int32) * block_rows
    score_scale = (3.0 * HD) ** (-0.5)

    def row_forward(row_inputs, row_lengths):
        segment_ends = jnp.cumsum(row_lengths).astype(jnp.int32)
        places = jnp.arange(TOK_DEV, dtype=jnp.int32)
        segment = lax.optimization_barrier(jnp.sum((places[:, None] >= segment_ends[None, :]).astype(jnp.int32), axis=1)).astype(jnp.int32)
        query_rows = split_heads(low_back(low(product(row_inputs, w_query) + vector_rows[8])))
        key_rows = split_heads(low_back(low(product(row_inputs, w_key) + vector_rows[9])))
        value_rows = split_heads(low_back(low(product(row_inputs, w_value) + vector_rows[10])))
        c2p_all = low_back(jnp.einsum('qhd,bhd->hqb', query_rows, key_table, precision=HIGHEST, preferred_element_type=jnp.float32))
        p2c_all = low_back(jnp.einsum('khd,bhd->hkb', key_rows, query_table, precision=HIGHEST, preferred_element_type=jnp.float32))

        def block_context(block_start):
            query_block = lax.dynamic_slice_in_dim(query_rows, block_start, block_rows, 0)
            c2p_block = lax.dynamic_slice_in_dim(c2p_all, block_start, block_rows, 1)
            pair_rows = lax.dynamic_slice_in_dim(pair_index, block_start, block_rows, 0)
            pair_cols = lax.dynamic_slice_in_dim(pair_index, block_start, block_rows, 1)
            raw_scores = jnp.einsum('qhd,khd->hqk', query_block, key_rows, precision=HIGHEST, preferred_element_type=jnp.float32)
            raw_scores = raw_scores + jnp.take_along_axis(c2p_block, jnp.broadcast_to(pair_rows[None], (HEADS, block_rows, TOK_DEV)), axis=2)
            raw_scores = raw_scores + jnp.swapaxes(jnp.take_along_axis(p2c_all, jnp.broadcast_to(pair_cols[None], (HEADS, TOK_DEV, block_rows)), axis=2), 1, 2)
            segment_block = lax.dynamic_slice_in_dim(segment, block_start, block_rows, 0)
            same_segment = segment_block[:, None] == segment[None, :]
            scores = jnp.where(same_segment[None], score_scale * low_back(raw_scores), MASKED)
            row_max = lax.optimization_barrier(jnp.max(scores, axis=-1, keepdims=True))
            exp_scores = jnp.exp(scores - row_max)
            probabilities = exp_scores / lax.optimization_barrier(jnp.sum(exp_scores, axis=-1, keepdims=True))
            return jnp.einsum('hqk,khd->qhd', low(probabilities), value_rows, precision=HIGHEST, preferred_element_type=jnp.float32)
        context = lax.map(jax.checkpoint(block_context), starts).reshape(TOK_DEV, D)
        context = low_back(low(context))
        attention = low_back(product(context, w_output))
        first_norm = layer_norm(row_inputs + attention + vector_rows[6], vector_rows[0], vector_rows[1])
        upward = low_back(product(low(first_norm), w_upward) + bias_up)
        hidden = low(jax.nn.gelu(upward, approximate=False))
        downward = low_back(product(hidden, w_downward))
        return layer_norm(first_norm + downward + vector_rows[7], vector_rows[2], vector_rows[3])

    def scan_step(carried, row_pair):
        return (carried, row_forward(row_pair[0], row_pair[1]))
    _, results = lax.scan(jax.checkpoint(scan_step), None, (inputs.reshape(N_DP, TOK_DEV, D), seg_lengths))
    return results.reshape(TOKENS, D)

def reference(inputs, seg_lengths, cotangent, qkv_weight, qkv_moment, qkv_average, out_weight, out_moment, out_average, up_weight, up_moment, up_average, down_weight, down_moment, down_average, rel_table, table_moment, table_average, vectors, vector_moment, vector_average):

    def forward(input_rows, qkv_param, out_param, up_param, down_param, table_param, vector_param):
        return layer_forward(input_rows, seg_lengths, qkv_param, out_param, up_param, down_param, table_param, vector_param)
    result, pullback = jax.vjp(forward, inputs.astype(jnp.float32), qkv_weight, out_weight, up_weight, down_weight, rel_table, vectors)
    gradients = pullback(cotangent.astype(jnp.float32))
    new_qkv = nesterov(qkv_weight, qkv_moment, qkv_average, gradients[1], 0.75 / math.sqrt(D * TOKENS))
    new_out = nesterov(out_weight, out_moment, out_average, gradients[2], 0.125 * MAXLEN / math.sqrt(D * TOKENS))
    new_up = nesterov(up_weight, up_moment, up_average, gradients[3], 1.1 / math.sqrt(D * TOKENS))
    new_down = nesterov(down_weight, down_moment, down_average, gradients[4], 1.0 / math.sqrt(FF * TOKENS))
    new_table = nesterov(rel_table, table_moment, table_average, gradients[5], 0.55 * math.sqrt(MAXLEN / TOKENS))
    new_vector = nesterov(vectors, vector_moment, vector_average, gradients[6], 0.3 / math.sqrt(TOKENS))
    return (result.astype(jnp.bfloat16), gradients[0], new_qkv[0], new_qkv[1], new_qkv[2], new_out[0], new_out[1], new_out[2], new_up[0], new_up[1], new_up[2], new_down[0], new_down[1], new_down[2], new_table[0], new_table[1], new_table[2], new_vector[0], new_vector[1], new_vector[2])
```

```python
import functools
import math

import jax
import jax.numpy as jnp
import numpy as np
from jax import lax
from jax.experimental import pallas as pl
from jax.experimental.pallas import tpu as pltpu
from jax.sharding import PartitionSpec as P

D = 768
HEADS = 12
HD = 64
FF = 3072
BUCKETS = 256
MAXLEN = 512

EPSILON = 1e-07
MOMENTUM = 0.9
DECAY = 0.01
AVERAGE = 0.7
MASKED = -1e30

TILE = 128
NARROW = 5
SCALE = (3.0 * HD) ** -0.5
LOG2E = math.log2(math.e)
HALF = jnp.bfloat16
FULL = jnp.float32
NN = (((1,), (0,)), ((), ()))
NT = (((1,), (1,)), ((), ()))
TN = (((0,), (0,)), ((), ()))


def dot(left, right, dims=NN):
    return lax.dot_general(left, right, dims, preferred_element_type=FULL)


def shear(values, count, low):
    rolled = [
        pltpu.roll(values[:, m * TILE : (m + 1) * TILE], 1, 1, stride=1, stride_axis=0)
        for m in range(count + 1)
    ]
    return jnp.concatenate(
        [jnp.where(low, rolled[m], rolled[m + 1]) for m in range(count)], axis=1
    )


def unshear(values, count, after):
    rolled = [
        pltpu.roll(values[:, m * TILE : (m + 1) * TILE], 0, 1, stride=1, stride_axis=0)
        for m in range(count)
    ]
    zero = jnp.zeros((TILE, TILE), values.dtype)
    return jnp.concatenate(
        [
            jnp.where(
                after, rolled[m] if m < count else zero, rolled[m - 1] if m > 0 else zero
            ).astype(HALF)
            for m in range(count + 1)
        ],
        axis=1,
    )


def flip_matrix():
    across = lax.broadcasted_iota(jnp.int32, (TILE, TILE), 1)
    down = lax.broadcasted_iota(jnp.int32, (TILE, TILE), 0)
    return (across + down == TILE - 1).astype(FULL).astype(HALF)


def tiles_of(block, count=1):
    return pl.ds(pl.multiple_of(block * TILE, TILE), count * TILE)


def sequence_bounds(lengths, first, last):
    total, start, stop = jnp.int32(0), jnp.int32(0), jnp.int32(0)
    for s in range(lengths.shape[0]):
        begin = total
        total = total + lengths[s]
        start = jnp.where((begin <= first) & (first < total), begin, start)
        stop = jnp.where((begin <= last) & (last < total), total, stop)
    return start, stop


def by_window(lengths, block, tiles, body):
    start, stop = sequence_bounds(lengths, block * TILE, block * TILE + TILE - 1)
    first = start // TILE
    narrow = min(NARROW, tiles)
    fits = (stop + TILE - 1) // TILE - first <= narrow

    @pl.when(fits)
    def _():
        body(narrow, jnp.minimum(first, tiles - narrow))

    @pl.when(jnp.logical_not(fits))
    def _():
        body(tiles, jnp.int32(0))


def forward_kernel(
    lengths, q_ref, k_ref, v_ref, kb_ref, qb_ref, row_ref, col_ref, ctx_ref, p_ref, p2c_ref
):
    heads, tiles = q_ref.shape[0], q_ref.shape[1] // TILE
    across = lax.broadcasted_iota(jnp.int32, (TILE, TILE), 1)
    down = lax.broadcasted_iota(jnp.int32, (TILE, TILE), 0)
    low = across <= down
    flip = flip_matrix()

    def p2c_block(block, carried):
        rows = tiles_of(block)

        def body(count, first):
            offsets = tiles_of(first - block + tiles - 1, count + 1)
            for h in range(heads):
                sheared = shear(dot(k_ref[h, rows, :], qb_ref[h, offsets, :], NT), count, low)
                for m in range(count):
                    p2c_ref[h, tiles_of(first + m), rows] = sheared[
                        :, m * TILE : (m + 1) * TILE
                    ].T

        by_window(lengths, block, tiles, body)
        return carried

    lax.fori_loop(0, tiles, p2c_block, 0)

    def score_block(block, carried):
        rows = tiles_of(block)

        def body(count, first):
            cols = tiles_of(first, count)
            offsets = tiles_of(first - block + tiles - 1, count + 1)
            same = col_ref[rows, :1] == row_ref[:1, cols]
            for h in range(heads):
                query = q_ref[h, rows, :]
                c2p = shear(dot(query, kb_ref[h, offsets, :], NT), count, low)
                raw = dot(query, k_ref[h, cols, :], NT) + c2p + p2c_ref[h, rows, cols]
                scores = jnp.where(same, (SCALE * LOG2E) * raw, MASKED)
                powers = jnp.exp2(scores - jnp.max(scores, axis=1, keepdims=True))
                probs = (powers * (1.0 / jnp.sum(powers, axis=1, keepdims=True))).astype(HALF)
                for m in range(count):
                    p_ref[h, rows, tiles_of(tiles - 1 - first - m)] = dot(
                        probs[:, m * TILE : (m + 1) * TILE], flip
                    ).astype(HALF)
                ctx_ref[h, rows, :] = dot(probs, v_ref[h, cols, :]).astype(HALF)

        by_window(lengths, block, tiles, body)
        return carried

    lax.fori_loop(0, tiles, score_block, 0)


def backward_kernel(
    lengths,
    q_ref,
    k_ref,
    v_ref,
    kbs_ref,
    qbs_ref,
    p_ref,
    g_ref,
    dq_ref,
    dk_ref,
    dv_ref,
    gkb_ref,
    gqb_ref,
    dst_ref,
    krev_ref,
    vrev_ref,
    dvt_ref,
):
    heads, tiles = q_ref.shape[0], q_ref.shape[1] // TILE
    across = lax.broadcasted_iota(jnp.int32, (TILE, TILE), 1)
    down = lax.broadcasted_iota(jnp.int32, (TILE, TILE), 0)
    after = across >= down
    flip = flip_matrix()
    dst_ref[...] = jnp.zeros_like(dst_ref)
    dvt_ref[...] = jnp.zeros_like(dvt_ref)
    gkb_ref[...] = jnp.zeros_like(gkb_ref)
    gqb_ref[...] = jnp.zeros_like(gqb_ref)
    for h in range(heads):
        for m in range(tiles):
            here, there = slice(m * TILE, (m + 1) * TILE), slice((tiles - 1 - m) * TILE, (tiles - m) * TILE)
            krev_ref[h, there, :] = dot(flip, k_ref[h, here, :]).astype(HALF)
            vrev_ref[h, there, :] = dot(flip, v_ref[h, here, :]).astype(HALF)

    def query_block(block, carried):
        rows = tiles_of(block)

        def body(count, first):
            start = tiles - first - count
            cols = tiles_of(start, count)
            offsets = tiles_of(block + start, count + 1)
            for h in range(heads):
                grad, probs_low = g_ref[h, rows, :], p_ref[h, rows, cols]
                probs = probs_low.astype(FULL)
                grad_probs = dot(grad, vrev_ref[h, cols, :], NT)
                inner = jnp.sum(probs * grad_probs, axis=1, keepdims=True)
                grad_raw = (probs * (grad_probs - inner)) * SCALE
                by_offset = unshear(grad_raw, count, after)
                dq_ref[h, rows, :] = (
                    dot(grad_raw.astype(HALF), krev_ref[h, cols, :])
                    + dot(by_offset, kbs_ref[h, offsets, :])
                ).astype(HALF)
                gkb_ref[h, :, offsets] += dot(
                    q_ref[h, rows, :].astype(FULL).T.astype(HALF), by_offset
                )
                dvt_ref[h, :, cols] += dot(grad.astype(FULL).T.astype(HALF), probs_low)
                for m in range(count):
                    dst_ref[h, tiles_of(start + m), rows] = grad_raw[
                        :, m * TILE : (m + 1) * TILE
                    ].T

        by_window(lengths, block, tiles, body)
        return carried

    lax.fori_loop(0, tiles, query_block, 0)

    def key_block(block, carried):
        rows, back = tiles_of(block), tiles_of(tiles - 1 - block)

        def body(count, first):
            cols = tiles_of(first, count)
            offsets = tiles_of(tiles - 1 - block + first, count + 1)
            for h in range(heads):
                grad_raw = dst_ref[h, back, cols]
                by_offset = unshear(grad_raw, count, after)
                grad_key = (
                    dot(grad_raw.astype(HALF), q_ref[h, cols, :])
                    + dot(by_offset, qbs_ref[h, offsets, :])
                ).astype(HALF)
                dk_ref[h, rows, :] = dot(flip, grad_key).astype(HALF)
                gqb_ref[h, :, offsets] += dot(
                    krev_ref[h, back, :].astype(FULL).T.astype(HALF), by_offset
                )
                dv_ref[h, rows, :] = dot(flip, dvt_ref[h, :, back].astype(HALF), NT).astype(HALF)

        by_window(lengths, block, tiles, body)
        return carried

    lax.fori_loop(0, tiles, key_block, 0)


SMEM_SPEC = pl.BlockSpec(memory_space=pltpu.SMEM)
VMEM_SPEC = pl.BlockSpec(memory_space=pltpu.VMEM)


def kernel_cost(microseconds):
    return pl.CostEstimate(
        flops=int(microseconds * 1e9), bytes_accessed=int(microseconds * 1e6), transcendentals=0
    )


def attention_forward(lengths, q, k, v, kb, qb, row_ids, col_ids):
    heads, rows, width = q.shape
    return pl.pallas_call(
        forward_kernel,
        out_shape=(
            jax.ShapeDtypeStruct((heads, rows, width), HALF),
            jax.ShapeDtypeStruct((heads, rows, rows), HALF),
        ),
        in_specs=[SMEM_SPEC] + [VMEM_SPEC] * 7,
        out_specs=(VMEM_SPEC,) * 2,
        scratch_shapes=[pltpu.VMEM((heads, rows, rows), FULL)],
        compiler_params=pltpu.CompilerParams(vmem_limit_bytes=52 * 2**20),
        cost_estimate=kernel_cost(40),
    )(lengths, q, k, v, kb, qb, row_ids, col_ids)


def attention_backward(lengths, q, k, v, kbs, qbs, probs, grad):
    heads, rows, width = q.shape
    shape = jax.ShapeDtypeStruct
    return pl.pallas_call(
        backward_kernel,
        out_shape=(shape((heads, rows, width), HALF),) * 3
        + (shape((heads, width, 2 * rows), FULL),) * 2,
        in_specs=[SMEM_SPEC] + [VMEM_SPEC] * 7,
        out_specs=(VMEM_SPEC,) * 5,
        scratch_shapes=[
            pltpu.VMEM((heads, rows, rows), FULL),
            pltpu.VMEM((heads, rows, width), HALF),
            pltpu.VMEM((heads, rows, width), HALF),
            pltpu.VMEM((heads, width, rows), FULL),
        ],
        compiler_params=pltpu.CompilerParams(vmem_limit_bytes=56 * 2**20),
        cost_estimate=kernel_cost(48),
    )(lengths, q, k, v, kbs, qbs, probs, grad)


def index_bits(axis):
    size = lax.axis_size(axis)
    bits, bit = [], size // 2
    while bit >= 1:
        bits.append((axis, bit))
        bit //= 2
    return bits


def own_bit(step):
    axis, bit = step
    return (lax.axis_index(axis) // bit) % 2


def swap(values, step):
    axis, bit = step
    return lax.ppermute(values, axis, [(i, i ^ bit) for i in range(lax.axis_size(axis))])


def gather_by(values, steps, layout):
    present = []
    for step in steps:
        other = swap(values, step)
        place = sum(1 for kept in layout if kept in present and layout.index(kept) < layout.index(step))
        present.append(step)
        mine = own_bit(step) == 0
        values = jnp.where(
            mine, jnp.stack([values, other], axis=place), jnp.stack([other, values], axis=place)
        )
    return values


def scatter_by(values, steps, layout):
    remaining = list(layout)
    kind = values.dtype
    for step in steps:
        place = remaining.index(step)
        remaining.remove(step)
        mine = own_bit(step)
        kept = lax.dynamic_index_in_dim(values, mine, place, keepdims=False)
        other = swap(lax.dynamic_index_in_dim(values, 1 - mine, place, keepdims=False), step)
        values = kept.astype(FULL) + other.astype(FULL)
        if len(remaining):
            values = values.astype(kind)
    return values


def split_bits(values, layout):
    return values.reshape((2,) * len(layout) + values.shape[1:])


def bucket_of(offset, buckets, longest):
    middle = buckets // 2
    distance = middle - 1 if abs(offset) < middle else abs(offset)
    sign_of = 1 if offset > 0 else -1 if offset < 0 else 0
    far_bucket = (
        math.ceil(math.log(distance / middle) / math.log((longest - 1) / middle) * (middle - 1))
        + middle
    )
    bucket = offset if distance <= middle else sign_of * far_bucket
    return min(max(bucket + buckets, 0), 2 * buckets - 1)


def offset_selector():
    selector = np.zeros((4 * MAXLEN, 2 * BUCKETS), dtype=np.float32)
    for offset in range(1 - MAXLEN, MAXLEN):
        selector[offset + 2 * MAXLEN - 1, bucket_of(offset, BUCKETS, MAXLEN)] = 1.0
    return selector


def mirrored(selector):
    turned = np.zeros_like(selector)
    turned[:-1] = selector[-2::-1]
    return turned


def standardise(values):
    center = values - jnp.mean(values, axis=-1, keepdims=True)
    spread = jnp.mean(center * center, axis=-1, keepdims=True)
    inverse = lax.rsqrt(spread + EPSILON)
    return center * inverse, inverse


def standardise_back(grad, unit, inverse):
    return inverse * (
        grad
        - jnp.mean(grad, axis=-1, keepdims=True)
        - unit * jnp.mean(grad * unit, axis=-1, keepdims=True)
    )


def gelu_exact(values):
    return jax.nn.gelu(values, approximate=False)


def nesterov(weight, moment, average, gradient, step_rate):
    decayed = gradient + DECAY * weight
    moment_new = MOMENTUM * moment + decayed
    weight_new = weight - step_rate * (decayed + MOMENTUM * moment_new)
    average_new = AVERAGE * average + (1.0 - AVERAGE) * weight_new
    return (weight_new, moment_new, average_new)


def column_sums(matrix):
    return jnp.sum(matrix, axis=0, dtype=FULL)


def per_device(
    inputs,
    seg_lengths,
    cotangent,
    qkv_weight,
    qkv_moment,
    qkv_average,
    out_weight,
    out_moment,
    out_average,
    up_weight,
    up_moment,
    up_average,
    down_weight,
    down_moment,
    down_average,
    rel_table,
    table_moment,
    table_average,
    vectors,
    vector_moment,
    vector_average,
):
    tok_rows = inputs.shape[0]
    head_count = lax.axis_size("head")
    dp_count = lax.axis_size("dp")
    head_rank = lax.axis_index("head")
    local_heads = HEADS // head_count
    local_width = local_heads * HD
    quarter = tok_rows // head_count
    total_tokens = tok_rows * dp_count
    up_local = up_weight.shape[1]
    dp_bits, head_bits = index_bits("dp"), index_bits("head")
    all_bits = dp_bits + head_bits

    w_qkv_own = jnp.concatenate([qkv_weight[i] for i in range(3)], axis=1).astype(HALF)
    w_qkv = gather_by(w_qkv_own, dp_bits, dp_bits).reshape(D, 3 * local_width)

    unit_own, inverse_own = standardise(rel_table)
    vec_rows = vectors.shape[0]
    table_part = rel_table.shape[0]
    lanes = -(-2 * vec_rows // table_part // 128) * 128
    half_span = table_part * lanes // 2
    vec_high = vectors.astype(HALF)
    vec_low = (vectors - vec_high.astype(FULL)).astype(HALF)
    vec_pack = jnp.concatenate(
        [
            jnp.pad(vec_high, (0, half_span - vec_rows)),
            jnp.pad(vec_low, (0, half_span - vec_rows)),
        ]
    ).reshape(table_part, lanes)
    small_own = jnp.concatenate([unit_own.astype(HALF), vec_pack], axis=1)
    small = gather_by(small_own, dp_bits + head_bits[::-1], all_bits).reshape(
        dp_count * head_count, table_part, D + lanes
    )
    unit_table = small[:, :, :D].reshape(dp_count * head_count * table_part, D).astype(FULL)
    vec_all = small[:, :, D:].reshape(dp_count * head_count, 2 * half_span).astype(FULL)
    vector_full = (vec_all[:, :vec_rows] + vec_all[:, half_span : half_span + vec_rows]).reshape(-1)
    vector_rows = vector_full[: 11 * D].reshape(11, D)
    bias_up = vector_full[11 * D :]

    up_out_own = jnp.concatenate([up_weight, out_weight.T], axis=1).astype(HALF)
    down_own = down_weight.T.astype(HALF)
    weight_layout = head_bits + dp_bits
    up_out = gather_by(up_out_own, dp_bits + head_bits, weight_layout).reshape(
        head_count, D, up_local + local_width
    )
    w_down_t = gather_by(
        down_own, head_bits[:1] + dp_bits + head_bits[1:], weight_layout
    ).reshape(head_count, D, up_local)
    w_up = [up_out[h, :, :up_local] for h in range(head_count)]
    w_out_t = [up_out[h, :, up_local:] for h in range(head_count)]

    def head_part(row_values):
        return lax.dynamic_slice_in_dim(row_values, head_rank * local_width, local_width)

    bias_qkv = jnp.concatenate([head_part(vector_rows[8 + i]) for i in range(3)])
    normed = (unit_table * vector_rows[4] + vector_rows[5]).astype(HALF)
    tables = (dot(normed, w_qkv[:, : 2 * local_width]) + bias_qkv[: 2 * local_width]).astype(HALF)

    def split_heads(values):
        return values.reshape(values.shape[0], -1, HD).transpose(1, 0, 2)

    selector = offset_selector()
    by_sum = jnp.asarray(selector, dtype=HALF)
    by_difference = jnp.asarray(mirrored(selector), dtype=HALF)
    query_flat, key_flat = tables[:, :local_width], tables[:, local_width:]
    kb = split_heads(dot(by_difference, key_flat).astype(HALF))
    qb = split_heads(dot(by_difference, query_flat).astype(HALF))
    kbs = split_heads(dot(by_sum, key_flat).astype(HALF))
    qkv = split_heads((dot(inputs, w_qkv) + bias_qkv).astype(HALF))
    q, k, v = (qkv[i * local_heads : (i + 1) * local_heads] for i in range(3))

    lengths = seg_lengths[0]
    order = jnp.arange(lengths.shape[0], dtype=jnp.int32)
    ends = jnp.sum(jnp.where(order[None, :] <= order[:, None], lengths[None, :], 0), axis=1)
    places = jnp.arange(tok_rows, dtype=jnp.int32)
    segment = jnp.sum((places[:, None] >= ends[None, :]).astype(jnp.int32), axis=1)
    row_ids = jnp.broadcast_to(segment[None, :], (8, tok_rows))
    col_ids = jnp.broadcast_to(segment[:, None], (tok_rows, TILE))

    context, probs = attention_forward(lengths, q, k, v, kb, qb, row_ids, col_ids)

    def exchange(blocks):
        result = jnp.zeros_like(blocks)
        result = lax.dynamic_update_index_in_dim(
            result, lax.dynamic_index_in_dim(blocks, head_rank, 0, keepdims=False), head_rank, 0
        )
        for offset in range(1, head_count):
            partner = head_rank ^ offset
            got = swap(
                lax.dynamic_index_in_dim(blocks, partner, 0, keepdims=False), ("head", offset)
            )
            result = lax.dynamic_update_index_in_dim(result, got, partner, 0)
        return result

    context_own = (
        context.reshape(local_heads, head_count, quarter, HD)
        .transpose(1, 2, 0, 3)
        .reshape(head_count, quarter, local_width)
    )
    context_low = exchange(context_own)

    def own_tokens(values):
        return lax.dynamic_slice_in_dim(values, head_rank * quarter, quarter, 0)

    attention = sum(dot(context_low[h], w_out_t[h], NT) for h in range(head_count))
    unit_first, inverse_first = standardise(
        own_tokens(inputs).astype(FULL) + attention + vector_rows[6]
    )
    first_norm = unit_first * vector_rows[0] + vector_rows[1]
    first_low = first_norm.astype(HALF)
    up_pre = jnp.concatenate([dot(first_low, w_up[h]) for h in range(head_count)], axis=1) + bias_up
    up_values, gelu_back = jax.vjp(gelu_exact, up_pre)
    hidden_low = up_values.astype(HALF)

    def hidden_part(values, h):
        return values[:, h * up_local : (h + 1) * up_local]

    down = sum(dot(hidden_part(hidden_low, h), w_down_t[h], NT) for h in range(head_count))
    unit_second, inverse_second = standardise(first_norm + down + vector_rows[7])
    output = (unit_second * vector_rows[2] + vector_rows[3]).astype(HALF)

    grad_out = own_tokens(cotangent).astype(FULL)
    grad_second_gain = column_sums(grad_out * unit_second)
    grad_second_bias = column_sums(grad_out)
    grad_second = standardise_back(grad_out * vector_rows[2], unit_second, inverse_second)
    grad_bias_down = column_sums(grad_second)
    grad_down_low = grad_second.astype(HALF)
    grad_hidden = jnp.concatenate(
        [dot(grad_down_low, w_down_t[h]) for h in range(head_count)], axis=1
    )
    (grad_up_pre,) = gelu_back(grad_hidden)
    grad_up_low = grad_up_pre.astype(HALF)
    grad_bias_up = column_sums(grad_up_low)

    def send_weight(grads, steps):
        stacked = jnp.stack([g.astype(HALF) for g in grads])
        shape = (2,) * len(weight_layout) + (D // dp_count, stacked.shape[2])
        return scatter_by(stacked.reshape(shape), steps, weight_layout)

    grad_down_wt = [dot(grad_down_low, hidden_part(hidden_low, h), TN) for h in range(head_count)]
    down_shard = send_weight(grad_down_wt, head_bits[::-1] + dp_bits[::-1]).T
    grad_first = grad_second + sum(
        dot(hidden_part(grad_up_low, h), w_up[h], NT) for h in range(head_count)
    )
    grad_first_gain = column_sums(grad_first * unit_first)
    grad_first_bias = column_sums(grad_first)
    grad_pre_first = standardise_back(grad_first * vector_rows[0], unit_first, inverse_first)
    grad_bias_out = column_sums(grad_pre_first)
    grad_attn_low = grad_pre_first.astype(HALF)
    grad_context_own = jnp.stack(
        [dot(grad_attn_low, w_out_t[h]).astype(HALF) for h in range(head_count)]
    )
    grad_context = exchange(grad_context_own)
    grad_context = split_heads(grad_context.reshape(tok_rows, local_width))
    grad_up_out = [
        jnp.concatenate(
            [
                dot(first_low, hidden_part(grad_up_low, h), TN),
                dot(grad_attn_low, context_low[h], TN),
            ],
            axis=1,
        )
        for h in range(head_count)
    ]
    up_out_shard = send_weight(
        grad_up_out, head_bits[1:] + dp_bits[::-1] + head_bits[:1]
    )
    up_shard, out_shard = up_out_shard[:, :up_local], up_out_shard[:, up_local:].T

    dq, dk, dv, grad_kb, grad_qb = attention_backward(
        lengths, q, k, v, kbs, qb, probs, grad_context
    )

    def join_heads(values):
        return values.transpose(1, 0, 2).reshape(values.shape[1], -1)

    grad_qkv_low = join_heads(jnp.concatenate([dq, dk, dv], axis=0))
    wide_kb = grad_kb.reshape(local_width, -1).astype(HALF)
    wide_qb = grad_qb.reshape(local_width, -1).astype(HALF)
    grad_tables = jnp.concatenate(
        [
            dot(by_difference, wide_qb, (((0,), (1,)), ((), ()))),
            dot(by_sum, wide_kb, (((0,), (1,)), ((), ()))),
        ],
        axis=1,
    ).astype(HALF)
    grad_normed = dot(grad_tables, w_qkv[:, : 2 * local_width], NT)
    grad_rel_gain = column_sums(grad_normed * unit_table)
    grad_rel_bias = column_sums(grad_normed)
    grad_input_part = dot(grad_qkv_low, w_qkv, NT).astype(HALF)
    grad_qkv = dot(inputs, grad_qkv_low, TN)
    grad_qkv = jnp.concatenate(
        [
            grad_qkv[:, : 2 * local_width] + dot(normed, grad_tables, TN),
            grad_qkv[:, 2 * local_width :],
        ],
        axis=1,
    ).astype(HALF)
    qkv_shard = scatter_by(
        grad_qkv.reshape((2,) * len(dp_bits) + (D // dp_count, 3 * local_width)),
        dp_bits[::-1],
        dp_bits,
    )
    input_grad = grad_pre_first + scatter_by(
        grad_input_part.reshape((2,) * len(head_bits) + (quarter, D)), head_bits[::-1], head_bits
    )
    normed_shard = scatter_by(
        grad_normed.astype(HALF).reshape((2,) * len(all_bits) + (table_part, D)),
        head_bits[::-1] + dp_bits[::-1],
        all_bits,
    )
    table_shard = standardise_back(normed_shard * vector_rows[4], unit_own, inverse_own)

    grad_bias_qkv = column_sums(grad_qkv_low)
    grad_bias_tables = column_sums(grad_tables)
    grad_bias_qkv = grad_bias_qkv + jnp.pad(grad_bias_tables, (0, local_width))

    def place_part(part_values):
        return lax.dynamic_update_slice_in_dim(
            jnp.zeros((D,), FULL), part_values, head_rank * local_width, 0
        )

    grad_vector = jnp.concatenate(
        [
            grad_first_gain,
            grad_first_bias,
            grad_second_gain,
            grad_second_bias,
            grad_rel_gain,
            grad_rel_bias,
            grad_bias_out,
            grad_bias_down,
        ]
        + [place_part(grad_bias_qkv[i * local_width : (i + 1) * local_width]) for i in range(3)]
        + [grad_bias_up]
    )
    vec_lanes = -(-vec_rows // 128) * 128
    grad_vector = jnp.pad(
        grad_vector.reshape(dp_count * head_count, vec_rows), ((0, 0), (0, vec_lanes - vec_rows))
    )
    vector_shard = scatter_by(
        grad_vector.reshape((2,) * len(all_bits) + (vec_lanes // 128, 128)),
        head_bits[::-1] + dp_bits[::-1],
        all_bits,
    ).reshape(-1)[:vec_rows]

    qkv_grad_shard = jnp.stack(
        [qkv_shard[:, i * local_width : (i + 1) * local_width] for i in range(3)]
    )
    new_qkv = nesterov(
        qkv_weight, qkv_moment, qkv_average, qkv_grad_shard, 0.75 / math.sqrt(D * total_tokens)
    )
    new_out = nesterov(
        out_weight,
        out_moment,
        out_average,
        out_shard,
        0.125 * MAXLEN / math.sqrt(D * total_tokens),
    )
    new_up = nesterov(up_weight, up_moment, up_average, up_shard, 1.1 / math.sqrt(D * total_tokens))
    new_down = nesterov(
        down_weight, down_moment, down_average, down_shard, 1.0 / math.sqrt(FF * total_tokens)
    )
    new_table = nesterov(
        rel_table,
        table_moment,
        table_average,
        table_shard,
        0.55 * math.sqrt(MAXLEN / total_tokens),
    )
    new_vector = nesterov(
        vectors, vector_moment, vector_average, vector_shard, 0.3 / math.sqrt(total_tokens)
    )
    return (output, input_grad) + new_qkv + new_out + new_up + new_down + new_table + new_vector


def solution(mesh):
    rows = P("dp", None)
    owned = P(("dp", "head"), None)
    qkv = P(None, "dp", "head")
    out = P("head", "dp")
    up = P("dp", "head")
    vector = P(("dp", "head"))
    return jax.shard_map(
        per_device,
        mesh=mesh,
        in_specs=(rows,) * 3 + (qkv,) * 3 + (out,) * 3 + (up,) * 3 + (out,) * 3 + (owned,) * 3 + (vector,) * 3,
        out_specs=(owned,) * 2 + (qkv,) * 3 + (out,) * 3 + (up,) * 3 + (out,) * 3 + (owned,) * 3 + (vector,) * 3,
        check_vma=False,
    )
```

```python
import functools
import math

import jax
import jax.numpy as jnp
import numpy as np
from jax import lax
from jax.experimental import pallas as pl
from jax.experimental.pallas import tpu as pltpu
from jax.sharding import PartitionSpec as P

D = 768
HEADS = 12
HD = 64
FF = 3072
BUCKETS = 256
MAXLEN = 512

EPSILON = 1e-07
MOMENTUM = 0.9
DECAY = 0.01
AVERAGE = 0.7
MASKED = -1e30

TILE = 128
NARROW = 5
SCALE = (3.0 * HD) ** -0.5
LOG2E = math.log2(math.e)
HALF = jnp.bfloat16
FULL = jnp.float32
NN = (((1,), (0,)), ((), ()))
NT = (((1,), (1,)), ((), ()))
TN = (((0,), (0,)), ((), ()))


def dot(left, right, dims=NN):
    return lax.dot_general(left, right, dims, preferred_element_type=FULL)


def shear(values, count, low):
    rolled = [
        pltpu.roll(values[:, m * TILE : (m + 1) * TILE], 1, 1, stride=1, stride_axis=0)
        for m in range(count + 1)
    ]
    return jnp.concatenate(
        [jnp.where(low, rolled[m], rolled[m + 1]) for m in range(count)], axis=1
    )


def unshear(values, count, after):
    rolled = [
        pltpu.roll(values[:, m * TILE : (m + 1) * TILE], 0, 1, stride=1, stride_axis=0)
        for m in range(count)
    ]
    zero = jnp.zeros((TILE, TILE), values.dtype)
    return jnp.concatenate(
        [
            jnp.where(
                after, rolled[m] if m < count else zero, rolled[m - 1] if m > 0 else zero
            ).astype(HALF)
            for m in range(count + 1)
        ],
        axis=1,
    )


def flip_matrix():
    across = lax.broadcasted_iota(jnp.int32, (TILE, TILE), 1)
    down = lax.broadcasted_iota(jnp.int32, (TILE, TILE), 0)
    return (across + down == TILE - 1).astype(FULL).astype(HALF)


def tiles_of(block, count=1):
    return pl.ds(pl.multiple_of(block * TILE, TILE), count * TILE)


def sequence_bounds(ends, first, last):
    start, stop = jnp.int32(0), jnp.int32(0)
    begin = jnp.int32(0)
    for end in ends:
        start = jnp.where((begin <= first) & (first < end), begin, start)
        stop = jnp.where((begin <= last) & (last < end), end, stop)
        begin = end
    return start, stop


def by_window(ends, block, tiles, body):
    start, stop = sequence_bounds(ends, block * TILE, block * TILE + TILE - 1)
    first = start // TILE
    narrow = min(NARROW, tiles)
    fits = (stop + TILE - 1) // TILE - first <= narrow

    @pl.when(fits)
    def _():
        body(narrow, jnp.minimum(first, tiles - narrow))

    @pl.when(jnp.logical_not(fits))
    def _():
        body(tiles, jnp.int32(0))


def sequence_ends(info, count):
    ends, total = [], jnp.int32(0)
    for s in range(count):
        total = total + info[s]
        ends.append(total)
    return ends


def sequence_of(places, ends):
    return sum((places >= end).astype(jnp.int32) for end in ends[:-1])


def turned(block, rank, per_owner):
    return ((block // per_owner) ^ rank) * per_owner + block % per_owner


def forward_kernel(
    info, qkv_ref, tab_ref, ctx_ref, p_ref, q_ref, k_ref, v_ref, qb_ref, kb_ref, p2c_ref, *, owners
):
    heads, tiles = q_ref.shape[0], q_ref.shape[1] // TILE
    segments = info.shape[0] - 1
    rank, per_owner = info[segments], tiles // owners
    ends = sequence_ends(info, segments)
    across = lax.broadcasted_iota(jnp.int32, (TILE, TILE), 1)
    down = lax.broadcasted_iota(jnp.int32, (TILE, TILE), 0)
    low = across <= down
    flip = flip_matrix()
    for h in range(heads):
        for i, ref in enumerate((q_ref, k_ref, v_ref)):
            ref[h] = qkv_ref[:, (i * heads + h) * HD : (i * heads + h + 1) * HD]
        for i, ref in enumerate((qb_ref, kb_ref)):
            ref[h] = tab_ref[:, (i * heads + h) * HD : (i * heads + h + 1) * HD]

    def p2c_block(block, carried):
        rows = tiles_of(block)

        def body(count, first):
            offsets = tiles_of(first - block + tiles - 1, count + 1)
            for h in range(heads):
                sheared = shear(dot(k_ref[h, rows, :], qb_ref[h, offsets, :], NT), count, low)
                for m in range(count):
                    p2c_ref[h, tiles_of(first + m), rows] = sheared[
                        :, m * TILE : (m + 1) * TILE
                    ].T

        by_window(ends, block, tiles, body)
        return carried

    lax.fori_loop(0, tiles, p2c_block, 0)

    def score_block(block, carried):
        rows = tiles_of(block)
        row_sequence = sequence_of(down + block * TILE, ends)

        def body(count, first):
            cols = tiles_of(first, count)
            offsets = tiles_of(first - block + tiles - 1, count + 1)
            same = [
                row_sequence == sequence_of(across + (first + m) * TILE, ends) for m in range(count)
            ]
            same = jnp.concatenate(same, axis=1)
            contexts = []
            for h in range(heads):
                query = q_ref[h, rows, :]
                c2p = shear(dot(query, kb_ref[h, offsets, :], NT), count, low)
                raw = dot(query, k_ref[h, cols, :], NT) + c2p + p2c_ref[h, rows, cols]
                scores = jnp.where(same, (SCALE * LOG2E) * raw, MASKED)
                powers = jnp.exp2(scores - jnp.max(scores, axis=1, keepdims=True))
                probs = (powers * (1.0 / jnp.sum(powers, axis=1, keepdims=True))).astype(HALF)
                for m in range(count):
                    p_ref[h, rows, tiles_of(tiles - 1 - first - m)] = dot(
                        probs[:, m * TILE : (m + 1) * TILE], flip
                    ).astype(HALF)
                contexts.append(dot(probs, v_ref[h, cols, :]).astype(HALF))
            ctx_ref[tiles_of(turned(block, rank, per_owner)), :] = jnp.concatenate(contexts, axis=1)

        by_window(ends, block, tiles, body)
        return carried

    lax.fori_loop(0, tiles, score_block, 0)


def backward_kernel(
    info,
    qkv_ref,
    tab_ref,
    p_ref,
    g_ref,
    _up_ref,
    _down_ref,
    dqkv_ref,
    gtab_ref,
    q_ref,
    k_ref,
    krev_ref,
    vrev_ref,
    qbs_ref,
    kbs_ref,
    grad_ref,
    dst_ref,
    dvt_ref,
    gsum_ref,
    *,
    owners,
):
    heads, tiles = q_ref.shape[0], q_ref.shape[1] // TILE
    width = heads * HD
    segments = info.shape[0] - 1
    rank, per_owner = info[segments], tiles // owners
    ends = sequence_ends(info, segments)
    across = lax.broadcasted_iota(jnp.int32, (TILE, TILE), 1)
    down = lax.broadcasted_iota(jnp.int32, (TILE, TILE), 0)
    after = across >= down
    flip = flip_matrix()
    dst_ref[...] = jnp.zeros_like(dst_ref)
    dvt_ref[...] = jnp.zeros_like(dvt_ref)
    gsum_ref[...] = jnp.zeros_like(gsum_ref)
    for h in range(heads):
        q_ref[h] = qkv_ref[:, h * HD : (h + 1) * HD]
        k_ref[h] = qkv_ref[:, width + h * HD : width + (h + 1) * HD]
        qbs_ref[h] = tab_ref[:, h * HD : (h + 1) * HD]
        kbs_ref[h] = tab_ref[:, width + h * HD : width + (h + 1) * HD]
        grad_ref[h] = g_ref[:, h * HD : (h + 1) * HD]
    for m in range(tiles):
        here, there = slice(m * TILE, (m + 1) * TILE), slice((tiles - 1 - m) * TILE, (tiles - m) * TILE)
        turned_rows = dot(flip, qkv_ref[here, width:]).astype(HALF)
        for h in range(heads):
            krev_ref[h, there, :] = turned_rows[:, h * HD : (h + 1) * HD]
            vrev_ref[h, there, :] = turned_rows[:, width + h * HD : width + (h + 1) * HD]

    def query_block(block, carried):
        rows = tiles_of(block)

        def body(count, first):
            start = tiles - first - count
            cols = tiles_of(start, count)
            offsets = tiles_of(block + start, count + 1)
            grads = []
            for h in range(heads):
                grad = grad_ref[h, tiles_of(turned(block, rank, per_owner)), :]
                probs_low = p_ref[h, rows, cols]
                probs = probs_low.astype(FULL)
                grad_probs = dot(grad, vrev_ref[h, cols, :], NT)
                inner = jnp.sum(probs * grad_probs, axis=1, keepdims=True)
                grad_raw = (probs * (grad_probs - inner)) * SCALE
                by_offset = unshear(grad_raw, count, after)
                grads.append(
                    (
                        dot(grad_raw.astype(HALF), krev_ref[h, cols, :])
                        + dot(by_offset, kbs_ref[h, offsets, :])
                    ).astype(HALF)
                )
                gsum_ref[heads + h, :, offsets] += dot(
                    q_ref[h, rows, :].astype(FULL).T.astype(HALF), by_offset
                )
                dvt_ref[h, :, cols] += dot(grad.astype(FULL).T.astype(HALF), probs_low)
                for m in range(count):
                    dst_ref[h, tiles_of(start + m), rows] = grad_raw[
                        :, m * TILE : (m + 1) * TILE
                    ].T
            dqkv_ref[rows, :width] = jnp.concatenate(grads, axis=1)

        by_window(ends, block, tiles, body)
        return carried

    lax.fori_loop(0, tiles, query_block, 0)

    def key_block(block, carried):
        rows, back = tiles_of(block), tiles_of(tiles - 1 - block)

        def body(count, first):
            cols = tiles_of(first, count)
            offsets = tiles_of(tiles - 1 - block + first, count + 1)
            grads = []
            for h in range(heads):
                grad_raw = dst_ref[h, back, cols]
                by_offset = unshear(grad_raw, count, after)
                grads.append(
                    (
                        dot(grad_raw.astype(HALF), q_ref[h, cols, :])
                        + dot(by_offset, qbs_ref[h, offsets, :])
                    ).astype(HALF)
                )
                gsum_ref[h, :, offsets] += dot(
                    krev_ref[h, back, :].astype(FULL).T.astype(HALF), by_offset
                )
            grads += [dvt_ref[h, :, back].T.astype(HALF) for h in range(heads)]
            dqkv_ref[rows, width:] = dot(flip, jnp.concatenate(grads, axis=1)).astype(HALF)

        by_window(ends, block, tiles, body)
        return carried

    lax.fori_loop(0, tiles, key_block, 0)
    for i in range(2 * heads):
        gtab_ref[i * HD : (i + 1) * HD, :] = gsum_ref[i].astype(HALF)


SMEM_SPEC = pl.BlockSpec(memory_space=pltpu.SMEM)
VMEM_SPEC = pl.BlockSpec(memory_space=pltpu.VMEM)


def kernel_cost(microseconds):
    return pl.CostEstimate(
        flops=int(microseconds * 1e9), bytes_accessed=int(microseconds * 1e6), transcendentals=0
    )


def attention_forward(info, qkv, tables, owners):
    rows, heads = qkv.shape[0], qkv.shape[1] // (3 * HD)
    small, wide = pltpu.VMEM((heads, rows, HD), HALF), pltpu.VMEM((heads, 2 * rows, HD), HALF)
    return pl.pallas_call(
        functools.partial(forward_kernel, owners=owners),
        out_shape=(
            jax.ShapeDtypeStruct((rows, heads * HD), HALF),
            jax.ShapeDtypeStruct((heads, rows, rows), HALF),
        ),
        in_specs=[SMEM_SPEC] + [VMEM_SPEC] * 2,
        out_specs=(VMEM_SPEC,) * 2,
        scratch_shapes=[small] * 3 + [wide] * 2 + [pltpu.VMEM((heads, rows, rows), FULL)],
        compiler_params=pltpu.CompilerParams(vmem_limit_bytes=48 * 2**20),
        cost_estimate=kernel_cost(30),
    )(info, qkv, tables)


def attention_backward(info, qkv, tables, probs, grad, owners, before):
    rows, heads = qkv.shape[0], qkv.shape[1] // (3 * HD)
    shape = jax.ShapeDtypeStruct
    small, wide = pltpu.VMEM((heads, rows, HD), HALF), pltpu.VMEM((heads, 2 * rows, HD), HALF)
    return pl.pallas_call(
        functools.partial(backward_kernel, owners=owners),
        out_shape=(shape(qkv.shape, HALF), shape((2 * heads * HD, 2 * rows), HALF)),
        in_specs=[SMEM_SPEC] + [VMEM_SPEC] * 4 + [pl.BlockSpec(memory_space=pl.ANY)] * len(before),
        out_specs=(VMEM_SPEC,) * 2,
        scratch_shapes=[small] * 4
        + [wide] * 2
        + [
            small,
            pltpu.VMEM((heads, rows, rows), FULL),
            pltpu.VMEM((heads, HD, rows), FULL),
            pltpu.VMEM((2 * heads, HD, 2 * rows), FULL),
        ],
        compiler_params=pltpu.CompilerParams(vmem_limit_bytes=52 * 2**20),
        cost_estimate=kernel_cost(34),
    )(info, qkv, tables, probs, grad, *before)


def standardise(values):
    center = values - jnp.mean(values, axis=-1, keepdims=True)
    spread = jnp.mean(center * center, axis=-1, keepdims=True)
    inverse = lax.rsqrt(spread + EPSILON)
    return center * inverse, inverse


def standardise_back(grad, unit, inverse):
    return inverse * (
        grad
        - jnp.mean(grad, axis=-1, keepdims=True)
        - unit * jnp.mean(grad * unit, axis=-1, keepdims=True)
    )


def exact_dot(values, order, dims):
    high = values.astype(HALF)
    rest = values - high.astype(FULL)
    middle = rest.astype(HALF)
    last = (rest - middle.astype(FULL)).astype(HALF)
    return dot(high, order, dims) + dot(middle, order, dims) + dot(last, order, dims)


def turn(values):
    return values.astype(FULL).T.astype(HALF)


def middle_kernel(info, x_ref, cot_ref, order_ref, vec_ref, bias_ref, *refs):
    heads = bias_ref.shape[0]
    ctx, up, down = (refs[i * heads : (i + 1) * heads] for i in range(3))
    out_ref, pre_ref, sums_ref, grad_bias_ref = refs[3 * heads : 3 * heads + 4]
    grad_ctx = refs[3 * heads + 4 : 4 * heads + 4]
    up_keep, up_send, down_keep, down_send, slope_ref, hidden_ref = refs[4 * heads + 4 :]
    grad_up = [(up_send if o % 2 else up_keep).at[o // 2] for o in range(heads)]
    grad_down = [(down_send if o % 2 else down_keep).at[o // 2] for o in range(heads)]
    rank = info[info.shape[0] - 1]
    wide = bias_ref.shape[1]
    span = ctx[0].shape[1]
    order = order_ref[...]
    vec = exact_dot(vec_ref[...], order, NT)
    gain1, bias1, gain2, bias2, bias_out, bias_down = (vec[i : i + 1] for i in range(6))

    pre_first = dot(x_ref[...], order, NT) + bias_out
    for o in range(heads):
        pre_first = pre_first + dot(ctx[o][...], up[o][:, wide : wide + span], NT)
    unit_first, inverse_first = standardise(pre_first)
    first = unit_first * gain1 + bias1
    first_low = first.astype(HALF)
    total = first + bias_down
    for o in range(heads):
        values = dot(first_low, up[o][:, :wide]) + bias_ref[pl.ds(rank ^ o, 1), :]
        below = 0.5 + 0.5 * lax.erf(values * math.sqrt(0.5))
        hidden = (values * below).astype(HALF)
        hidden_ref[o] = hidden
        slope_ref[o] = below + values * (
            jnp.exp2(values * values * (-0.5 * LOG2E)) * (1.0 / math.sqrt(2.0 * math.pi))
        )
        total = total + dot(hidden, down[o][...], NT)
    unit_second, inverse_second = standardise(total)
    out_ref[...] = dot((unit_second * gain2 + bias2).astype(HALF), order).astype(HALF)

    grad_out = dot(cot_ref[...], order, NT)
    grad_second = standardise_back(grad_out * gain2, unit_second, inverse_second)
    grad_down_low = grad_second.astype(HALF)
    grad_down_turned, first_turned = turn(grad_down_low), turn(first_low)
    grad_first = grad_second
    for o in range(heads):
        grad_down[o][...] = dot(grad_down_turned, hidden_ref[o]).astype(HALF)
        grad_values = (slope_ref[o] * dot(grad_down_low, down[o][...])).astype(HALF)
        grad_bias_ref[pl.ds(rank ^ o, 1), :] = jnp.sum(
            grad_values.astype(FULL), axis=0, keepdims=True
        )
        grad_up[o][:, :wide] = dot(first_turned, grad_values).astype(HALF)
        grad_first = grad_first + dot(grad_values, up[o][:, :wide], NT)
    grad_pre = standardise_back(grad_first * gain1, unit_first, inverse_first)
    grad_low = grad_pre.astype(HALF)
    grad_turned = turn(grad_low)
    for o in range(heads):
        grad_ctx[o][...] = dot(grad_low, up[o][:, wide : wide + span]).astype(HALF)
        grad_up[o][:, wide : wide + span] = dot(grad_turned, ctx[o][...]).astype(HALF)
        if wide + span < up[o].shape[1]:
            grad_up[o][:, wide + span :] = jnp.zeros(
                (up[o].shape[0], up[o].shape[1] - wide - span), HALF
            )
    pre_ref[...] = exact_dot(grad_pre, order, NN)
    sums = [
        jnp.sum(part, axis=0, keepdims=True)
        for part in (
            grad_first * unit_first,
            grad_first,
            grad_out * unit_second,
            grad_out,
            grad_pre,
            grad_second,
        )
    ]
    sums_ref[...] = exact_dot(jnp.concatenate(sums + [jnp.zeros_like(sums[0])] * 2, axis=0), order, NN)


def middle(info, x, cot, order, vec, bias, ctx, up, down):
    heads, (rows, width), wide = len(ctx), x.shape, bias.shape[1]
    shape = jax.ShapeDtypeStruct
    count = 6 + 3 * heads
    results = pl.pallas_call(
        middle_kernel,
        out_shape=(
            shape((rows, width), HALF),
            shape((rows, width), FULL),
            shape(vec.shape, FULL),
            shape(bias.shape, FULL),
        )
        + tuple(shape(c.shape, HALF) for c in ctx)
        + (shape((heads // 2,) + up[0].shape, HALF),) * 2
        + (shape((heads // 2,) + down[0].shape, HALF),) * 2,
        in_specs=[SMEM_SPEC] + [VMEM_SPEC] * (count - 1),
        out_specs=(VMEM_SPEC,) * (8 + heads),
        scratch_shapes=[pltpu.VMEM((heads, rows, wide), FULL), pltpu.VMEM((heads, rows, wide), HALF)],
        compiler_params=pltpu.CompilerParams(vmem_limit_bytes=48 * 2**20),
        cost_estimate=kernel_cost(20),
    )(info, x, cot, order, vec, bias, *ctx, *up, *down)
    return results[:4] + (results[4 : 4 + heads],) + results[4 + heads :]


def by_row(parts, count):
    row = lax.broadcasted_iota(jnp.int32, (count, parts[0].shape[1]), 0)
    total = jnp.zeros(row.shape, FULL)
    for i, part in enumerate(parts):
        total = jnp.where(row == i, part, total)
    return total


def tail_kernel(
    info,
    dqkv_ref,
    offsets_ref,
    w_ref,
    inputs_ref,
    normed_ref,
    unit_ref,
    difference_ref,
    sum_ref,
    order_ref,
    norm_sums_ref,
    bias_up_ref,
    *refs,
):
    qkv_ref, parts_ref, normed_grad_ref, vector_ref = refs[-4:]
    rank = info[info.shape[0] - 1]
    width = dqkv_ref.shape[1] // 3
    owners, quarter = parts_ref.shape[:2]
    tables = jnp.concatenate(
        [
            dot(difference_ref[...], offsets_ref[:width, :], NT),
            dot(sum_ref[...], offsets_ref[width:, :], NT),
        ],
        axis=1,
    ).astype(HALF)
    turned_tables = dot(order_ref[...], tables).astype(HALF)
    weights = w_ref[...]
    grad_normed = dot(turned_tables, weights[:, : 2 * width], NT)
    normed_grad_ref[...] = grad_normed.astype(HALF)
    grads = dqkv_ref[...]
    grad_qkv = dot(inputs_ref[...], grads)
    qkv_ref[:, : 3 * width] = (
        jnp.concatenate(
            [
                grad_qkv[:, : 2 * width] + dot(normed_ref[...], turned_tables),
                grad_qkv[:, 2 * width :],
            ],
            axis=1,
        )
    ).astype(HALF)
    if 3 * width < qkv_ref.shape[1]:
        qkv_ref[:, 3 * width :] = jnp.zeros((qkv_ref.shape[0], qkv_ref.shape[1] - 3 * width), HALF)
    for o in range(owners):
        apart = rank ^ o
        parts_ref[(apart % 2) * (owners // 2) + apart // 2] = dot(
            dqkv_ref[o * quarter : (o + 1) * quarter, :], weights, NT
        ).astype(HALF)
    sums = jnp.sum(grads.astype(FULL), axis=0, keepdims=True)
    table_sums = jnp.sum(turned_tables.astype(FULL), axis=0, keepdims=True)
    sums = jnp.concatenate([sums[:, : 2 * width] + table_sums, sums[:, 2 * width :]], axis=1)
    sums = by_row([sums[:, i * width : (i + 1) * width] for i in range(3)], 8)
    places = (
        lax.broadcasted_iota(jnp.int32, (width, D), 1)
        == lax.broadcasted_iota(jnp.int32, (width, D), 0) + rank * width
    ).astype(FULL).astype(HALF)
    placed = exact_dot(sums, places, NN)
    norm_sums, bias_up = norm_sums_ref[...], bias_up_ref[...]
    parts = [norm_sums[i : i + 1] for i in range(4)]
    parts.append(jnp.sum(grad_normed * unit_ref[...].astype(FULL), axis=0, keepdims=True))
    parts.append(jnp.sum(grad_normed, axis=0, keepdims=True))
    parts += [norm_sums[i : i + 1] for i in range(4, 6)]
    parts += [placed[i : i + 1] for i in range(3)]
    parts += [bias_up[i : i + 1] for i in range(bias_up.shape[0])]
    vector_ref[...] = by_row(parts, vector_ref.shape[0])


def tail(
    info, dqkv, offsets, weights, inputs, normed, unit, difference, by_sum, order, norm_sums, bias_up,
    owners, lanes, before,
):
    rows, shape = dqkv.shape[0], jax.ShapeDtypeStruct
    return pl.pallas_call(
        tail_kernel,
        out_shape=(
            shape((D, lanes), HALF),
            shape((owners, rows // owners, D), HALF),
            shape(normed.shape[::-1], HALF),
            shape((-(-(11 + bias_up.shape[0]) // 8) * 8, D), FULL),
        ),
        in_specs=[SMEM_SPEC] + [VMEM_SPEC] * 11 + [pl.BlockSpec(memory_space=pl.ANY)] * len(before),
        out_specs=(VMEM_SPEC,) * 4,
        compiler_params=pltpu.CompilerParams(vmem_limit_bytes=40 * 2**20),
        cost_estimate=kernel_cost(8),
    )(info, dqkv, offsets, weights, inputs, normed, unit, difference, by_sum, order, norm_sums, bias_up, *before)


def index_steps(axis):
    size = lax.axis_size(axis)
    steps, bit = [], size // 2
    while bit >= 1:
        steps.append((axis, bit))
        bit //= 2
    return steps


def swap(values, step):
    axis, bit = step
    return lax.ppermute(values, axis, [(i, i ^ bit) for i in range(lax.axis_size(axis))])


def gather_rows(values, steps):
    for step in steps:
        values = jnp.concatenate([values, swap(values, step)], axis=0)
    return values


def scatter_rows(values, steps):
    kind = values.dtype
    for i, step in enumerate(steps):
        half = values.shape[0] // 2
        values = values[:half].astype(FULL) + swap(values[half:], step).astype(FULL)
        if i < len(steps) - 1:
            values = values.astype(kind)
    return values


def add(kept, received):
    return (kept.astype(FULL) + received.astype(FULL)).astype(HALF)


def block_owner(rank, steps, axis):
    places = np.arange(2 ** len(steps))
    offsets = sum(
        ((places >> i) & 1) * bit for i, (along, bit) in enumerate(steps) if along == axis
    )
    return jnp.asarray(offsets, jnp.int32) ^ rank


def one_hot(owners, per_block):
    own = (owners[:, None] * per_block + jnp.arange(per_block, dtype=jnp.int32)[None, :]).reshape(-1)
    return (own[:, None] == jnp.arange(own.shape[0], dtype=jnp.int32)[None, :]).astype(HALF)


def bucket_of(offset, buckets, longest):
    middle = buckets // 2
    distance = middle - 1 if abs(offset) < middle else abs(offset)
    sign_of = 1 if offset > 0 else -1 if offset < 0 else 0
    far_bucket = (
        math.ceil(math.log(distance / middle) / math.log((longest - 1) / middle) * (middle - 1))
        + middle
    )
    bucket = offset if distance <= middle else sign_of * far_bucket
    return min(max(bucket + buckets, 0), 2 * buckets - 1)


def offset_selector():
    selector = np.zeros((4 * MAXLEN, 2 * BUCKETS), dtype=np.float32)
    for offset in range(1 - MAXLEN, MAXLEN):
        selector[offset + 2 * MAXLEN - 1, bucket_of(offset, BUCKETS, MAXLEN)] = 1.0
    return selector


def mirrored(selector):
    turned = np.zeros_like(selector)
    turned[:-1] = selector[-2::-1]
    return turned


def nesterov(weight, moment, average, gradient, step_rate):
    decayed = gradient + DECAY * weight
    moment_new = MOMENTUM * moment + decayed
    weight_new = weight - step_rate * (decayed + MOMENTUM * moment_new)
    average_new = AVERAGE * average + (1.0 - AVERAGE) * weight_new
    return (weight_new, moment_new, average_new)


def column_sums(matrix):
    return jnp.sum(matrix, axis=0, dtype=FULL)


def per_device(
    inputs,
    seg_lengths,
    cotangent,
    qkv_weight,
    qkv_moment,
    qkv_average,
    out_weight,
    out_moment,
    out_average,
    up_weight,
    up_moment,
    up_average,
    down_weight,
    down_moment,
    down_average,
    rel_table,
    table_moment,
    table_average,
    vectors,
    vector_moment,
    vector_average,
):
    tok_rows = inputs.shape[0]
    head_count = lax.axis_size("head")
    dp_count = lax.axis_size("dp")
    head_rank = lax.axis_index("head")
    dp_rank = lax.axis_index("dp")
    local_heads = HEADS // head_count
    local_width = local_heads * HD
    quarter = tok_rows // head_count
    total_tokens = tok_rows * dp_count
    up_local = up_weight.shape[1]
    dp_steps, head_steps = index_steps("dp"), index_steps("head")
    device_count = dp_count * head_count

    w_qkv_own = jnp.concatenate([qkv_weight[i] for i in range(3)], axis=1).astype(HALF)
    qkv_lanes = -(-3 * local_width // 128) * 128
    w_qkv_own = jnp.pad(w_qkv_own, ((0, 0), (0, qkv_lanes - 3 * local_width)))
    w_qkv_turned = gather_rows(w_qkv_own, dp_steps)

    unit_own, inverse_own = standardise(rel_table)
    vec_rows = vectors.shape[0]
    table_part = rel_table.shape[0]
    lanes = -(-2 * vec_rows // table_part // 128) * 128
    half_span = table_part * lanes // 2
    vec_high = vectors.astype(HALF)
    vec_low = (vectors - vec_high.astype(FULL)).astype(HALF)
    vec_pack = jnp.concatenate(
        [
            jnp.pad(vec_high, (0, half_span - vec_rows)),
            jnp.pad(vec_low, (0, half_span - vec_rows)),
        ]
    ).reshape(table_part, lanes)
    small_own = jnp.concatenate([unit_own.astype(HALF), vec_pack], axis=1)
    small_steps = dp_steps + head_steps
    small = gather_rows(small_own, small_steps)
    unit_table = small[:, :D].astype(FULL)
    owner = block_owner(dp_rank, small_steps, "dp") * head_count + block_owner(
        head_rank, small_steps, "head"
    )
    vec_all = small[:, D:].reshape(device_count, 2 * half_span)
    vec_all = dot(one_hot(owner, 1), vec_all, TN)
    vector_full = (vec_all[:, :vec_rows] + vec_all[:, half_span : half_span + vec_rows]).reshape(-1)
    vector_rows = vector_full[: 11 * D].reshape(11, D)

    wide_lanes = -(-(up_local + local_width) // 256) * 256
    up_out_own = jnp.pad(
        jnp.concatenate([up_weight, out_weight.T], axis=1).astype(HALF),
        ((0, 0), (0, wide_lanes - up_local - local_width)),
    )
    up_out = {0: gather_rows(up_out_own, dp_steps)}
    for step in head_steps:
        up_out.update({o ^ step[1]: swap(w, step) for o, w in up_out.items()})
    w_down_t = {0: gather_rows(down_weight.T.astype(HALF), dp_steps[:-1])}
    for step in head_steps[:-1]:
        w_down_t.update({o ^ step[1]: swap(w, step) for o, w in w_down_t.items()})
    w_down_t = {o: gather_rows(w, dp_steps[-1:]) for o, w in w_down_t.items()}
    for step in head_steps[-1:]:
        w_down_t.update({o ^ step[1]: swap(w, step) for o, w in w_down_t.items()})
    differences = sorted(w_down_t)

    width_order = one_hot(block_owner(dp_rank, dp_steps, "dp"), D // dp_count)
    table_order = one_hot(owner, table_part)
    w_qkv = dot(width_order, w_qkv_turned, TN).astype(HALF)[:, : 3 * local_width]
    inputs_across = dot(width_order, inputs, NT).astype(HALF)

    def head_part(row_values):
        return lax.dynamic_slice_in_dim(row_values, head_rank * local_width, local_width)

    bias_qkv = jnp.concatenate([head_part(vector_rows[8 + i]) for i in range(3)])
    normed = (unit_table * vector_rows[4] + vector_rows[5]).astype(HALF)
    normed_across = dot(width_order, normed, NT).astype(HALF)
    tables = (dot(normed, w_qkv[:, : 2 * local_width]) + bias_qkv[: 2 * local_width]).astype(HALF)
    tables = dot(table_order, tables, TN).astype(HALF)
    selector = offset_selector()
    by_sum = jnp.asarray(selector, dtype=HALF)
    by_difference = jnp.asarray(mirrored(selector), dtype=HALF)
    tables_difference = dot(by_difference, tables).astype(HALF)
    qkv = (dot(inputs, w_qkv) + bias_qkv).astype(HALF)
    info = jnp.concatenate([seg_lengths[0], head_rank[None].astype(jnp.int32)])
    context, probs = attention_forward(info, qkv, tables_difference, head_count)

    def exchange(blocks):
        return {
            o: swap(block, ("head", o)) if o else block for o, block in blocks.items()
        }

    context_low = exchange({o: context[o * quarter : (o + 1) * quarter] for o in differences})

    def own_tokens(values):
        return lax.dynamic_slice_in_dim(values, head_rank * quarter, quarter, 0)

    vec = jnp.concatenate([vector_rows[:4], vector_rows[6:8], vector_rows[:2]], axis=0)
    bias_up = vector_full[11 * D :].reshape(head_count, up_local)
    output, grad_pre_first, norm_sums, grad_bias_up, grad_context, *weight_grads = middle(
        info,
        own_tokens(inputs),
        own_tokens(cotangent),
        width_order,
        vec,
        bias_up,
        [context_low[o] for o in differences],
        [up_out[o] for o in differences],
        [w_down_t[o] for o in differences],
    )

    def fold(blocks, step):
        bit = step[1]
        return {
            o: (block.astype(FULL) + swap(blocks[o ^ bit], step).astype(FULL)).astype(HALF)
            for o, block in blocks.items()
            if not o & bit
        }

    up_keep, up_send, down_keep, down_send = weight_grads
    down_both = add(down_keep, swap(down_send, head_steps[-1]))
    up_both = add(up_keep, swap(up_send, head_steps[-1]))
    grad_context = exchange(dict(zip(differences, grad_context)))
    grad_context = jnp.concatenate([grad_context[o] for o in differences], axis=0)

    tables_sum = dot(by_sum, tables[:, local_width:]).astype(HALF)
    grad_qkv_low, grad_offsets = attention_backward(
        info,
        qkv,
        jnp.concatenate([tables_difference[:, :local_width], tables_sum], axis=1),
        probs,
        grad_context,
        head_count,
        (up_both, down_both),
    )
    while up_both.shape[0] > 1:
        up_both = scatter_rows(up_both, head_steps[-2:-1]).astype(HALF)
    half = down_both.shape[1] // 2
    down_both = add(down_both[:, :half], swap(down_both[:, half:], dp_steps[-1]))
    grad_qkv, input_parts, grad_normed, grad_vector = tail(
        info,
        grad_qkv_low,
        grad_offsets,
        w_qkv,
        inputs_across,
        normed_across,
        small[:, :D],
        by_difference.T,
        by_sum.T,
        table_order,
        norm_sums,
        grad_bias_up,
        head_count,
        qkv_lanes,
        (up_both, down_both),
    )
    up_out_shard = scatter_rows(up_both[0], dp_steps[::-1])
    up_shard = up_out_shard[:, :up_local]
    out_shard = up_out_shard[:, up_local : up_local + local_width].T
    down_both = scatter_rows(down_both, head_steps[:-1][::-1]).astype(HALF)
    down_shard = scatter_rows(down_both[0], dp_steps[:-1][::-1]).T
    qkv_shard = scatter_rows(grad_qkv, dp_steps[::-1])
    input_both = scatter_rows(input_parts, head_steps[-1:]).astype(HALF)
    input_grad = grad_pre_first + scatter_rows(input_both, head_steps[:-1][::-1])[0]

    vec_lanes = -(-vec_rows // 128) * 128
    grad_vector = jnp.pad(
        grad_vector.reshape(-1)[: device_count * vec_rows].reshape(device_count, vec_rows),
        ((0, 0), (0, vec_lanes - vec_rows)),
    )
    grad_vector = dot(one_hot(owner, 1), grad_vector.astype(HALF)).astype(HALF)
    spare = -(-vec_lanes // table_part // 128) * 128 * table_part
    grad_vector = jnp.pad(grad_vector, ((0, 0), (0, spare - vec_lanes)))
    grad_vector = grad_vector.reshape(device_count * table_part, -1)
    small_shard = scatter_rows(
        jnp.concatenate([grad_normed, grad_vector], axis=1), small_steps[::-1]
    )
    table_shard = standardise_back(small_shard[:, :D] * vector_rows[4], unit_own, inverse_own)
    vector_shard = small_shard[:, D:].reshape(-1)[:vec_rows]

    qkv_grad_shard = jnp.stack(
        [qkv_shard[:, i * local_width : (i + 1) * local_width] for i in range(3)]
    )
    new_qkv = nesterov(
        qkv_weight, qkv_moment, qkv_average, qkv_grad_shard, 0.75 / math.sqrt(D * total_tokens)
    )
    new_out = nesterov(
        out_weight,
        out_moment,
        out_average,
        out_shard,
        0.125 * MAXLEN / math.sqrt(D * total_tokens),
    )
    new_up = nesterov(up_weight, up_moment, up_average, up_shard, 1.1 / math.sqrt(D * total_tokens))
    new_down = nesterov(
        down_weight, down_moment, down_average, down_shard, 1.0 / math.sqrt(FF * total_tokens)
    )
    new_table = nesterov(
        rel_table,
        table_moment,
        table_average,
        table_shard,
        0.55 * math.sqrt(MAXLEN / total_tokens),
    )
    new_vector = nesterov(
        vectors, vector_moment, vector_average, vector_shard, 0.3 / math.sqrt(total_tokens)
    )
    return (output, input_grad) + new_qkv + new_out + new_up + new_down + new_table + new_vector


def solution(mesh):
    rows = P("dp", None)
    owned = P(("dp", "head"), None)
    qkv = P(None, "dp", "head")
    out = P("head", "dp")
    up = P("dp", "head")
    vector = P(("dp", "head"))
    return jax.shard_map(
        per_device,
        mesh=mesh,
        in_specs=(rows,) * 3 + (qkv,) * 3 + (out,) * 3 + (up,) * 3 + (out,) * 3 + (owned,) * 3 + (vector,) * 3,
        out_specs=(owned,) * 2 + (qkv,) * 3 + (out,) * 3 + (up,) * 3 + (out,) * 3 + (owned,) * 3 + (vector,) * 3,
        check_vma=False,
    )
```

```python
import functools
import math

import jax
import jax.numpy as jnp
import numpy as np
from jax import lax
from jax.experimental import pallas as pl
from jax.experimental.pallas import tpu as pltpu
from jax.sharding import PartitionSpec as P

D = 768
HEADS = 12
HD = 64
FF = 3072
BUCKETS = 256
MAXLEN = 512

EPSILON = 1e-07
MOMENTUM = 0.9
DECAY = 0.01
AVERAGE = 0.7
MASKED = -1e30

TILE = 128
NARROW = 5
SCALE = (3.0 * HD) ** -0.5
LOG2E = math.log2(math.e)
HALF = jnp.bfloat16
FULL = jnp.float32
NN = (((1,), (0,)), ((), ()))
NT = (((1,), (1,)), ((), ()))
TN = (((0,), (0,)), ((), ()))


def dot(left, right, dims=NN):
    return lax.dot_general(left, right, dims, preferred_element_type=FULL)


def shear(values, count, low):
    rolled = [
        pltpu.roll(values[:, m * TILE : (m + 1) * TILE], 0, 1, stride=1, stride_axis=0)
        for m in range(count + 1)
    ]
    return jnp.concatenate(
        [jnp.where(low, rolled[m], rolled[m + 1]) for m in range(count)], axis=1
    )


def unshear(values, count, after, shift):
    rolled = [
        pltpu.roll(values[:, m * TILE : (m + 1) * TILE], shift, 1, stride=1, stride_axis=0)
        for m in range(count)
    ]
    zero = jnp.zeros((TILE, TILE), values.dtype)
    return jnp.concatenate(
        [
            jnp.where(
                after, rolled[m] if m < count else zero, rolled[m - 1] if m > 0 else zero
            ).astype(HALF)
            for m in range(count + 1)
        ],
        axis=1,
    )


def flip_matrix():
    across = lax.broadcasted_iota(jnp.int32, (TILE, TILE), 1)
    down = lax.broadcasted_iota(jnp.int32, (TILE, TILE), 0)
    return (across + down == TILE - 1).astype(FULL).astype(HALF)


def tiles_of(block, count=1):
    return pl.ds(pl.multiple_of(block * TILE, TILE), count * TILE)


def sequence_bounds(ends, first, last):
    start, stop = jnp.int32(0), jnp.int32(0)
    begin = jnp.int32(0)
    for end in ends:
        start = jnp.where((begin <= first) & (first < end), begin, start)
        stop = jnp.where((begin <= last) & (last < end), end, stop)
        begin = end
    return start, stop


def by_window(ends, block, tiles, body):
    start, stop = sequence_bounds(ends, block * TILE, block * TILE + TILE - 1)
    first = start // TILE
    narrow = min(NARROW, tiles)
    fits = (stop + TILE - 1) // TILE - first <= narrow

    @pl.when(fits)
    def _():
        body(narrow, jnp.minimum(first, tiles - narrow))

    @pl.when(jnp.logical_not(fits))
    def _():
        body(tiles, jnp.int32(0))


def sequence_ends(info, count):
    ends, total = [], jnp.int32(0)
    for s in range(count):
        total = total + info[s]
        ends.append(total)
    return ends


def sequence_of(places, ends):
    return sum((places >= end).astype(jnp.int32) for end in ends[:-1])


def turned(block, rank, per_owner):
    return ((block // per_owner) ^ rank) * per_owner + block % per_owner


def forward_kernel(
    info,
    qkv_ref,
    tab_ref,
    _up_ref,
    _down_ref,
    ctx_ref,
    p_ref,
    q_ref,
    k_ref,
    v_ref,
    qb_ref,
    kb_ref,
    p2c_ref,
    *,
    owners,
):
    heads, tiles = q_ref.shape[0], q_ref.shape[1] // TILE
    segments = info.shape[0] - 1
    rank, per_owner = info[segments], tiles // owners
    ends = sequence_ends(info, segments)
    across = lax.broadcasted_iota(jnp.int32, (TILE, TILE), 1)
    down = lax.broadcasted_iota(jnp.int32, (TILE, TILE), 0)
    low = across < down
    flip = flip_matrix()
    for h in range(heads):
        for i, ref in enumerate((q_ref, k_ref, v_ref)):
            ref[h] = qkv_ref[:, (i * heads + h) * HD : (i * heads + h + 1) * HD]
        for i, ref in enumerate((qb_ref, kb_ref)):
            ref[h] = tab_ref[:, (i * heads + h) * HD : (i * heads + h + 1) * HD]

    def p2c_block(block, carried):
        rows = tiles_of(block)

        def body(count, first):
            offsets = tiles_of(first - block + tiles - 1, count + 1)
            for h in range(heads):
                sheared = shear(dot(k_ref[h, rows, :], qb_ref[h, offsets, :], NT), count, low)
                for m in range(count):
                    p2c_ref[h, tiles_of(first + m), rows] = sheared[
                        :, m * TILE : (m + 1) * TILE
                    ].T

        by_window(ends, block, tiles, body)
        return carried

    lax.fori_loop(0, tiles, p2c_block, 0)

    def score_block(block, carried):
        rows = tiles_of(block)
        row_sequence = sequence_of(down + block * TILE, ends)

        def body(count, first):
            cols = tiles_of(first, count)
            offsets = tiles_of(first - block + tiles - 1, count + 1)
            same = [
                row_sequence == sequence_of(across + (first + m) * TILE, ends) for m in range(count)
            ]
            same = jnp.concatenate(same, axis=1)
            contexts = []
            for h in range(heads):
                query = q_ref[h, rows, :]
                c2p = shear(dot(query, kb_ref[h, offsets, :], NT), count, low)
                raw = dot(query, k_ref[h, cols, :], NT) + c2p + p2c_ref[h, rows, cols]
                scores = jnp.where(same, (SCALE * LOG2E) * raw, MASKED)
                powers = jnp.exp2(scores - jnp.max(scores, axis=1, keepdims=True))
                probs = (powers * (1.0 / jnp.sum(powers, axis=1, keepdims=True))).astype(HALF)
                for m in range(count):
                    p_ref[h, rows, tiles_of(tiles - 1 - first - m)] = dot(
                        probs[:, m * TILE : (m + 1) * TILE], flip
                    ).astype(HALF)
                contexts.append(dot(probs, v_ref[h, cols, :]).astype(HALF))
            ctx_ref[tiles_of(turned(block, rank, per_owner)), :] = jnp.concatenate(contexts, axis=1)

        by_window(ends, block, tiles, body)
        return carried

    lax.fori_loop(0, tiles, score_block, 0)


def backward_kernel(
    info,
    qkv_ref,
    tab_ref,
    p_ref,
    g_ref,
    _up_ref,
    _down_ref,
    dqkv_ref,
    gtab_ref,
    q_ref,
    k_ref,
    krev_ref,
    vrev_ref,
    qbs_ref,
    kbs_ref,
    grad_ref,
    dst_ref,
    dvt_ref,
    gsum_ref,
    *,
    owners,
):
    heads, tiles = q_ref.shape[0], q_ref.shape[1] // TILE
    width = heads * HD
    segments = info.shape[0] - 1
    rank, per_owner = info[segments], tiles // owners
    ends = sequence_ends(info, segments)
    across = lax.broadcasted_iota(jnp.int32, (TILE, TILE), 1)
    down = lax.broadcasted_iota(jnp.int32, (TILE, TILE), 0)
    flip = flip_matrix()
    dst_ref[...] = jnp.zeros_like(dst_ref)
    dvt_ref[...] = jnp.zeros_like(dvt_ref)
    gsum_ref[...] = jnp.zeros_like(gsum_ref)
    for h in range(heads):
        q_ref[h] = qkv_ref[:, h * HD : (h + 1) * HD]
        k_ref[h] = qkv_ref[:, width + h * HD : width + (h + 1) * HD]
        qbs_ref[h] = tab_ref[:, h * HD : (h + 1) * HD]
        grad_ref[h] = g_ref[:, h * HD : (h + 1) * HD]
    for m in range(tiles):
        here, there = slice(m * TILE, (m + 1) * TILE), slice((tiles - 1 - m) * TILE, (tiles - m) * TILE)
        turned_rows = dot(flip, qkv_ref[here, width:]).astype(HALF)
        for h in range(heads):
            krev_ref[h, there, :] = turned_rows[:, h * HD : (h + 1) * HD]
            vrev_ref[h, there, :] = turned_rows[:, width + h * HD : width + (h + 1) * HD]
    for m in range(2 * tiles):
        here = slice(m * TILE, (m + 1) * TILE)
        there = slice((2 * tiles - 1 - m) * TILE, (2 * tiles - m) * TILE)
        turned_rows = dot(flip, tab_ref[here, width:]).astype(HALF)
        for h in range(heads):
            kbs_ref[h, there, :] = turned_rows[:, h * HD : (h + 1) * HD]

    def query_block(block, carried):
        rows = tiles_of(block)

        def body(count, first):
            start = tiles - first - count
            cols = tiles_of(start, count)
            offsets = tiles_of(block + start, count + 1)
            grads = []
            for h in range(heads):
                grad = grad_ref[h, tiles_of(turned(block, rank, per_owner)), :]
                probs_low = p_ref[h, rows, cols]
                probs = probs_low.astype(FULL)
                grad_probs = dot(grad, vrev_ref[h, cols, :], NT)
                inner = jnp.sum(probs * grad_probs, axis=1, keepdims=True)
                grad_raw = (probs * (grad_probs - inner)) * SCALE
                by_offset = unshear(grad_raw, count, across >= down, 0)
                grads.append(
                    (
                        dot(grad_raw.astype(HALF), krev_ref[h, cols, :])
                        + dot(by_offset, kbs_ref[h, offsets, :])
                    ).astype(HALF)
                )
                gsum_ref[heads + h, :, offsets] += dot(
                    q_ref[h, rows, :].astype(FULL).T.astype(HALF), by_offset
                )
                dvt_ref[h, :, cols] += dot(grad.astype(FULL).T.astype(HALF), probs_low)
                for m in range(count):
                    dst_ref[h, tiles_of(start + m), rows] = grad_raw[
                        :, m * TILE : (m + 1) * TILE
                    ].T
            dqkv_ref[rows, :width] = jnp.concatenate(grads, axis=1)

        by_window(ends, block, tiles, body)
        return carried

    lax.fori_loop(0, tiles, query_block, 0)

    def key_block(block, carried):
        rows, back = tiles_of(block), tiles_of(tiles - 1 - block)

        def body(count, first):
            cols = tiles_of(first, count)
            offsets = tiles_of(tiles - 1 - block + first, count + 1)
            grads = []
            for h in range(heads):
                grad_raw = dst_ref[h, back, cols]
                by_offset = unshear(grad_raw, count, across > down, 1)
                grads.append(
                    (
                        dot(grad_raw.astype(HALF), q_ref[h, cols, :])
                        + dot(by_offset, qbs_ref[h, offsets, :])
                    ).astype(HALF)
                )
                gsum_ref[h, :, offsets] += dot(
                    krev_ref[h, back, :].astype(FULL).T.astype(HALF), by_offset
                )
            grads += [dvt_ref[h, :, back].T.astype(HALF) for h in range(heads)]
            dqkv_ref[rows, width:] = dot(flip, jnp.concatenate(grads, axis=1)).astype(HALF)

        by_window(ends, block, tiles, body)
        return carried

    lax.fori_loop(0, tiles, key_block, 0)
    for i in range(heads):
        gtab_ref[i * HD : (i + 1) * HD, :] = gsum_ref[i].astype(HALF)
        for m in range(2 * tiles):
            there = slice((2 * tiles - 1 - m) * TILE, (2 * tiles - m) * TILE)
            gtab_ref[width + i * HD : width + (i + 1) * HD, there] = dot(
                gsum_ref[heads + i, :, m * TILE : (m + 1) * TILE].astype(HALF), flip
            ).astype(HALF)


SMEM_SPEC = pl.BlockSpec(memory_space=pltpu.SMEM)
VMEM_SPEC = pl.BlockSpec(memory_space=pltpu.VMEM)
ANY_SPEC = pl.BlockSpec(memory_space=pl.ANY)


def kernel_cost(microseconds):
    return pl.CostEstimate(
        flops=int(microseconds * 1e9), bytes_accessed=int(microseconds * 1e6), transcendentals=0
    )


def attention_forward(info, qkv, tables, owners, before):
    rows, heads = qkv.shape[0], qkv.shape[1] // (3 * HD)
    small, wide = pltpu.VMEM((heads, rows, HD), HALF), pltpu.VMEM((heads, 2 * rows, HD), HALF)
    return pl.pallas_call(
        functools.partial(forward_kernel, owners=owners),
        out_shape=(
            jax.ShapeDtypeStruct((rows, heads * HD), HALF),
            jax.ShapeDtypeStruct((heads, rows, rows), HALF),
        ),
        in_specs=[SMEM_SPEC] + [VMEM_SPEC] * 2 + [ANY_SPEC] * len(before),
        out_specs=(VMEM_SPEC,) * 2,
        scratch_shapes=[small] * 3 + [wide] * 2 + [pltpu.VMEM((heads, rows, rows), FULL)],
        compiler_params=pltpu.CompilerParams(vmem_limit_bytes=48 * 2**20),
        cost_estimate=kernel_cost(30),
    )(info, qkv, tables, *before)


def attention_backward(info, qkv, tables, probs, grad, owners, before):
    rows, heads = qkv.shape[0], qkv.shape[1] // (3 * HD)
    shape = jax.ShapeDtypeStruct
    small, wide = pltpu.VMEM((heads, rows, HD), HALF), pltpu.VMEM((heads, 2 * rows, HD), HALF)
    return pl.pallas_call(
        functools.partial(backward_kernel, owners=owners),
        out_shape=(shape(qkv.shape, HALF), shape((2 * heads * HD, 2 * rows), HALF)),
        in_specs=[SMEM_SPEC] + [VMEM_SPEC] * 4 + [ANY_SPEC] * len(before),
        out_specs=(VMEM_SPEC,) * 2,
        scratch_shapes=[small] * 4
        + [wide] * 2
        + [
            small,
            pltpu.VMEM((heads, rows, rows), FULL),
            pltpu.VMEM((heads, HD, rows), FULL),
            pltpu.VMEM((2 * heads, HD, 2 * rows), FULL),
        ],
        compiler_params=pltpu.CompilerParams(vmem_limit_bytes=52 * 2**20),
        cost_estimate=kernel_cost(34),
    )(info, qkv, tables, probs, grad, *before)


def standardise(values):
    center = values - jnp.mean(values, axis=-1, keepdims=True)
    spread = jnp.mean(center * center, axis=-1, keepdims=True)
    inverse = lax.rsqrt(spread + EPSILON)
    return center * inverse, inverse


def standardise_back(grad, unit, inverse):
    return inverse * (
        grad
        - jnp.mean(grad, axis=-1, keepdims=True)
        - unit * jnp.mean(grad * unit, axis=-1, keepdims=True)
    )


def exact_dot(values, order, dims):
    high = values.astype(HALF)
    rest = values - high.astype(FULL)
    middle = rest.astype(HALF)
    last = (rest - middle.astype(FULL)).astype(HALF)
    return dot(high, order, dims) + dot(middle, order, dims) + dot(last, order, dims)


def turn(values):
    return values.astype(FULL).T.astype(HALF)


def middle_kernel(info, x_ref, cot_ref, order_ref, vec_ref, bias_ref, *refs):
    heads = bias_ref.shape[0]
    ctx, up_far, down_far = refs[:heads], refs[heads : heads + 4], refs[heads + 4 : heads + 8]
    half = up_far[0].shape[1]
    refs = refs[len(refs) - heads - 16 :]
    out_ref, pre_ref, sums_ref, grad_bias_ref = refs[:4]
    grad_ctx = refs[4 : heads + 4]
    up_keep, up_send, down_keep, down_send = refs[heads + 4 : heads + 8]
    slope_ref, hidden_ref, up, down, grad_up, grad_down, sems_in, sems_out = refs[heads + 8 :]
    arrivals = [
        [
            pltpu.make_async_copy(
                up_far[2 * (o % 2) + i].at[o // 2], up.at[o, i * half : (i + 1) * half], sems_in.at[i, o]
            )
            for o in range(heads)
        ]
        for i in range(2)
    ]
    arrivals.append(
        [pltpu.make_async_copy(down_far[o], down.at[o], sems_in.at[2, o]) for o in range(heads)]
    )
    for copies in arrivals:
        for copy in copies:
            copy.start()
    departures = []

    def depart(i, o):
        near, keep, send = ((grad_up, up_keep, up_send), (grad_down, down_keep, down_send))[i]
        copy = pltpu.make_async_copy(
            near.at[o], (send if o % 2 else keep).at[o // 2], sems_out.at[i, o]
        )
        copy.start()
        departures.append(copy)

    rank = info[info.shape[0] - 1]
    wide = bias_ref.shape[1]
    span = ctx[0].shape[1]
    order = order_ref[...]
    vec = exact_dot(vec_ref[...], order, NT)
    gain1, bias1, gain2, bias2, bias_out, bias_down = (vec[i : i + 1] for i in range(6))

    pre_first = dot(x_ref[...], order, NT) + bias_out
    for o in range(heads):
        arrivals[0][o].wait()
        arrivals[1][o].wait()
        pre_first = pre_first + dot(ctx[o][...], up[o, :, wide : wide + span], NT)
    unit_first, inverse_first = standardise(pre_first)
    first = unit_first * gain1 + bias1
    first_low = first.astype(HALF)
    total = first + bias_down
    for o in range(heads):
        values = dot(first_low, up[o, :, :wide]) + bias_ref[pl.ds(rank ^ o, 1), :]
        below = 0.5 + 0.5 * lax.erf(values * math.sqrt(0.5))
        hidden = (values * below).astype(HALF)
        hidden_ref[o] = hidden
        slope_ref[o] = below + values * (
            jnp.exp2(values * values * (-0.5 * LOG2E)) * (1.0 / math.sqrt(2.0 * math.pi))
        )
        arrivals[2][o].wait()
        total = total + dot(hidden, down[o], NT)
    unit_second, inverse_second = standardise(total)
    out_ref[...] = dot((unit_second * gain2 + bias2).astype(HALF), order).astype(HALF)

    grad_out = dot(cot_ref[...], order, NT)
    grad_second = standardise_back(grad_out * gain2, unit_second, inverse_second)
    grad_down_low = grad_second.astype(HALF)
    grad_down_turned, first_turned = turn(grad_down_low), turn(first_low)
    grad_first = grad_second
    for o in range(heads):
        grad_down[o] = dot(grad_down_turned, hidden_ref[o]).astype(HALF)
        depart(1, o)
        grad_values = (slope_ref[o] * dot(grad_down_low, down[o])).astype(HALF)
        grad_bias_ref[pl.ds(rank ^ o, 1), :] = jnp.sum(
            grad_values.astype(FULL), axis=0, keepdims=True
        )
        grad_up[o, :, :wide] = dot(first_turned, grad_values).astype(HALF)
        grad_first = grad_first + dot(grad_values, up[o, :, :wide], NT)
    grad_pre = standardise_back(grad_first * gain1, unit_first, inverse_first)
    grad_low = grad_pre.astype(HALF)
    grad_turned = turn(grad_low)
    for o in range(heads):
        grad_ctx[o][...] = dot(grad_low, up[o, :, wide : wide + span]).astype(HALF)
        grad_up[o, :, wide : wide + span] = dot(grad_turned, ctx[o][...]).astype(HALF)
        if wide + span < up.shape[2]:
            grad_up[o, :, wide + span :] = jnp.zeros((up.shape[1], up.shape[2] - wide - span), HALF)
        depart(0, o)
    pre_ref[...] = exact_dot(grad_pre, order, NN)
    sums = [
        jnp.sum(part, axis=0, keepdims=True)
        for part in (
            grad_first * unit_first,
            grad_first,
            grad_out * unit_second,
            grad_out,
            grad_pre,
            grad_second,
        )
    ]
    sums_ref[...] = exact_dot(jnp.concatenate(sums + [jnp.zeros_like(sums[0])] * 2, axis=0), order, NN)
    for copy in departures:
        copy.wait()


def middle(info, x, cot, order, vec, bias, ctx, up, down, before):
    heads, (rows, width), wide = len(ctx), x.shape, bias.shape[1]
    up_shape, down_shape = (width, up[0].shape[2]), (width, wide)
    shape = jax.ShapeDtypeStruct
    results = pl.pallas_call(
        middle_kernel,
        out_shape=(
            shape((rows, width), HALF),
            shape((rows, width), FULL),
            shape(vec.shape, FULL),
            shape(bias.shape, FULL),
        )
        + tuple(shape(c.shape, HALF) for c in ctx)
        + tuple(shape((heads // 2,) + w, HALF) for w in (up_shape, up_shape, down_shape, down_shape)),
        in_specs=[SMEM_SPEC] + [VMEM_SPEC] * (5 + heads) + [ANY_SPEC] * (8 + len(before)),
        out_specs=(VMEM_SPEC,) * (4 + heads) + (ANY_SPEC,) * 4,
        scratch_shapes=[pltpu.VMEM((heads, rows, wide), FULL), pltpu.VMEM((heads, rows, wide), HALF)]
        + [pltpu.VMEM((heads,) + w, HALF) for w in (up_shape, down_shape, up_shape, down_shape)]
        + [pltpu.SemaphoreType.DMA((3, heads))] * 2,
        compiler_params=pltpu.CompilerParams(vmem_limit_bytes=48 * 2**20),
        cost_estimate=kernel_cost(20),
    )(info, x, cot, order, vec, bias, *ctx, *up, *down, *before)
    return results[:4] + (results[4 : 4 + heads],) + results[4 + heads :]


def by_row(parts, count):
    row = lax.broadcasted_iota(jnp.int32, (count, parts[0].shape[1]), 0)
    total = jnp.zeros(row.shape, FULL)
    for i, part in enumerate(parts):
        total = jnp.where(row == i, part, total)
    return total


def tail_kernel(
    info,
    dqkv_ref,
    offsets_ref,
    w_ref,
    inputs_ref,
    normed_ref,
    unit_ref,
    selector_ref,
    order_ref,
    norm_sums_ref,
    bias_up_ref,
    *refs,
):
    qkv_ref, parts_ref, normed_grad_ref, vector_ref = refs[-4:]
    rank = info[info.shape[0] - 1]
    width = dqkv_ref.shape[1] // 3
    owners, quarter = parts_ref.shape[:2]
    tables = dot(selector_ref[...], offsets_ref[...], NT).astype(HALF)
    turned_tables = dot(order_ref[...], tables).astype(HALF)
    weights = w_ref[...]
    grad_normed = dot(turned_tables, weights[:, : 2 * width], NT)
    normed_grad_ref[...] = grad_normed.astype(HALF)
    grads = dqkv_ref[...]
    grad_qkv = dot(inputs_ref[...], grads)
    qkv_ref[:, : 3 * width] = (
        jnp.concatenate(
            [
                grad_qkv[:, : 2 * width] + dot(normed_ref[...], turned_tables),
                grad_qkv[:, 2 * width :],
            ],
            axis=1,
        )
    ).astype(HALF)
    if 3 * width < qkv_ref.shape[1]:
        qkv_ref[:, 3 * width :] = jnp.zeros((qkv_ref.shape[0], qkv_ref.shape[1] - 3 * width), HALF)
    for o in range(owners):
        apart = rank ^ o
        parts_ref[(apart % 2) * (owners // 2) + apart // 2] = dot(
            dqkv_ref[o * quarter : (o + 1) * quarter, :], weights, NT
        ).astype(HALF)
    sums = jnp.sum(grads.astype(FULL), axis=0, keepdims=True)
    table_sums = jnp.sum(turned_tables.astype(FULL), axis=0, keepdims=True)
    sums = jnp.concatenate([sums[:, : 2 * width] + table_sums, sums[:, 2 * width :]], axis=1)
    sums = by_row([sums[:, i * width : (i + 1) * width] for i in range(3)], 8)
    places = (
        lax.broadcasted_iota(jnp.int32, (width, D), 1)
        == lax.broadcasted_iota(jnp.int32, (width, D), 0) + rank * width
    ).astype(FULL).astype(HALF)
    placed = exact_dot(sums, places, NN)
    norm_sums, bias_up = norm_sums_ref[...], bias_up_ref[...]
    parts = [norm_sums[i : i + 1] for i in range(4)]
    parts.append(jnp.sum(grad_normed * unit_ref[...].astype(FULL), axis=0, keepdims=True))
    parts.append(jnp.sum(grad_normed, axis=0, keepdims=True))
    parts += [norm_sums[i : i + 1] for i in range(4, 6)]
    parts += [placed[i : i + 1] for i in range(3)]
    parts += [bias_up[i : i + 1] for i in range(bias_up.shape[0])]
    vector_ref[...] = by_row(parts, vector_ref.shape[0])


def tail(
    info, dqkv, offsets, weights, inputs, normed, unit, selector, order, norm_sums, bias_up,
    owners, lanes, before,
):
    rows, shape = dqkv.shape[0], jax.ShapeDtypeStruct
    return pl.pallas_call(
        tail_kernel,
        out_shape=(
            shape((D, lanes), HALF),
            shape((owners, rows // owners, D), HALF),
            shape(normed.shape[::-1], HALF),
            shape((-(-(11 + bias_up.shape[0]) // 8) * 8, D), FULL),
        ),
        in_specs=[SMEM_SPEC] + [VMEM_SPEC] * 10 + [ANY_SPEC] * len(before),
        out_specs=(VMEM_SPEC,) * 4,
        compiler_params=pltpu.CompilerParams(vmem_limit_bytes=40 * 2**20),
        cost_estimate=kernel_cost(8),
    )(info, dqkv, offsets, weights, inputs, normed, unit, selector, order, norm_sums, bias_up, *before)


def index_steps(axis):
    size = lax.axis_size(axis)
    steps, bit = [], size // 2
    while bit >= 1:
        steps.append((axis, bit))
        bit //= 2
    return steps


def swap(values, step):
    axis, bit = step
    return lax.ppermute(values, axis, [(i, i ^ bit) for i in range(lax.axis_size(axis))])


def after(values, *others):
    return lax.optimization_barrier((values,) + others)[0]


def gather_blocks(values, steps, layout):
    taken = []
    for step in steps:
        place = sum(1 for other in taken if layout.index(other) < layout.index(step))
        taken.append(step)
        other = swap(values, step)
        values = jnp.concatenate(
            [jnp.expand_dims(values, place), jnp.expand_dims(other, place)], axis=place
        )
    return values


def gather_rows(values, steps):
    for step in steps:
        values = jnp.concatenate([values, swap(values, step)], axis=0)
    return values


def scatter_rows(values, steps):
    kind = values.dtype
    for i, step in enumerate(steps):
        half = values.shape[0] // 2
        values = values[:half].astype(FULL) + swap(values[half:], step).astype(FULL)
        if i < len(steps) - 1:
            values = values.astype(kind)
    return values


def add(*parts):
    return sum(part.astype(FULL) for part in parts).astype(HALF)


def block_owner(rank, steps, axis):
    places = np.arange(2 ** len(steps))
    offsets = sum(
        ((places >> i) & 1) * bit for i, (along, bit) in enumerate(steps) if along == axis
    )
    return jnp.asarray(offsets, jnp.int32) ^ rank


def one_hot(owners, per_block):
    own = (owners[:, None] * per_block + jnp.arange(per_block, dtype=jnp.int32)[None, :]).reshape(-1)
    return (own[:, None] == jnp.arange(own.shape[0], dtype=jnp.int32)[None, :]).astype(HALF)


def bucket_of(offset, buckets, longest):
    middle = buckets // 2
    distance = middle - 1 if abs(offset) < middle else abs(offset)
    sign_of = 1 if offset > 0 else -1 if offset < 0 else 0
    far_bucket = (
        math.ceil(math.log(distance / middle) / math.log((longest - 1) / middle) * (middle - 1))
        + middle
    )
    bucket = offset if distance <= middle else sign_of * far_bucket
    return min(max(bucket + buckets, 0), 2 * buckets - 1)


def offset_selector():
    selector = np.zeros((4 * MAXLEN, 2 * BUCKETS), dtype=np.float32)
    for offset in range(1 - MAXLEN, MAXLEN):
        selector[offset + 2 * MAXLEN - 1, bucket_of(offset, BUCKETS, MAXLEN)] = 1.0
    return selector


def nesterov(weight, moment, average, gradient, step_rate):
    decayed = gradient + DECAY * weight
    moment_new = MOMENTUM * moment + decayed
    weight_new = weight - step_rate * (decayed + MOMENTUM * moment_new)
    average_new = AVERAGE * average + (1.0 - AVERAGE) * weight_new
    return (weight_new, moment_new, average_new)


def column_sums(matrix):
    return jnp.sum(matrix, axis=0, dtype=FULL)


def per_device(
    inputs,
    seg_lengths,
    cotangent,
    qkv_weight,
    qkv_moment,
    qkv_average,
    out_weight,
    out_moment,
    out_average,
    up_weight,
    up_moment,
    up_average,
    down_weight,
    down_moment,
    down_average,
    rel_table,
    table_moment,
    table_average,
    vectors,
    vector_moment,
    vector_average,
):
    tok_rows = inputs.shape[0]
    head_count = lax.axis_size("head")
    dp_count = lax.axis_size("dp")
    head_rank = lax.axis_index("head")
    dp_rank = lax.axis_index("dp")
    local_heads = HEADS // head_count
    local_width = local_heads * HD
    quarter = tok_rows // head_count
    total_tokens = tok_rows * dp_count
    up_local = up_weight.shape[1]
    dp_steps, head_steps = index_steps("dp"), index_steps("head")
    device_count = dp_count * head_count

    width_order = one_hot(block_owner(dp_rank, dp_steps, "dp"), D // dp_count)
    inputs_across = dot(width_order, inputs, NT).astype(HALF)
    qkv_span = 3 * local_width
    qkv_lanes = -(-qkv_span // 128) * 128
    w_qkv_own = jnp.pad(
        jnp.concatenate([qkv_weight[i].astype(HALF) for i in range(3)], axis=1),
        ((0, 0), (0, qkv_lanes - qkv_span)),
    )
    unit_own, inverse_own = standardise(rel_table)
    vec_rows = vectors.shape[0]
    table_part = rel_table.shape[0]
    vec_high = vectors.astype(HALF)
    vec_low = (vectors - vec_high.astype(FULL)).astype(HALF)
    vec_lanes = -(-2 * vec_rows // table_part // 128) * 128
    vec_pack = jnp.pad(
        jnp.concatenate([vec_high, vec_low]), (0, table_part * vec_lanes - 2 * vec_rows)
    ).reshape(table_part, vec_lanes)
    small = jnp.concatenate([unit_own.astype(HALF), vec_pack], axis=1)
    small_steps = dp_steps[-1:] + head_steps[:1] + dp_steps[:-1] + head_steps[1:]
    small = gather_rows(small, small_steps)
    both_first = gather_rows(w_qkv_own, dp_steps[:1])
    w_qkv_turned = gather_rows(after(both_first, inputs_across), dp_steps[1:])[:, :qkv_span]
    owner = block_owner(dp_rank, small_steps, "dp") * head_count + block_owner(
        head_rank, small_steps, "head"
    )
    unit_table = small[:, :D]
    vec_used = -(-2 * vec_rows // vec_lanes)
    vec_all = (
        small[:, D:]
        .reshape(device_count, table_part, vec_lanes)[:, :vec_used]
        .reshape(device_count, vec_used * vec_lanes)
    )
    vec_all = dot(one_hot(owner, 1), vec_all, TN)
    vector_full = (vec_all[:, :vec_rows] + vec_all[:, vec_rows : 2 * vec_rows]).reshape(-1)
    vector_rows = vector_full[: 11 * D].reshape(11, D)

    far, core, low = head_steps[0], head_steps[1], dp_steps[-1]
    layout = [far] + dp_steps[::-1]
    half = D // 2
    wide_lanes = -(-(up_local + local_width) // 256) * 256
    up_out_own = jnp.pad(
        jnp.concatenate([up_weight, out_weight.T], axis=1).astype(HALF),
        ((0, 0), (0, wide_lanes - up_local - local_width)),
    )
    up_low = gather_blocks(up_out_own, dp_steps[:-1] + [far], layout)
    up_low = up_low.reshape(2, half, wide_lanes)
    down_near = gather_rows(after(down_weight.T.astype(HALF), both_first), dp_steps)
    up_high, down_far = swap(up_low, low), swap(down_near, far)
    up_low_core, down_near_core = swap(up_low, core), swap(down_near, core)
    differences = list(range(head_count))

    table_order = one_hot(owner, table_part)
    w_qkv = dot(width_order, w_qkv_turned, TN).astype(HALF)

    def head_part(row_values):
        return lax.dynamic_slice_in_dim(row_values, head_rank * local_width, local_width)

    bias_qkv = jnp.concatenate([head_part(vector_rows[8 + i]) for i in range(3)])
    normed = (unit_table.astype(FULL) * vector_rows[4] + vector_rows[5]).astype(HALF)
    normed_across = dot(width_order, normed, NT).astype(HALF)
    tables = (dot(normed, w_qkv[:, : 2 * local_width]) + bias_qkv[: 2 * local_width]).astype(HALF)
    tables = dot(table_order, tables, TN).astype(HALF)
    selector = offset_selector()[::-1]
    by_offset = dot(jnp.asarray(selector, dtype=HALF), tables).astype(HALF)
    qkv = (dot(inputs, w_qkv) + bias_qkv).astype(HALF)
    info = jnp.concatenate([seg_lengths[0], head_rank[None].astype(jnp.int32)])
    context, probs = attention_forward(info, qkv, by_offset, head_count, (up_low, down_near))
    up_high, down_far, _ = lax.optimization_barrier((up_high, down_far, context))
    up_high_core, down_far_core = swap(up_high, core), swap(down_far, core)

    def exchange(blocks):
        return {
            o: swap(block, ("head", o)) if o else block for o, block in blocks.items()
        }

    context_low = exchange({o: context[o * quarter : (o + 1) * quarter] for o in differences})

    def own_tokens(values):
        return lax.dynamic_slice_in_dim(values, head_rank * quarter, quarter, 0)

    vec = jnp.concatenate([vector_rows[:4], vector_rows[6:8], vector_rows[:2]], axis=0)
    bias_up = vector_full[11 * D :].reshape(head_count, up_local)
    output, grad_pre_first, norm_sums, grad_bias_up, grad_context, *weight_grads = middle(
        info,
        own_tokens(inputs),
        own_tokens(cotangent),
        width_order,
        vec,
        bias_up,
        [context_low[o] for o in differences],
        (up_low, up_high, up_low_core, up_high_core),
        (down_near, down_near_core, down_far, down_far_core),
        (normed_across, table_order),
    )

    def fold(blocks, step):
        bit = step[1]
        return {
            o: (block.astype(FULL) + swap(blocks[o ^ bit], step).astype(FULL)).astype(HALF)
            for o, block in blocks.items()
            if not o & bit
        }

    up_keep, up_send, down_keep, down_send = weight_grads
    grad_context = exchange(dict(zip(differences, grad_context)))
    grad_context = jnp.concatenate([grad_context[o] for o in differences], axis=0)
    up_got, down_got, _ = lax.optimization_barrier(
        (swap(up_send, core), swap(down_send, core), grad_context)
    )
    up_leaves = add(up_keep[:, half:], up_got[:, half:])
    down_leaves = add(down_keep[1], down_got[1])
    grad_qkv_low, grad_offsets = attention_backward(
        info,
        qkv,
        by_offset,
        probs,
        grad_context,
        head_count,
        (up_leaves, down_leaves),
    )
    up_got_low, down_got_far, _ = lax.optimization_barrier(
        (swap(up_leaves, low), swap(down_leaves, far), grad_qkv_low)
    )
    up_next, up_stays = (
        add(up_keep[i, :half], up_got[i, :half], up_got_low[i]) for i in (1, 0)
    )
    down_next, down_stays = (
        add(down_keep[0, rows], down_got[0, rows], down_got_far[rows])
        for rows in (slice(half, D), slice(0, half))
    )
    grad_qkv, input_parts, grad_normed, grad_vector = tail(
        info,
        grad_qkv_low,
        grad_offsets,
        w_qkv,
        inputs_across,
        normed_across,
        unit_table,
        jnp.asarray(selector.T, dtype=HALF),
        table_order,
        norm_sums,
        grad_bias_up,
        head_count,
        qkv_lanes,
        (up_next, down_next),
    )
    up_out_shard = scatter_rows(add(up_stays, swap(up_next, far)), dp_steps[:-1][::-1])
    up_shard = up_out_shard[:, :up_local]
    out_shard = up_out_shard[:, up_local : up_local + local_width].T
    down_shard = scatter_rows(add(down_stays, swap(down_next, low)), dp_steps[:-1][::-1]).T
    qkv_shard = scatter_rows(grad_qkv, dp_steps[::-1])
    input_both = scatter_rows(input_parts, head_steps[-1:]).astype(HALF)
    input_grad = grad_pre_first + scatter_rows(input_both, head_steps[:-1][::-1])[0]

    vec_lanes = -(-vec_rows // 128) * 128
    grad_vector = jnp.pad(
        grad_vector.reshape(-1)[: device_count * vec_rows].reshape(device_count, vec_rows),
        ((0, 0), (0, vec_lanes - vec_rows)),
    )
    grad_vector = dot(one_hot(owner, 1), grad_vector.astype(HALF)).astype(HALF)
    spare = -(-vec_lanes // table_part // 128) * 128 * table_part
    grad_vector = jnp.pad(grad_vector, ((0, 0), (0, spare - vec_lanes)))
    grad_vector = grad_vector.reshape(device_count * table_part, -1)
    small_shard = scatter_rows(
        jnp.concatenate([grad_normed, grad_vector], axis=1), small_steps[::-1]
    )
    table_shard = standardise_back(small_shard[:, :D] * vector_rows[4], unit_own, inverse_own)
    vector_shard = small_shard[:, D:].reshape(-1)[:vec_rows]

    qkv_grad_shard = jnp.stack(
        [qkv_shard[:, i * local_width : (i + 1) * local_width] for i in range(3)]
    )
    new_qkv = nesterov(
        qkv_weight, qkv_moment, qkv_average, qkv_grad_shard, 0.75 / math.sqrt(D * total_tokens)
    )
    new_out = nesterov(
        out_weight,
        out_moment,
        out_average,
        out_shard,
        0.125 * MAXLEN / math.sqrt(D * total_tokens),
    )
    new_up = nesterov(up_weight, up_moment, up_average, up_shard, 1.1 / math.sqrt(D * total_tokens))
    new_down = nesterov(
        down_weight, down_moment, down_average, down_shard, 1.0 / math.sqrt(FF * total_tokens)
    )
    new_table = nesterov(
        rel_table,
        table_moment,
        table_average,
        table_shard,
        0.55 * math.sqrt(MAXLEN / total_tokens),
    )
    new_vector = nesterov(
        vectors, vector_moment, vector_average, vector_shard, 0.3 / math.sqrt(total_tokens)
    )
    return (output, input_grad) + new_qkv + new_out + new_up + new_down + new_table + new_vector


def solution(mesh):
    rows = P("dp", None)
    owned = P(("dp", "head"), None)
    qkv = P(None, "dp", "head")
    out = P("head", "dp")
    up = P("dp", "head")
    vector = P(("dp", "head"))
    return jax.shard_map(
        per_device,
        mesh=mesh,
        in_specs=(rows,) * 3 + (qkv,) * 3 + (out,) * 3 + (up,) * 3 + (out,) * 3 + (owned,) * 3 + (vector,) * 3,
        out_specs=(owned,) * 2 + (qkv,) * 3 + (out,) * 3 + (up,) * 3 + (out,) * 3 + (owned,) * 3 + (vector,) * 3,
        check_vma=False,
    )
```

```python
import functools
import math

import jax
import jax.numpy as jnp
import numpy as np
from jax import lax
from jax.experimental import pallas as pl
from jax.experimental.pallas import tpu as pltpu
from jax.sharding import PartitionSpec as P

D = 768
HEADS = 12
HD = 64
FF = 3072
BUCKETS = 256
MAXLEN = 512

EPSILON = 1e-07
MOMENTUM = 0.9
DECAY = 0.01
AVERAGE = 0.7
MASKED = -1e30

TILE = 128
NARROW = 5
SCALE = (3.0 * HD) ** -0.5
LOG2E = math.log2(math.e)
HALF = jnp.bfloat16
FULL = jnp.float32
NN = (((1,), (0,)), ((), ()))
NT = (((1,), (1,)), ((), ()))
TN = (((0,), (0,)), ((), ()))


def dot(left, right, dims=NN):
    return lax.dot_general(left, right, dims, preferred_element_type=FULL)


def shear(values, count, low):
    rolled = [
        pltpu.roll(values[:, m * TILE : (m + 1) * TILE], 0, 1, stride=1, stride_axis=0)
        for m in range(count + 1)
    ]
    return jnp.concatenate(
        [jnp.where(low, rolled[m], rolled[m + 1]) for m in range(count)], axis=1
    )


def unshear(values, count, after, shift):
    rolled = [
        pltpu.roll(values[:, m * TILE : (m + 1) * TILE], shift, 1, stride=1, stride_axis=0)
        for m in range(count)
    ]
    zero = jnp.zeros((TILE, TILE), values.dtype)
    return jnp.concatenate(
        [
            jnp.where(
                after, rolled[m] if m < count else zero, rolled[m - 1] if m > 0 else zero
            ).astype(HALF)
            for m in range(count + 1)
        ],
        axis=1,
    )


def flip_matrix():
    across = lax.broadcasted_iota(jnp.int32, (TILE, TILE), 1)
    down = lax.broadcasted_iota(jnp.int32, (TILE, TILE), 0)
    return (across + down == TILE - 1).astype(FULL).astype(HALF)


def tiles_of(block, count=1):
    return pl.ds(pl.multiple_of(block * TILE, TILE), count * TILE)


def sequence_bounds(ends, first, last):
    start, stop = jnp.int32(0), jnp.int32(0)
    begin = jnp.int32(0)
    for end in ends:
        start = jnp.where((begin <= first) & (first < end), begin, start)
        stop = jnp.where((begin <= last) & (last < end), end, stop)
        begin = end
    return start, stop


def by_window(ends, block, tiles, body):
    start, stop = sequence_bounds(ends, block * TILE, block * TILE + TILE - 1)
    first = start // TILE
    narrow = min(NARROW, tiles)
    fits = (stop + TILE - 1) // TILE - first <= narrow

    @pl.when(fits)
    def _():
        body(narrow, jnp.minimum(first, tiles - narrow))

    @pl.when(jnp.logical_not(fits))
    def _():
        body(tiles, jnp.int32(0))


def sequence_ends(info, count):
    ends, total = [], jnp.int32(0)
    for s in range(count):
        total = total + info[s]
        ends.append(total)
    return ends


def sequence_of(places, ends):
    return sum((places >= end).astype(jnp.int32) for end in ends[:-1])


def turned(block, rank, per_owner):
    return ((block // per_owner) ^ rank) * per_owner + block % per_owner


def forward_kernel(
    info,
    qkv_ref,
    tab_ref,
    _up_ref,
    _down_ref,
    ctx_ref,
    p_ref,
    q_ref,
    k_ref,
    v_ref,
    qb_ref,
    kb_ref,
    p2c_ref,
    *,
    owners,
):
    heads, tiles = q_ref.shape[0], q_ref.shape[1] // TILE
    segments = info.shape[0] - 1
    rank, per_owner = info[segments], tiles // owners
    ends = sequence_ends(info, segments)
    across = lax.broadcasted_iota(jnp.int32, (TILE, TILE), 1)
    down = lax.broadcasted_iota(jnp.int32, (TILE, TILE), 0)
    low = across < down
    flip = flip_matrix()
    for h in range(heads):
        for i, ref in enumerate((q_ref, k_ref, v_ref)):
            ref[h] = qkv_ref[:, (i * heads + h) * HD : (i * heads + h + 1) * HD]
        for i, ref in enumerate((qb_ref, kb_ref)):
            ref[h] = tab_ref[:, (i * heads + h) * HD : (i * heads + h + 1) * HD]

    def p2c_block(block, carried):
        rows = tiles_of(block)

        def body(count, first):
            offsets = tiles_of(first - block + tiles - 1, count + 1)
            for h in range(heads):
                sheared = shear(dot(k_ref[h, rows, :], qb_ref[h, offsets, :], NT), count, low)
                for m in range(count):
                    p2c_ref[h, tiles_of(first + m), rows] = sheared[
                        :, m * TILE : (m + 1) * TILE
                    ].T

        by_window(ends, block, tiles, body)
        return carried

    lax.fori_loop(0, tiles, p2c_block, 0)

    def score_block(block, carried):
        rows = tiles_of(block)
        row_sequence = sequence_of(down + block * TILE, ends)

        def body(count, first):
            cols = tiles_of(first, count)
            offsets = tiles_of(first - block + tiles - 1, count + 1)
            same = [
                row_sequence == sequence_of(across + (first + m) * TILE, ends) for m in range(count)
            ]
            same = jnp.concatenate(same, axis=1)
            contexts = []
            for h in range(heads):
                query = q_ref[h, rows, :]
                c2p = shear(dot(query, kb_ref[h, offsets, :], NT), count, low)
                raw = dot(query, k_ref[h, cols, :], NT) + c2p + p2c_ref[h, rows, cols]
                scores = jnp.where(same, (SCALE * LOG2E) * raw, MASKED)
                powers = jnp.exp2(scores - jnp.max(scores, axis=1, keepdims=True))
                probs = (powers * (1.0 / jnp.sum(powers, axis=1, keepdims=True))).astype(HALF)
                for m in range(count):
                    p_ref[h, rows, tiles_of(tiles - 1 - first - m)] = dot(
                        probs[:, m * TILE : (m + 1) * TILE], flip
                    ).astype(HALF)
                contexts.append(dot(probs, v_ref[h, cols, :]).astype(HALF))
            ctx_ref[tiles_of(turned(block, rank, per_owner)), :] = jnp.concatenate(contexts, axis=1)

        by_window(ends, block, tiles, body)
        return carried

    lax.fori_loop(0, tiles, score_block, 0)


def backward_kernel(
    info,
    qkv_ref,
    tab_ref,
    p_ref,
    g_ref,
    *refs,
    owners,
):
    dqkv_ref, gtab_ref, q_ref, k_ref, krev_ref, vrev_ref, qbs_ref, kbs_ref = refs[-12:-4]
    grad_ref, dst_ref, dvt_ref, gsum_ref = refs[-4:]
    heads, tiles = q_ref.shape[0], q_ref.shape[1] // TILE
    width = heads * HD
    segments = info.shape[0] - 1
    rank, per_owner = info[segments], tiles // owners
    ends = sequence_ends(info, segments)
    across = lax.broadcasted_iota(jnp.int32, (TILE, TILE), 1)
    down = lax.broadcasted_iota(jnp.int32, (TILE, TILE), 0)
    flip = flip_matrix()
    dst_ref[...] = jnp.zeros_like(dst_ref)
    dvt_ref[...] = jnp.zeros_like(dvt_ref)
    gsum_ref[...] = jnp.zeros_like(gsum_ref)
    for h in range(heads):
        q_ref[h] = qkv_ref[:, h * HD : (h + 1) * HD]
        k_ref[h] = qkv_ref[:, width + h * HD : width + (h + 1) * HD]
        qbs_ref[h] = tab_ref[:, h * HD : (h + 1) * HD]
        grad_ref[h] = g_ref[:, h * HD : (h + 1) * HD]
    for m in range(tiles):
        here, there = slice(m * TILE, (m + 1) * TILE), slice((tiles - 1 - m) * TILE, (tiles - m) * TILE)
        turned_rows = dot(flip, qkv_ref[here, width:]).astype(HALF)
        for h in range(heads):
            krev_ref[h, there, :] = turned_rows[:, h * HD : (h + 1) * HD]
            vrev_ref[h, there, :] = turned_rows[:, width + h * HD : width + (h + 1) * HD]
    for m in range(2 * tiles):
        here = slice(m * TILE, (m + 1) * TILE)
        there = slice((2 * tiles - 1 - m) * TILE, (2 * tiles - m) * TILE)
        turned_rows = dot(flip, tab_ref[here, width:]).astype(HALF)
        for h in range(heads):
            kbs_ref[h, there, :] = turned_rows[:, h * HD : (h + 1) * HD]

    def query_block(block, carried):
        rows = tiles_of(block)

        def body(count, first):
            start = tiles - first - count
            cols = tiles_of(start, count)
            offsets = tiles_of(block + start, count + 1)
            grads = []
            for h in range(heads):
                grad = grad_ref[h, tiles_of(turned(block, rank, per_owner)), :]
                probs_low = p_ref[h, rows, cols]
                probs = probs_low.astype(FULL)
                grad_probs = dot(grad, vrev_ref[h, cols, :], NT)
                inner = jnp.sum(probs * grad_probs, axis=1, keepdims=True)
                grad_raw = (probs * (grad_probs - inner)) * SCALE
                by_offset = unshear(grad_raw, count, across >= down, 0)
                grads.append(
                    (
                        dot(grad_raw.astype(HALF), krev_ref[h, cols, :])
                        + dot(by_offset, kbs_ref[h, offsets, :])
                    ).astype(HALF)
                )
                gsum_ref[heads + h, :, offsets] += dot(
                    q_ref[h, rows, :].astype(FULL).T.astype(HALF), by_offset
                )
                dvt_ref[h, :, cols] += dot(grad.astype(FULL).T.astype(HALF), probs_low)
                for m in range(count):
                    dst_ref[h, tiles_of(start + m), rows] = grad_raw[
                        :, m * TILE : (m + 1) * TILE
                    ].T
            dqkv_ref[rows, :width] = jnp.concatenate(grads, axis=1)

        by_window(ends, block, tiles, body)
        return carried

    lax.fori_loop(0, tiles, query_block, 0)

    def key_block(block, carried):
        rows, back = tiles_of(block), tiles_of(tiles - 1 - block)

        def body(count, first):
            cols = tiles_of(first, count)
            offsets = tiles_of(tiles - 1 - block + first, count + 1)
            grads = []
            for h in range(heads):
                grad_raw = dst_ref[h, back, cols]
                by_offset = unshear(grad_raw, count, across > down, 1)
                grads.append(
                    (
                        dot(grad_raw.astype(HALF), q_ref[h, cols, :])
                        + dot(by_offset, qbs_ref[h, offsets, :])
                    ).astype(HALF)
                )
                gsum_ref[h, :, offsets] += dot(
                    krev_ref[h, back, :].astype(FULL).T.astype(HALF), by_offset
                )
            grads += [dvt_ref[h, :, back].T.astype(HALF) for h in range(heads)]
            dqkv_ref[rows, width:] = dot(flip, jnp.concatenate(grads, axis=1)).astype(HALF)

        by_window(ends, block, tiles, body)
        return carried

    lax.fori_loop(0, tiles, key_block, 0)
    for i in range(heads):
        gtab_ref[i * HD : (i + 1) * HD, :] = gsum_ref[i].astype(HALF)
        for m in range(2 * tiles):
            there = slice((2 * tiles - 1 - m) * TILE, (2 * tiles - m) * TILE)
            gtab_ref[width + i * HD : width + (i + 1) * HD, there] = dot(
                gsum_ref[heads + i, :, m * TILE : (m + 1) * TILE].astype(HALF), flip
            ).astype(HALF)


SMEM_SPEC = pl.BlockSpec(memory_space=pltpu.SMEM)
VMEM_SPEC = pl.BlockSpec(memory_space=pltpu.VMEM)
ANY_SPEC = pl.BlockSpec(memory_space=pl.ANY)


def kernel_cost(microseconds):
    return pl.CostEstimate(
        flops=int(microseconds * 1e9), bytes_accessed=int(microseconds * 1e6), transcendentals=0
    )


def attention_forward(info, qkv, tables, owners, before):
    rows, heads = qkv.shape[0], qkv.shape[1] // (3 * HD)
    small, wide = pltpu.VMEM((heads, rows, HD), HALF), pltpu.VMEM((heads, 2 * rows, HD), HALF)
    return pl.pallas_call(
        functools.partial(forward_kernel, owners=owners),
        out_shape=(
            jax.ShapeDtypeStruct((rows, heads * HD), HALF),
            jax.ShapeDtypeStruct((heads, rows, rows), HALF),
        ),
        in_specs=[SMEM_SPEC] + [VMEM_SPEC] * 2 + [ANY_SPEC] * len(before),
        out_specs=(VMEM_SPEC,) * 2,
        scratch_shapes=[small] * 3 + [wide] * 2 + [pltpu.VMEM((heads, rows, rows), FULL)],
        compiler_params=pltpu.CompilerParams(vmem_limit_bytes=48 * 2**20),
        cost_estimate=kernel_cost(30),
    )(info, qkv, tables, *before)


def attention_backward(info, qkv, tables, probs, grad, owners, before):
    rows, heads = qkv.shape[0], qkv.shape[1] // (3 * HD)
    shape = jax.ShapeDtypeStruct
    small, wide = pltpu.VMEM((heads, rows, HD), HALF), pltpu.VMEM((heads, 2 * rows, HD), HALF)
    return pl.pallas_call(
        functools.partial(backward_kernel, owners=owners),
        out_shape=(shape(qkv.shape, HALF), shape((2 * heads * HD, 2 * rows), HALF)),
        in_specs=[SMEM_SPEC] + [VMEM_SPEC] * 4 + [ANY_SPEC] * len(before),
        out_specs=(VMEM_SPEC,) * 2,
        scratch_shapes=[small] * 4
        + [wide] * 2
        + [
            small,
            pltpu.VMEM((heads, rows, rows), FULL),
            pltpu.VMEM((heads, HD, rows), FULL),
            pltpu.VMEM((2 * heads, HD, 2 * rows), FULL),
        ],
        compiler_params=pltpu.CompilerParams(vmem_limit_bytes=52 * 2**20),
        cost_estimate=kernel_cost(34),
    )(info, qkv, tables, probs, grad, *before)


def standardise(values):
    center = values - jnp.mean(values, axis=-1, keepdims=True)
    spread = jnp.mean(center * center, axis=-1, keepdims=True)
    inverse = lax.rsqrt(spread + EPSILON)
    return center * inverse, inverse


def standardise_back(grad, unit, inverse):
    return inverse * (
        grad
        - jnp.mean(grad, axis=-1, keepdims=True)
        - unit * jnp.mean(grad * unit, axis=-1, keepdims=True)
    )


def exact_dot(values, order, dims):
    high = values.astype(HALF)
    rest = values - high.astype(FULL)
    middle = rest.astype(HALF)
    last = (rest - middle.astype(FULL)).astype(HALF)
    return dot(high, order, dims) + dot(middle, order, dims) + dot(last, order, dims)


def turn(values):
    return values.astype(FULL).T.astype(HALF)


def middle_kernel(info, x_ref, cot_ref, order_ref, vec_ref, bias_ref, *refs):
    heads = bias_ref.shape[0]
    ctx, up_far, down_far = refs[:heads], refs[heads : heads + 8], refs[heads + 8 : heads + 12]
    half, chunk = up_far[0].shape[0], down_far[0].shape[1]
    refs = refs[len(refs) - heads - 16 :]
    out_ref, pre_ref, sums_ref, grad_bias_ref = refs[:4]
    grad_ctx = refs[4 : heads + 4]
    up_keep, up_send, down_keep, down_send = refs[heads + 4 : heads + 8]
    slope_ref, hidden_ref, up, down, grad_up, grad_down, sems_in, sems_out = refs[heads + 8 :]
    arrivals = [
        [
            pltpu.make_async_copy(
                up_far[4 * (o % 2) + 2 * (o // 2) + i],
                up.at[o, i * half : (i + 1) * half],
                sems_in.at[i, o],
            )
            for o in range(heads)
        ]
        for i in range(2)
    ]
    arrivals += [
        [
            pltpu.make_async_copy(
                down_far[2 * (o % 2) + i % 2].at[2 * (o // 2) + i // 2],
                down.at[o, i * chunk : (i + 1) * chunk],
                sems_in.at[2 + i, o],
            )
            for o in range(heads)
        ]
        for i in range(4)
    ]
    for copies in arrivals:
        for copy in copies:
            copy.start()
    departures = []

    def depart(i, o):
        near, keep, send = ((grad_up, up_keep, up_send), (grad_down, down_keep, down_send))[i]
        copy = pltpu.make_async_copy(
            near.at[o], (send if o % 2 else keep).at[o // 2], sems_out.at[i, o]
        )
        copy.start()
        departures.append(copy)

    rank = info[info.shape[0] - 1]
    wide = bias_ref.shape[1]
    span = ctx[0].shape[1]
    order = order_ref[...]
    vec = exact_dot(vec_ref[...], order, NT)
    gain1, bias1, gain2, bias2, bias_out, bias_down = (vec[i : i + 1] for i in range(6))

    pre_first = dot(x_ref[...], order, NT) + bias_out
    for o in range(heads):
        arrivals[0][o].wait()
        arrivals[1][o].wait()
        pre_first = pre_first + dot(ctx[o][...], up[o, :, wide : wide + span], NT)
    unit_first, inverse_first = standardise(pre_first)
    first = unit_first * gain1 + bias1
    first_low = first.astype(HALF)
    total = first + bias_down
    for o in range(heads):
        values = dot(first_low, up[o, :, :wide]) + bias_ref[pl.ds(rank ^ o, 1), :]
        below = 0.5 + 0.5 * lax.erf(values * math.sqrt(0.5))
        hidden = (values * below).astype(HALF)
        hidden_ref[o] = hidden
        slope_ref[o] = below + values * (
            jnp.exp2(values * values * (-0.5 * LOG2E)) * (1.0 / math.sqrt(2.0 * math.pi))
        )
        for copies in arrivals[2:]:
            copies[o].wait()
        total = total + dot(hidden, down[o], NT)
    unit_second, inverse_second = standardise(total)
    out_ref[...] = dot((unit_second * gain2 + bias2).astype(HALF), order).astype(HALF)

    grad_out = dot(cot_ref[...], order, NT)
    grad_second = standardise_back(grad_out * gain2, unit_second, inverse_second)
    grad_down_low = grad_second.astype(HALF)
    grad_down_turned, first_turned = turn(grad_down_low), turn(first_low)
    grad_first = grad_second
    for o in range(heads):
        grad_down[o] = dot(grad_down_turned, hidden_ref[o]).astype(HALF)
        depart(1, o)
        grad_values = (slope_ref[o] * dot(grad_down_low, down[o])).astype(HALF)
        grad_bias_ref[pl.ds(rank ^ o, 1), :] = jnp.sum(
            grad_values.astype(FULL), axis=0, keepdims=True
        )
        grad_up[o, :, :wide] = dot(first_turned, grad_values).astype(HALF)
        grad_first = grad_first + dot(grad_values, up[o, :, :wide], NT)
    grad_pre = standardise_back(grad_first * gain1, unit_first, inverse_first)
    grad_low = grad_pre.astype(HALF)
    grad_turned = turn(grad_low)
    for o in range(heads):
        grad_ctx[o][...] = dot(grad_low, up[o, :, wide : wide + span]).astype(HALF)
        grad_up[o, :, wide : wide + span] = dot(grad_turned, ctx[o][...]).astype(HALF)
        if wide + span < up.shape[2]:
            grad_up[o, :, wide + span :] = jnp.zeros((up.shape[1], up.shape[2] - wide - span), HALF)
        depart(0, o)
    pre_ref[...] = exact_dot(grad_pre, order, NN)
    sums = [
        jnp.sum(part, axis=0, keepdims=True)
        for part in (
            grad_first * unit_first,
            grad_first,
            grad_out * unit_second,
            grad_out,
            grad_pre,
            grad_second,
        )
    ]
    sums_ref[...] = exact_dot(jnp.concatenate(sums + [jnp.zeros_like(sums[0])] * 2, axis=0), order, NN)
    for copy in departures:
        copy.wait()


def middle(info, x, cot, order, vec, bias, ctx, up, down, before):
    heads, (rows, width), wide = len(ctx), x.shape, bias.shape[1]
    up_shape, down_shape = (width, up[0].shape[1]), (width, wide)
    shape = jax.ShapeDtypeStruct
    results = pl.pallas_call(
        middle_kernel,
        out_shape=(
            shape((rows, width), HALF),
            shape((rows, width), FULL),
            shape(vec.shape, FULL),
            shape(bias.shape, FULL),
        )
        + tuple(shape(c.shape, HALF) for c in ctx)
        + tuple(shape((heads // 2,) + w, HALF) for w in (up_shape, up_shape, down_shape, down_shape)),
        in_specs=[SMEM_SPEC] + [VMEM_SPEC] * (5 + heads) + [ANY_SPEC] * (12 + len(before)),
        out_specs=(VMEM_SPEC,) * (4 + heads) + (ANY_SPEC,) * 4,
        scratch_shapes=[pltpu.VMEM((heads, rows, wide), FULL), pltpu.VMEM((heads, rows, wide), HALF)]
        + [pltpu.VMEM((heads,) + w, HALF) for w in (up_shape, down_shape, up_shape, down_shape)]
        + [pltpu.SemaphoreType.DMA((6, heads))] * 2,
        compiler_params=pltpu.CompilerParams(vmem_limit_bytes=48 * 2**20),
        cost_estimate=kernel_cost(20),
    )(info, x, cot, order, vec, bias, *ctx, *up, *down, *before)
    return results[:4] + (results[4 : 4 + heads],) + results[4 + heads :]


def by_row(parts, count):
    row = lax.broadcasted_iota(jnp.int32, (count, parts[0].shape[1]), 0)
    total = jnp.zeros(row.shape, FULL)
    for i, part in enumerate(parts):
        total = jnp.where(row == i, part, total)
    return total


def tail_kernel(
    info,
    dqkv_ref,
    offsets_ref,
    w_ref,
    inputs_ref,
    normed_ref,
    unit_ref,
    selector_ref,
    order_ref,
    norm_sums_ref,
    bias_up_ref,
    *refs,
):
    qkv_ref, parts_ref, normed_grad_ref, vector_ref = refs[-4:]
    rank = info[info.shape[0] - 1]
    width = dqkv_ref.shape[1] // 3
    owners, quarter = parts_ref.shape[:2]
    tables = dot(selector_ref[...], offsets_ref[...], NT).astype(HALF)
    turned_tables = dot(order_ref[...], tables).astype(HALF)
    weights = w_ref[...]
    grad_normed = dot(turned_tables, weights[:, : 2 * width], NT)
    normed_grad_ref[...] = grad_normed.astype(HALF)
    grads = dqkv_ref[...]
    grad_qkv = dot(inputs_ref[...], grads)
    qkv_ref[:, : 3 * width] = (
        jnp.concatenate(
            [
                grad_qkv[:, : 2 * width] + dot(normed_ref[...], turned_tables),
                grad_qkv[:, 2 * width :],
            ],
            axis=1,
        )
    ).astype(HALF)
    if 3 * width < qkv_ref.shape[1]:
        qkv_ref[:, 3 * width :] = jnp.zeros((qkv_ref.shape[0], qkv_ref.shape[1] - 3 * width), HALF)
    for o in range(owners):
        apart = rank ^ o
        parts_ref[(apart % 2) * (owners // 2) + apart // 2] = dot(
            dqkv_ref[o * quarter : (o + 1) * quarter, :], weights, NT
        ).astype(HALF)
    sums = jnp.sum(grads.astype(FULL), axis=0, keepdims=True)
    table_sums = jnp.sum(turned_tables.astype(FULL), axis=0, keepdims=True)
    sums = jnp.concatenate([sums[:, : 2 * width] + table_sums, sums[:, 2 * width :]], axis=1)
    sums = by_row([sums[:, i * width : (i + 1) * width] for i in range(3)], 8)
    places = (
        lax.broadcasted_iota(jnp.int32, (width, D), 1)
        == lax.broadcasted_iota(jnp.int32, (width, D), 0) + rank * width
    ).astype(FULL).astype(HALF)
    placed = exact_dot(sums, places, NN)
    norm_sums, bias_up = norm_sums_ref[...], bias_up_ref[...]
    parts = [norm_sums[i : i + 1] for i in range(4)]
    parts.append(jnp.sum(grad_normed * unit_ref[...].astype(FULL), axis=0, keepdims=True))
    parts.append(jnp.sum(grad_normed, axis=0, keepdims=True))
    parts += [norm_sums[i : i + 1] for i in range(4, 6)]
    parts += [placed[i : i + 1] for i in range(3)]
    parts += [bias_up[i : i + 1] for i in range(bias_up.shape[0])]
    vector_ref[...] = by_row(parts, vector_ref.shape[0])


def tail(
    info, dqkv, offsets, weights, inputs, normed, unit, selector, order, norm_sums, bias_up,
    owners, lanes, before,
):
    rows, shape = dqkv.shape[0], jax.ShapeDtypeStruct
    return pl.pallas_call(
        tail_kernel,
        out_shape=(
            shape((D, lanes), HALF),
            shape((owners, rows // owners, D), HALF),
            shape(normed.shape[::-1], HALF),
            shape((-(-(11 + bias_up.shape[0]) // 8) * 8, D), FULL),
        ),
        in_specs=[SMEM_SPEC] + [VMEM_SPEC] * 10 + [ANY_SPEC] * len(before),
        out_specs=(VMEM_SPEC,) * 4,
        compiler_params=pltpu.CompilerParams(vmem_limit_bytes=40 * 2**20),
        cost_estimate=kernel_cost(0.1),
    )(info, dqkv, offsets, weights, inputs, normed, unit, selector, order, norm_sums, bias_up, *before)


def index_steps(axis):
    size = lax.axis_size(axis)
    steps, bit = [], size // 2
    while bit >= 1:
        steps.append((axis, bit))
        bit //= 2
    return steps


def swap(values, step):
    axis, bit = step
    return lax.ppermute(values, axis, [(i, i ^ bit) for i in range(lax.axis_size(axis))])


def after(values, *others):
    return lax.optimization_barrier((values,) + others)[0]


def swap_both(values, one, other):
    (axis, bit), (along, place) = one, other
    width = lax.axis_size(along)
    count = lax.axis_size(axis) * width
    return lax.ppermute(
        values, (axis, along), [(i, i ^ (bit * width) ^ place) for i in range(count)]
    )


def gather_blocks(values, steps, layout):
    taken = []
    for step in steps:
        place = sum(1 for other in taken if layout.index(other) < layout.index(step))
        taken.append(step)
        other = swap(values, step)
        values = jnp.concatenate(
            [jnp.expand_dims(values, place), jnp.expand_dims(other, place)], axis=place
        )
    return values


def gather_rows(values, steps):
    for step in steps:
        values = jnp.concatenate([values, swap(values, step)], axis=0)
    return values


def scatter_rows(values, steps):
    kind = values.dtype
    for i, step in enumerate(steps):
        half = values.shape[0] // 2
        values = values[:half].astype(FULL) + swap(values[half:], step).astype(FULL)
        if i < len(steps) - 1:
            values = values.astype(kind)
    return values


def add(*parts):
    return sum(part.astype(FULL) for part in parts).astype(HALF)


def block_owner(rank, steps, axis):
    places = np.arange(2 ** len(steps))
    offsets = sum(
        ((places >> i) & 1) * bit for i, (along, bit) in enumerate(steps) if along == axis
    )
    return jnp.asarray(offsets, jnp.int32) ^ rank


def one_hot(owners, per_block):
    own = (owners[:, None] * per_block + jnp.arange(per_block, dtype=jnp.int32)[None, :]).reshape(-1)
    return (own[:, None] == jnp.arange(own.shape[0], dtype=jnp.int32)[None, :]).astype(HALF)


def bucket_of(offset, buckets, longest):
    middle = buckets // 2
    distance = middle - 1 if abs(offset) < middle else abs(offset)
    sign_of = 1 if offset > 0 else -1 if offset < 0 else 0
    far_bucket = (
        math.ceil(math.log(distance / middle) / math.log((longest - 1) / middle) * (middle - 1))
        + middle
    )
    bucket = offset if distance <= middle else sign_of * far_bucket
    return min(max(bucket + buckets, 0), 2 * buckets - 1)


def offset_selector():
    selector = np.zeros((4 * MAXLEN, 2 * BUCKETS), dtype=np.float32)
    for offset in range(1 - MAXLEN, MAXLEN):
        selector[offset + 2 * MAXLEN - 1, bucket_of(offset, BUCKETS, MAXLEN)] = 1.0
    return selector


def nesterov(weight, moment, average, gradient, step_rate):
    decayed = gradient + DECAY * weight
    moment_new = MOMENTUM * moment + decayed
    weight_new = weight - step_rate * (decayed + MOMENTUM * moment_new)
    average_new = AVERAGE * average + (1.0 - AVERAGE) * weight_new
    return (weight_new, moment_new, average_new)


def column_sums(matrix):
    return jnp.sum(matrix, axis=0, dtype=FULL)


def per_device(
    inputs,
    seg_lengths,
    cotangent,
    qkv_weight,
    qkv_moment,
    qkv_average,
    out_weight,
    out_moment,
    out_average,
    up_weight,
    up_moment,
    up_average,
    down_weight,
    down_moment,
    down_average,
    rel_table,
    table_moment,
    table_average,
    vectors,
    vector_moment,
    vector_average,
):
    tok_rows = inputs.shape[0]
    head_count = lax.axis_size("head")
    dp_count = lax.axis_size("dp")
    head_rank = lax.axis_index("head")
    dp_rank = lax.axis_index("dp")
    local_heads = HEADS // head_count
    local_width = local_heads * HD
    quarter = tok_rows // head_count
    total_tokens = tok_rows * dp_count
    up_local = up_weight.shape[1]
    dp_steps, head_steps = index_steps("dp"), index_steps("head")
    device_count = dp_count * head_count

    width_order = one_hot(block_owner(dp_rank, dp_steps, "dp"), D // dp_count)
    inputs_across = dot(width_order, inputs, NT).astype(HALF)
    qkv_span = 3 * local_width
    qkv_lanes = -(-qkv_span // 128) * 128
    w_qkv_own = jnp.pad(
        jnp.concatenate([qkv_weight[i].astype(HALF) for i in range(3)], axis=1),
        ((0, 0), (0, qkv_lanes - qkv_span)),
    )
    unit_own, inverse_own = standardise(rel_table)
    vec_rows = vectors.shape[0]
    table_part = rel_table.shape[0]
    vec_high = vectors.astype(HALF)
    vec_low = (vectors - vec_high.astype(FULL)).astype(HALF)
    vec_lanes = -(-2 * vec_rows // table_part // 128) * 128
    vec_pack = jnp.pad(
        jnp.concatenate([vec_high, vec_low]), (0, table_part * vec_lanes - 2 * vec_rows)
    ).reshape(table_part, vec_lanes)
    small = jnp.concatenate([unit_own.astype(HALF), vec_pack], axis=1)
    small_steps = dp_steps + head_steps
    small = gather_rows(small, small_steps)
    both_first = gather_rows(w_qkv_own, dp_steps[:1])
    inputs_own, cotangent_own = (
        lax.dynamic_slice_in_dim(values, head_rank * quarter, quarter, 0)
        for values in (inputs, cotangent)
    )
    both_first = after(both_first, inputs_across, inputs_own, cotangent_own)
    w_qkv_turned = gather_rows(both_first, dp_steps[1:])[:, :qkv_span]
    owner = block_owner(dp_rank, small_steps, "dp") * head_count + block_owner(
        head_rank, small_steps, "head"
    )
    unit_table = small[:, :D]
    vec_used = -(-2 * vec_rows // vec_lanes)
    vec_all = (
        small[:, D:]
        .reshape(device_count, table_part, vec_lanes)[:, :vec_used]
        .reshape(device_count, vec_used * vec_lanes)
    )
    vec_all = dot(one_hot(owner, 1), vec_all, TN)
    vector_full = (vec_all[:, :vec_rows] + vec_all[:, vec_rows : 2 * vec_rows]).reshape(-1)
    vector_rows = vector_full[: 11 * D].reshape(11, D)

    far, core, low, mid = head_steps[0], head_steps[1], dp_steps[-1], dp_steps[-2]
    half = D // 2
    wide_lanes = -(-(up_local + local_width) // 256) * 256
    up_out_own = jnp.pad(
        jnp.concatenate([up_weight, out_weight.T], axis=1).astype(HALF),
        ((0, 0), (0, wide_lanes - up_local - local_width)),
    )
    up_near = gather_rows(up_out_own, dp_steps[:-1])
    up_blocks = [up_near, swap(up_near, low), swap(up_near, far), swap_both(up_near, low, far)]
    up_near_core = swap(up_near, core)
    down_one = gather_rows(after(down_weight.T.astype(HALF), both_first), dp_steps[:-2])
    down_near = jnp.stack(
        [down_one, swap(down_one, low), swap(down_one, far), swap_both(down_one, low, far)]
    )
    down_far = swap(down_near, mid)
    down_near_core = swap(down_near, core)
    differences = list(range(head_count))

    table_order = one_hot(owner, table_part)
    w_qkv = dot(width_order, w_qkv_turned, TN).astype(HALF)

    def head_part(row_values):
        return lax.dynamic_slice_in_dim(row_values, head_rank * local_width, local_width)

    bias_qkv = jnp.concatenate([head_part(vector_rows[8 + i]) for i in range(3)])
    normed = (unit_table.astype(FULL) * vector_rows[4] + vector_rows[5]).astype(HALF)
    normed_across = dot(width_order, normed, NT).astype(HALF)
    tables = (dot(normed, w_qkv[:, : 2 * local_width]) + bias_qkv[: 2 * local_width]).astype(HALF)
    tables = dot(table_order, tables, TN).astype(HALF)
    selector = offset_selector()[::-1]
    by_offset = dot(jnp.asarray(selector, dtype=HALF), tables).astype(HALF)
    qkv = (dot(inputs, w_qkv) + bias_qkv).astype(HALF)
    info = jnp.concatenate([seg_lengths[0], head_rank[None].astype(jnp.int32)])
    context, probs = attention_forward(info, qkv, by_offset, head_count, (up_near, down_near))
    context, up_near_core, down_near_core = lax.optimization_barrier(
        (context, up_near_core, down_near_core)
    )
    *up_rest, down_far, _ = lax.optimization_barrier((*up_blocks[1:], down_far, context))
    up_blocks = [up_near] + up_rest + [up_near_core] + [swap(block, core) for block in up_rest]
    down_blocks = [down_near, down_far, down_near_core, swap(down_far, core)]

    def exchange(blocks):
        return {
            o: swap(block, ("head", o)) if o else block for o, block in blocks.items()
        }

    context_low = exchange({o: context[o * quarter : (o + 1) * quarter] for o in differences})

    vec = jnp.concatenate([vector_rows[:4], vector_rows[6:8], vector_rows[:2]], axis=0)
    bias_up = vector_full[11 * D :].reshape(head_count, up_local)
    output, grad_pre_first, norm_sums, grad_bias_up, grad_context, *weight_grads = middle(
        info,
        inputs_own,
        cotangent_own,
        width_order,
        vec,
        bias_up,
        [context_low[o] for o in differences],
        up_blocks,
        down_blocks,
        (normed_across, table_order),
    )

    def fold(blocks, step):
        bit = step[1]
        return {
            o: (block.astype(FULL) + swap(blocks[o ^ bit], step).astype(FULL)).astype(HALF)
            for o, block in blocks.items()
            if not o & bit
        }

    up_keep, up_send, down_keep, down_send = weight_grads
    grad_context = exchange(dict(zip(differences, grad_context)))
    grad_context = jnp.concatenate([grad_context[o] for o in differences], axis=0)
    up_got, down_got, _ = lax.optimization_barrier(
        (swap(up_send, core), swap(down_send, core), grad_context)
    )
    lower, upper = slice(0, half), slice(half, D)
    up_stays, up_low, up_far, up_both = (
        (up_keep[i, rows], up_got[i, rows])
        for i, rows in ((0, lower), (0, upper), (1, lower), (1, upper))
    )
    up_low, up_far, up_both = add(*up_low), add(*up_far), add(*up_both)
    down_keep, down_got = (
        values.reshape(2, 2, 2, D // 4, up_local) for values in (down_keep, down_got)
    )
    down_leaves = add(down_keep[:, :, 1], down_got[:, :, 1])
    grad_qkv_low, grad_offsets = attention_backward(
        info,
        qkv,
        by_offset,
        probs,
        grad_context,
        head_count,
        (up_low, up_far, up_both, down_leaves),
    )
    *up_got, down_got_mid, _ = lax.optimization_barrier(
        (
            swap(up_low, low),
            swap(up_far, far),
            swap_both(up_both, low, far),
            swap(down_leaves, mid),
            grad_qkv_low,
        )
    )
    up_next = add(*up_stays, *up_got)
    down_stays, down_low, down_far, down_both = (
        add(down_keep[i, j, 0], down_got[i, j, 0], down_got_mid[i, j])
        for i, j in ((0, 0), (0, 1), (1, 0), (1, 1))
    )
    grad_qkv, input_parts, grad_normed, grad_vector = tail(
        info,
        grad_qkv_low,
        grad_offsets,
        w_qkv,
        inputs_across,
        normed_across,
        unit_table,
        jnp.asarray(selector.T, dtype=HALF),
        table_order,
        norm_sums,
        grad_bias_up,
        head_count,
        qkv_lanes,
        (up_next, down_low, down_far, down_both),
    )
    up_out_shard = scatter_rows(up_next, dp_steps[:-1][::-1])
    up_shard = up_out_shard[:, :up_local]
    out_shard = up_out_shard[:, up_local : up_local + local_width].T
    down_next = add(
        down_stays, swap(down_low, low), swap(down_far, far), swap_both(down_both, low, far)
    )
    down_shard = scatter_rows(down_next, dp_steps[:-2][::-1]).T
    qkv_shard = scatter_rows(grad_qkv, dp_steps[::-1])
    input_both = scatter_rows(input_parts, head_steps[-1:]).astype(HALF)
    input_grad = grad_pre_first + scatter_rows(input_both, head_steps[:-1][::-1])[0]

    vec_lanes = -(-vec_rows // 128) * 128
    grad_vector = jnp.pad(
        grad_vector.reshape(-1)[: device_count * vec_rows].reshape(device_count, vec_rows),
        ((0, 0), (0, vec_lanes - vec_rows)),
    )
    grad_vector = dot(one_hot(owner, 1), grad_vector.astype(HALF)).astype(HALF)
    spare = -(-vec_lanes // table_part // 128) * 128 * table_part
    grad_vector = jnp.pad(grad_vector, ((0, 0), (0, spare - vec_lanes)))
    grad_vector = grad_vector.reshape(device_count * table_part, -1)
    small_shard = scatter_rows(
        jnp.concatenate([grad_normed, grad_vector], axis=1), small_steps[::-1]
    )
    table_shard = standardise_back(small_shard[:, :D] * vector_rows[4], unit_own, inverse_own)
    vector_shard = small_shard[:, D:].reshape(-1)[:vec_rows]

    qkv_grad_shard = jnp.stack(
        [qkv_shard[:, i * local_width : (i + 1) * local_width] for i in range(3)]
    )
    new_qkv = nesterov(
        qkv_weight, qkv_moment, qkv_average, qkv_grad_shard, 0.75 / math.sqrt(D * total_tokens)
    )
    new_out = nesterov(
        out_weight,
        out_moment,
        out_average,
        out_shard,
        0.125 * MAXLEN / math.sqrt(D * total_tokens),
    )
    new_up = nesterov(up_weight, up_moment, up_average, up_shard, 1.1 / math.sqrt(D * total_tokens))
    new_down = nesterov(
        down_weight, down_moment, down_average, down_shard, 1.0 / math.sqrt(FF * total_tokens)
    )
    new_table = nesterov(
        rel_table,
        table_moment,
        table_average,
        table_shard,
        0.55 * math.sqrt(MAXLEN / total_tokens),
    )
    new_vector = nesterov(
        vectors, vector_moment, vector_average, vector_shard, 0.3 / math.sqrt(total_tokens)
    )
    return (output, input_grad) + new_qkv + new_out + new_up + new_down + new_table + new_vector


def solution(mesh):
    rows = P("dp", None)
    owned = P(("dp", "head"), None)
    qkv = P(None, "dp", "head")
    out = P("head", "dp")
    up = P("dp", "head")
    vector = P(("dp", "head"))
    return jax.shard_map(
        per_device,
        mesh=mesh,
        in_specs=(rows,) * 3 + (qkv,) * 3 + (out,) * 3 + (up,) * 3 + (out,) * 3 + (owned,) * 3 + (vector,) * 3,
        out_specs=(owned,) * 2 + (qkv,) * 3 + (out,) * 3 + (up,) * 3 + (out,) * 3 + (owned,) * 3 + (vector,) * 3,
        check_vma=False,
    )
```

```python
import functools
import math

import jax
import jax.numpy as jnp
import numpy as np
from jax import lax
from jax.experimental import pallas as pl
from jax.experimental.pallas import tpu as pltpu
from jax.sharding import PartitionSpec as P

D = 768
HEADS = 12
HD = 64
FF = 3072
BUCKETS = 256
MAXLEN = 512

EPSILON = 1e-07
MOMENTUM = 0.9
DECAY = 0.01
AVERAGE = 0.7
MASKED = -1e30

TILE = 128
NARROW = 5
SCALE = (3.0 * HD) ** -0.5
LOG2E = math.log2(math.e)
HALF = jnp.bfloat16
FULL = jnp.float32
NN = (((1,), (0,)), ((), ()))
NT = (((1,), (1,)), ((), ()))
TN = (((0,), (0,)), ((), ()))


def dot(left, right, dims=NN):
    return lax.dot_general(left, right, dims, preferred_element_type=FULL)


def shear(values, count, low):
    rolled = [
        pltpu.roll(values[:, m * TILE : (m + 1) * TILE], 0, 1, stride=1, stride_axis=0)
        for m in range(count + 1)
    ]
    return jnp.concatenate(
        [jnp.where(low, rolled[m], rolled[m + 1]) for m in range(count)], axis=1
    )


def unshear(values, count, after, shift):
    rolled = [
        pltpu.roll(values[:, m * TILE : (m + 1) * TILE], shift, 1, stride=1, stride_axis=0)
        for m in range(count)
    ]
    zero = jnp.zeros((TILE, TILE), values.dtype)
    return jnp.concatenate(
        [
            jnp.where(
                after, rolled[m] if m < count else zero, rolled[m - 1] if m > 0 else zero
            ).astype(HALF)
            for m in range(count + 1)
        ],
        axis=1,
    )


def flip_matrix():
    across = lax.broadcasted_iota(jnp.int32, (TILE, TILE), 1)
    down = lax.broadcasted_iota(jnp.int32, (TILE, TILE), 0)
    return (across + down == TILE - 1).astype(FULL).astype(HALF)


def tiles_of(block, count=1):
    return pl.ds(pl.multiple_of(block * TILE, TILE), count * TILE)


def sequence_bounds(ends, first, last):
    start, stop = jnp.int32(0), jnp.int32(0)
    begin = jnp.int32(0)
    for end in ends:
        start = jnp.where((begin <= first) & (first < end), begin, start)
        stop = jnp.where((begin <= last) & (last < end), end, stop)
        begin = end
    return start, stop


def by_window(ends, block, tiles, body):
    start, stop = sequence_bounds(ends, block * TILE, block * TILE + TILE - 1)
    first = start // TILE
    narrow = min(NARROW, tiles)
    fits = (stop + TILE - 1) // TILE - first <= narrow

    @pl.when(fits)
    def _():
        body(narrow, jnp.minimum(first, tiles - narrow))

    @pl.when(jnp.logical_not(fits))
    def _():
        body(tiles, jnp.int32(0))


def sequence_ends(info, count):
    ends, total = [], jnp.int32(0)
    for s in range(count):
        total = total + info[s]
        ends.append(total)
    return ends


def sequence_of(places, ends):
    return sum((places >= end).astype(jnp.int32) for end in ends[:-1])


def turned(block, rank, per_owner):
    return ((block // per_owner) ^ rank) * per_owner + block % per_owner


def probs_copy(source, target, sems, block):
    rows = tiles_of(block)
    return pltpu.make_async_copy(source.at[:, rows], target.at[:, rows], sems.at[block])


def forward_kernel(info, qkv_ref, tab_ref, *refs, owners):
    ctx_ref, p_far, q_ref, k_ref, v_ref, qb_ref, kb_ref, p2c_ref, p_ref, sems = refs[-10:]
    heads, tiles = q_ref.shape[0], q_ref.shape[1] // TILE
    segments = info.shape[0] - 1
    rank, per_owner = info[segments], tiles // owners
    ends = sequence_ends(info, segments)
    across = lax.broadcasted_iota(jnp.int32, (TILE, TILE), 1)
    down = lax.broadcasted_iota(jnp.int32, (TILE, TILE), 0)
    low = across < down
    flip = flip_matrix()
    for h in range(heads):
        for i, ref in enumerate((q_ref, k_ref, v_ref)):
            ref[h] = qkv_ref[:, (i * heads + h) * HD : (i * heads + h + 1) * HD]
        for i, ref in enumerate((qb_ref, kb_ref)):
            ref[h] = tab_ref[:, (i * heads + h) * HD : (i * heads + h + 1) * HD]

    def p2c_block(block, carried):
        rows = tiles_of(block)

        def body(count, first):
            offsets = tiles_of(first - block + tiles - 1, count + 1)
            for h in range(heads):
                sheared = shear(dot(k_ref[h, rows, :], qb_ref[h, offsets, :], NT), count, low)
                for m in range(count):
                    p2c_ref[h, tiles_of(first + m), rows] = sheared[
                        :, m * TILE : (m + 1) * TILE
                    ].T

        by_window(ends, block, tiles, body)
        return carried

    lax.fori_loop(0, tiles, p2c_block, 0)

    def score_block(block, carried):
        rows = tiles_of(block)
        row_sequence = sequence_of(down + block * TILE, ends)

        def body(count, first):
            cols = tiles_of(first, count)
            offsets = tiles_of(first - block + tiles - 1, count + 1)
            same = [
                row_sequence == sequence_of(across + (first + m) * TILE, ends) for m in range(count)
            ]
            same = jnp.concatenate(same, axis=1)
            contexts = []
            for h in range(heads):
                query = q_ref[h, rows, :]
                c2p = shear(dot(query, kb_ref[h, offsets, :], NT), count, low)
                raw = dot(query, k_ref[h, cols, :], NT) + c2p + p2c_ref[h, rows, cols]
                scores = jnp.where(same, (SCALE * LOG2E) * raw, MASKED)
                powers = jnp.exp2(scores - jnp.max(scores, axis=1, keepdims=True))
                probs = (powers * (1.0 / jnp.sum(powers, axis=1, keepdims=True))).astype(HALF)
                for m in range(count):
                    p_ref[h, rows, tiles_of(tiles - 1 - first - m)] = dot(
                        probs[:, m * TILE : (m + 1) * TILE], flip
                    ).astype(HALF)
                contexts.append(dot(probs, v_ref[h, cols, :]).astype(HALF))
            ctx_ref[tiles_of(turned(block, rank, per_owner)), :] = jnp.concatenate(contexts, axis=1)

        by_window(ends, block, tiles, body)
        probs_copy(p_ref, p_far, sems, block).start()
        return carried

    lax.fori_loop(0, tiles, score_block, 0)

    def finish(block, carried):
        probs_copy(p_ref, p_far, sems, block).wait()
        return carried

    lax.fori_loop(0, tiles, finish, 0)


def backward_kernel(
    info,
    qkv_ref,
    tab_ref,
    p_far,
    g_ref,
    *refs,
    owners,
):
    dqkv_ref, gtab_ref, q_ref, k_ref, krev_ref, vrev_ref, qbs_ref, kbs_ref = refs[-14:-6]
    grad_ref, dst_ref, dvt_ref, gsum_ref, p_ref, sems = refs[-6:]
    heads, tiles = q_ref.shape[0], q_ref.shape[1] // TILE
    width = heads * HD
    segments = info.shape[0] - 1
    rank, per_owner = info[segments], tiles // owners
    ends = sequence_ends(info, segments)
    across = lax.broadcasted_iota(jnp.int32, (TILE, TILE), 1)
    down = lax.broadcasted_iota(jnp.int32, (TILE, TILE), 0)
    flip = flip_matrix()

    def begin(block, carried):
        probs_copy(p_far, p_ref, sems, block).start()
        return carried

    lax.fori_loop(0, tiles, begin, 0)
    dst_ref[...] = jnp.zeros_like(dst_ref)
    dvt_ref[...] = jnp.zeros_like(dvt_ref)
    gsum_ref[...] = jnp.zeros_like(gsum_ref)
    for h in range(heads):
        q_ref[h] = qkv_ref[:, h * HD : (h + 1) * HD]
        k_ref[h] = qkv_ref[:, width + h * HD : width + (h + 1) * HD]
        qbs_ref[h] = tab_ref[:, h * HD : (h + 1) * HD]
        grad_ref[h] = g_ref[:, h * HD : (h + 1) * HD]
    for m in range(tiles):
        here, there = slice(m * TILE, (m + 1) * TILE), slice((tiles - 1 - m) * TILE, (tiles - m) * TILE)
        turned_rows = dot(flip, qkv_ref[here, width:]).astype(HALF)
        for h in range(heads):
            krev_ref[h, there, :] = turned_rows[:, h * HD : (h + 1) * HD]
            vrev_ref[h, there, :] = turned_rows[:, width + h * HD : width + (h + 1) * HD]
    for m in range(2 * tiles):
        here = slice(m * TILE, (m + 1) * TILE)
        there = slice((2 * tiles - 1 - m) * TILE, (2 * tiles - m) * TILE)
        turned_rows = dot(flip, tab_ref[here, width:]).astype(HALF)
        for h in range(heads):
            kbs_ref[h, there, :] = turned_rows[:, h * HD : (h + 1) * HD]

    def query_block(block, carried):
        rows = tiles_of(block)
        probs_copy(p_far, p_ref, sems, block).wait()

        def body(count, first):
            start = tiles - first - count
            cols = tiles_of(start, count)
            offsets = tiles_of(block + start, count + 1)
            grads = []
            for h in range(heads):
                grad = grad_ref[h, tiles_of(turned(block, rank, per_owner)), :]
                probs_low = p_ref[h, rows, cols]
                probs = probs_low.astype(FULL)
                grad_probs = dot(grad, vrev_ref[h, cols, :], NT)
                inner = jnp.sum(probs * grad_probs, axis=1, keepdims=True)
                grad_raw = (probs * (grad_probs - inner)) * SCALE
                by_offset = unshear(grad_raw, count, across >= down, 0)
                grads.append(
                    (
                        dot(grad_raw.astype(HALF), krev_ref[h, cols, :])
                        + dot(by_offset, kbs_ref[h, offsets, :])
                    ).astype(HALF)
                )
                gsum_ref[heads + h, :, offsets] += dot(
                    q_ref[h, rows, :].astype(FULL).T.astype(HALF), by_offset
                )
                dvt_ref[h, :, cols] += dot(grad.astype(FULL).T.astype(HALF), probs_low)
                for m in range(count):
                    dst_ref[h, tiles_of(start + m), rows] = grad_raw[
                        :, m * TILE : (m + 1) * TILE
                    ].T
            dqkv_ref[rows, :width] = jnp.concatenate(grads, axis=1)

        by_window(ends, block, tiles, body)
        return carried

    lax.fori_loop(0, tiles, query_block, 0)

    def key_block(block, carried):
        rows, back = tiles_of(block), tiles_of(tiles - 1 - block)

        def body(count, first):
            cols = tiles_of(first, count)
            offsets = tiles_of(tiles - 1 - block + first, count + 1)
            grads = []
            for h in range(heads):
                grad_raw = dst_ref[h, back, cols]
                by_offset = unshear(grad_raw, count, across > down, 1)
                grads.append(
                    (
                        dot(grad_raw.astype(HALF), q_ref[h, cols, :])
                        + dot(by_offset, qbs_ref[h, offsets, :])
                    ).astype(HALF)
                )
                gsum_ref[h, :, offsets] += dot(
                    krev_ref[h, back, :].astype(FULL).T.astype(HALF), by_offset
                )
            grads += [dvt_ref[h, :, back].T.astype(HALF) for h in range(heads)]
            dqkv_ref[rows, width:] = dot(flip, jnp.concatenate(grads, axis=1)).astype(HALF)

        by_window(ends, block, tiles, body)
        return carried

    lax.fori_loop(0, tiles, key_block, 0)
    for i in range(heads):
        gtab_ref[i * HD : (i + 1) * HD, :] = gsum_ref[i].astype(HALF)
        for m in range(2 * tiles):
            there = slice((2 * tiles - 1 - m) * TILE, (2 * tiles - m) * TILE)
            gtab_ref[width + i * HD : width + (i + 1) * HD, there] = dot(
                gsum_ref[heads + i, :, m * TILE : (m + 1) * TILE].astype(HALF), flip
            ).astype(HALF)


SMEM_SPEC = pl.BlockSpec(memory_space=pltpu.SMEM)
VMEM_SPEC = pl.BlockSpec(memory_space=pltpu.VMEM)
ANY_SPEC = pl.BlockSpec(memory_space=pl.ANY)


def kernel_cost(microseconds):
    return pl.CostEstimate(
        flops=int(microseconds * 1e9), bytes_accessed=int(microseconds * 1e6), transcendentals=0
    )


def attention_forward(info, qkv, tables, owners, before):
    rows, heads = qkv.shape[0], qkv.shape[1] // (3 * HD)
    small, wide = pltpu.VMEM((heads, rows, HD), HALF), pltpu.VMEM((heads, 2 * rows, HD), HALF)
    return pl.pallas_call(
        functools.partial(forward_kernel, owners=owners),
        out_shape=(
            jax.ShapeDtypeStruct((rows, heads * HD), HALF),
            jax.ShapeDtypeStruct((heads, rows, rows), HALF),
        ),
        in_specs=[SMEM_SPEC] + [VMEM_SPEC] * 2 + [ANY_SPEC] * len(before),
        out_specs=(VMEM_SPEC, ANY_SPEC),
        scratch_shapes=[small] * 3
        + [wide] * 2
        + [
            pltpu.VMEM((heads, rows, rows), FULL),
            pltpu.VMEM((heads, rows, rows), HALF),
            pltpu.SemaphoreType.DMA((rows // TILE,)),
        ],
        compiler_params=pltpu.CompilerParams(vmem_limit_bytes=48 * 2**20),
        cost_estimate=kernel_cost(30),
    )(info, qkv, tables, *before)


def attention_backward(info, qkv, tables, probs, grad, owners, before):
    rows, heads = qkv.shape[0], qkv.shape[1] // (3 * HD)
    shape = jax.ShapeDtypeStruct
    small, wide = pltpu.VMEM((heads, rows, HD), HALF), pltpu.VMEM((heads, 2 * rows, HD), HALF)
    return pl.pallas_call(
        functools.partial(backward_kernel, owners=owners),
        out_shape=(shape(qkv.shape, HALF), shape((2 * heads * HD, 2 * rows), HALF)),
        in_specs=[SMEM_SPEC] + [VMEM_SPEC] * 2
        + [ANY_SPEC, VMEM_SPEC]
        + [ANY_SPEC] * len(before),
        out_specs=(VMEM_SPEC,) * 2,
        scratch_shapes=[small] * 4
        + [wide] * 2
        + [
            small,
            pltpu.VMEM((heads, rows, rows), FULL),
            pltpu.VMEM((heads, HD, rows), FULL),
            pltpu.VMEM((2 * heads, HD, 2 * rows), FULL),
            pltpu.VMEM((heads, rows, rows), HALF),
            pltpu.SemaphoreType.DMA((rows // TILE,)),
        ],
        compiler_params=pltpu.CompilerParams(vmem_limit_bytes=52 * 2**20),
        cost_estimate=kernel_cost(34),
    )(info, qkv, tables, probs, grad, *before)


def standardise(values):
    center = values - jnp.mean(values, axis=-1, keepdims=True)
    spread = jnp.mean(center * center, axis=-1, keepdims=True)
    inverse = lax.rsqrt(spread + EPSILON)
    return center * inverse, inverse


def standardise_back(grad, unit, inverse):
    return inverse * (
        grad
        - jnp.mean(grad, axis=-1, keepdims=True)
        - unit * jnp.mean(grad * unit, axis=-1, keepdims=True)
    )


def exact_dot(values, order, dims):
    high = values.astype(HALF)
    rest = values - high.astype(FULL)
    middle = rest.astype(HALF)
    last = (rest - middle.astype(FULL)).astype(HALF)
    return dot(high, order, dims) + dot(middle, order, dims) + dot(last, order, dims)


def turn(values):
    return values.astype(FULL).T.astype(HALF)


def middle_kernel(info, x_ref, cot_ref, order_ref, vec_ref, bias_ref, *refs):
    heads = bias_ref.shape[0]
    ctx, up_far, down_far = refs[:heads], refs[heads : heads + 8], refs[heads + 8 : heads + 12]
    half, chunk = up_far[0].shape[0], down_far[0].shape[1]
    refs = refs[len(refs) - heads - 16 :]
    out_ref, pre_ref, sums_ref, grad_bias_ref = refs[:4]
    grad_ctx = refs[4 : heads + 4]
    up_keep, up_send, down_keep, down_send = refs[heads + 4 : heads + 8]
    slope_ref, hidden_ref, up, down, grad_up, grad_down, sems_in, sems_out = refs[heads + 8 :]
    wide = bias_ref.shape[1]
    arrivals = [
        [
            pltpu.make_async_copy(
                up_far[4 * (o % 2) + 2 * (o // 2) + i].at[:, lanes],
                up.at[o, i * half : (i + 1) * half, lanes],
                sems_in.at[2 * j + i, o],
            )
            for o in range(heads)
        ]
        for j, lanes in enumerate((slice(wide, up.shape[2]), slice(0, wide)))
        for i in range(2)
    ]
    arrivals += [
        [
            pltpu.make_async_copy(
                down_far[2 * (o % 2) + i % 2].at[2 * (o // 2) + i // 2],
                down.at[o, i * chunk : (i + 1) * chunk],
                sems_in.at[4 + i, o],
            )
            for o in range(heads)
        ]
        for i in range(4)
    ]
    for copies in arrivals[:2]:
        for copy in copies:
            copy.start()
    for o in range(heads):
        for copies in arrivals[2:]:
            copies[o].start()
    departures = []

    def depart(i, o):
        near, keep, send = ((grad_up, up_keep, up_send), (grad_down, down_keep, down_send))[i > 1]
        lanes = (slice(0, wide), slice(wide, grad_up.shape[2]), slice(0, wide))[i]
        copy = pltpu.make_async_copy(
            near.at[o, :, lanes],
            (send if o % 2 else keep).at[o // 2, :, lanes],
            sems_out.at[i, o],
        )
        copy.start()
        departures.append(copy)

    rank = info[info.shape[0] - 1]
    wide = bias_ref.shape[1]
    span = ctx[0].shape[1]
    order = order_ref[...]
    vec = exact_dot(vec_ref[...], order, NT)
    gain1, bias1, gain2, bias2, bias_out, bias_down = (vec[i : i + 1] for i in range(6))

    pre_first = dot(x_ref[...], order, NT) + bias_out
    for o in range(heads):
        arrivals[0][o].wait()
        arrivals[1][o].wait()
        pre_first = pre_first + dot(ctx[o][...], up[o, :, wide : wide + span], NT)
    unit_first, inverse_first = standardise(pre_first)
    first = unit_first * gain1 + bias1
    first_low = first.astype(HALF)
    total = first + bias_down
    for o in range(heads):
        arrivals[2][o].wait()
        arrivals[3][o].wait()
        values = dot(first_low, up[o, :, :wide]) + bias_ref[pl.ds(rank ^ o, 1), :]
        below = 0.5 + 0.5 * lax.erf(values * math.sqrt(0.5))
        hidden = (values * below).astype(HALF)
        hidden_ref[o] = hidden
        slope_ref[o] = below + values * (
            jnp.exp2(values * values * (-0.5 * LOG2E)) * (1.0 / math.sqrt(2.0 * math.pi))
        )
        for copies in arrivals[4:]:
            copies[o].wait()
        total = total + dot(hidden, down[o], NT)
    unit_second, inverse_second = standardise(total)
    out_ref[...] = dot((unit_second * gain2 + bias2).astype(HALF), order).astype(HALF)

    grad_out = dot(cot_ref[...], order, NT)
    grad_second = standardise_back(grad_out * gain2, unit_second, inverse_second)
    grad_down_low = grad_second.astype(HALF)
    grad_down_turned, first_turned = turn(grad_down_low), turn(first_low)
    grad_first = grad_second
    for o in range(heads):
        grad_down[o] = dot(grad_down_turned, hidden_ref[o]).astype(HALF)
        depart(2, o)
        grad_values = (slope_ref[o] * dot(grad_down_low, down[o])).astype(HALF)
        grad_bias_ref[pl.ds(rank ^ o, 1), :] = jnp.sum(
            grad_values.astype(FULL), axis=0, keepdims=True
        )
        grad_up[o, :, :wide] = dot(first_turned, grad_values).astype(HALF)
        depart(0, o)
        grad_first = grad_first + dot(grad_values, up[o, :, :wide], NT)
    grad_pre = standardise_back(grad_first * gain1, unit_first, inverse_first)
    grad_low = grad_pre.astype(HALF)
    grad_turned = turn(grad_low)
    for o in range(heads):
        grad_ctx[o][...] = dot(grad_low, up[o, :, wide : wide + span]).astype(HALF)
        grad_up[o, :, wide : wide + span] = dot(grad_turned, ctx[o][...]).astype(HALF)
        if wide + span < up.shape[2]:
            grad_up[o, :, wide + span :] = jnp.zeros((up.shape[1], up.shape[2] - wide - span), HALF)
        depart(1, o)
    pre_ref[...] = exact_dot(grad_pre, order, NN)
    sums = [
        jnp.sum(part, axis=0, keepdims=True)
        for part in (
            grad_first * unit_first,
            grad_first,
            grad_out * unit_second,
            grad_out,
            grad_pre,
            grad_second,
        )
    ]
    sums_ref[...] = exact_dot(jnp.concatenate(sums + [jnp.zeros_like(sums[0])] * 2, axis=0), order, NN)
    for copy in departures:
        copy.wait()


def middle(info, x, cot, order, vec, bias, ctx, up, down, before):
    heads, (rows, width), wide = len(ctx), x.shape, bias.shape[1]
    up_shape, down_shape = (width, up[0].shape[1]), (width, wide)
    shape = jax.ShapeDtypeStruct
    results = pl.pallas_call(
        middle_kernel,
        out_shape=(
            shape((rows, width), HALF),
            shape((rows, width), FULL),
            shape(vec.shape, FULL),
            shape(bias.shape, FULL),
        )
        + tuple(shape(c.shape, HALF) for c in ctx)
        + tuple(shape((heads // 2,) + w, HALF) for w in (up_shape, up_shape, down_shape, down_shape)),
        in_specs=[SMEM_SPEC] + [VMEM_SPEC] * (5 + heads) + [ANY_SPEC] * (12 + len(before)),
        out_specs=(VMEM_SPEC,) * (4 + heads) + (ANY_SPEC,) * 4,
        scratch_shapes=[pltpu.VMEM((heads, rows, wide), FULL), pltpu.VMEM((heads, rows, wide), HALF)]
        + [pltpu.VMEM((heads,) + w, HALF) for w in (up_shape, down_shape, up_shape, down_shape)]
        + [pltpu.SemaphoreType.DMA((8, heads))] * 2,
        compiler_params=pltpu.CompilerParams(vmem_limit_bytes=48 * 2**20),
        cost_estimate=kernel_cost(20),
    )(info, x, cot, order, vec, bias, *ctx, *up, *down, *before)
    return results[:4] + (results[4 : 4 + heads],) + results[4 + heads :]


def by_row(parts, count):
    row = lax.broadcasted_iota(jnp.int32, (count, parts[0].shape[1]), 0)
    total = jnp.zeros(row.shape, FULL)
    for i, part in enumerate(parts):
        total = jnp.where(row == i, part, total)
    return total


def tail_kernel(
    info,
    dqkv_ref,
    offsets_ref,
    w_ref,
    inputs_ref,
    normed_ref,
    unit_ref,
    selector_ref,
    order_ref,
    norm_sums_ref,
    bias_up_ref,
    *refs,
):
    qkv_keep, qkv_send, parts_ref, normed_grad_ref, vector_ref = refs[-5:]
    rank = info[info.shape[0] - 1]
    width = dqkv_ref.shape[1] // 3
    owners, quarter = parts_ref.shape[:2]
    tables = dot(selector_ref[...], offsets_ref[...], NT).astype(HALF)
    turned_tables = dot(order_ref[...], tables).astype(HALF)
    weights = w_ref[...]
    grad_normed = dot(turned_tables, weights[:, : 2 * width], NT)
    normed_grad_ref[...] = grad_normed.astype(HALF)
    grads = dqkv_ref[...]
    grad_qkv = dot(inputs_ref[...], grads)
    grad_qkv = jnp.concatenate(
        [
            grad_qkv[:, : 2 * width] + dot(normed_ref[...], turned_tables),
            grad_qkv[:, 2 * width :],
        ],
        axis=1,
    ).astype(HALF)
    half = qkv_keep.shape[0]
    for i, ref in enumerate((qkv_keep, qkv_send)):
        ref[:, : 3 * width] = grad_qkv[i * half : (i + 1) * half]
        if 3 * width < ref.shape[1]:
            ref[:, 3 * width :] = jnp.zeros((half, ref.shape[1] - 3 * width), HALF)
    for o in range(owners):
        apart = rank ^ o
        parts_ref[(apart % 2) * (owners // 2) + apart // 2] = dot(
            dqkv_ref[o * quarter : (o + 1) * quarter, :], weights, NT
        ).astype(HALF)
    sums = jnp.sum(grads.astype(FULL), axis=0, keepdims=True)
    table_sums = jnp.sum(turned_tables.astype(FULL), axis=0, keepdims=True)
    sums = jnp.concatenate([sums[:, : 2 * width] + table_sums, sums[:, 2 * width :]], axis=1)
    sums = by_row([sums[:, i * width : (i + 1) * width] for i in range(3)], 8)
    places = (
        lax.broadcasted_iota(jnp.int32, (width, D), 1)
        == lax.broadcasted_iota(jnp.int32, (width, D), 0) + rank * width
    ).astype(FULL).astype(HALF)
    placed = exact_dot(sums, places, NN)
    norm_sums, bias_up = norm_sums_ref[...], bias_up_ref[...]
    parts = [norm_sums[i : i + 1] for i in range(4)]
    parts.append(jnp.sum(grad_normed * unit_ref[...].astype(FULL), axis=0, keepdims=True))
    parts.append(jnp.sum(grad_normed, axis=0, keepdims=True))
    parts += [norm_sums[i : i + 1] for i in range(4, 6)]
    parts += [placed[i : i + 1] for i in range(3)]
    parts += [bias_up[i : i + 1] for i in range(bias_up.shape[0])]
    vector_ref[...] = by_row(parts, vector_ref.shape[0])


def tail(
    info, dqkv, offsets, weights, inputs, normed, unit, selector, order, norm_sums, bias_up,
    owners, lanes, before,
):
    rows, shape = dqkv.shape[0], jax.ShapeDtypeStruct
    return pl.pallas_call(
        tail_kernel,
        out_shape=(
            shape((D // 2, lanes), HALF),
            shape((D // 2, lanes), HALF),
            shape((owners, rows // owners, D), HALF),
            shape(normed.shape[::-1], HALF),
            shape((-(-(11 + bias_up.shape[0]) // 8) * 8, D), FULL),
        ),
        in_specs=[SMEM_SPEC] + [VMEM_SPEC] * 10 + [ANY_SPEC] * len(before),
        out_specs=(VMEM_SPEC,) * 5,
        compiler_params=pltpu.CompilerParams(vmem_limit_bytes=40 * 2**20),
        cost_estimate=kernel_cost(0.1),
    )(info, dqkv, offsets, weights, inputs, normed, unit, selector, order, norm_sums, bias_up, *before)


def index_steps(axis):
    size = lax.axis_size(axis)
    steps, bit = [], size // 2
    while bit >= 1:
        steps.append((axis, bit))
        bit //= 2
    return steps


def swap(values, step):
    axis, bit = step
    return lax.ppermute(values, axis, [(i, i ^ bit) for i in range(lax.axis_size(axis))])


def after(values, *others):
    return lax.optimization_barrier((values,) + others)[0]


def swap_both(values, one, other):
    (axis, bit), (along, place) = one, other
    width = lax.axis_size(along)
    count = lax.axis_size(axis) * width
    return lax.ppermute(
        values, (axis, along), [(i, i ^ (bit * width) ^ place) for i in range(count)]
    )


def gather_blocks(values, steps, layout):
    taken = []
    for step in steps:
        place = sum(1 for other in taken if layout.index(other) < layout.index(step))
        taken.append(step)
        other = swap(values, step)
        values = jnp.concatenate(
            [jnp.expand_dims(values, place), jnp.expand_dims(other, place)], axis=place
        )
    return values


def gather_rows(values, steps):
    for step in steps:
        values = jnp.concatenate([values, swap(values, step)], axis=0)
    return values


def scatter_rows(values, steps):
    kind = values.dtype
    for i, step in enumerate(steps):
        half = values.shape[0] // 2
        values = values[:half].astype(FULL) + swap(values[half:], step).astype(FULL)
        if i < len(steps) - 1:
            values = values.astype(kind)
    return values


def add(*parts):
    return sum(part.astype(FULL) for part in parts).astype(HALF)


def block_owner(rank, steps, axis):
    places = np.arange(2 ** len(steps))
    offsets = sum(
        ((places >> i) & 1) * bit for i, (along, bit) in enumerate(steps) if along == axis
    )
    return jnp.asarray(offsets, jnp.int32) ^ rank


def one_hot(owners, per_block):
    own = (owners[:, None] * per_block + jnp.arange(per_block, dtype=jnp.int32)[None, :]).reshape(-1)
    return (own[:, None] == jnp.arange(own.shape[0], dtype=jnp.int32)[None, :]).astype(HALF)


def bucket_of(offset, buckets, longest):
    middle = buckets // 2
    distance = middle - 1 if abs(offset) < middle else abs(offset)
    sign_of = 1 if offset > 0 else -1 if offset < 0 else 0
    far_bucket = (
        math.ceil(math.log(distance / middle) / math.log((longest - 1) / middle) * (middle - 1))
        + middle
    )
    bucket = offset if distance <= middle else sign_of * far_bucket
    return min(max(bucket + buckets, 0), 2 * buckets - 1)


def offset_selector():
    selector = np.zeros((4 * MAXLEN, 2 * BUCKETS), dtype=np.float32)
    for offset in range(1 - MAXLEN, MAXLEN):
        selector[offset + 2 * MAXLEN - 1, bucket_of(offset, BUCKETS, MAXLEN)] = 1.0
    return selector


def nesterov(weight, moment, average, gradient, step_rate):
    decayed = gradient + DECAY * weight
    moment_new = MOMENTUM * moment + decayed
    weight_new = weight - step_rate * (decayed + MOMENTUM * moment_new)
    average_new = AVERAGE * average + (1.0 - AVERAGE) * weight_new
    return (weight_new, moment_new, average_new)


def column_sums(matrix):
    return jnp.sum(matrix, axis=0, dtype=FULL)


def per_device(
    inputs,
    seg_lengths,
    cotangent,
    qkv_weight,
    qkv_moment,
    qkv_average,
    out_weight,
    out_moment,
    out_average,
    up_weight,
    up_moment,
    up_average,
    down_weight,
    down_moment,
    down_average,
    rel_table,
    table_moment,
    table_average,
    vectors,
    vector_moment,
    vector_average,
):
    tok_rows = inputs.shape[0]
    head_count = lax.axis_size("head")
    dp_count = lax.axis_size("dp")
    head_rank = lax.axis_index("head")
    dp_rank = lax.axis_index("dp")
    local_heads = HEADS // head_count
    local_width = local_heads * HD
    quarter = tok_rows // head_count
    total_tokens = tok_rows * dp_count
    up_local = up_weight.shape[1]
    dp_steps, head_steps = index_steps("dp"), index_steps("head")
    device_count = dp_count * head_count

    width_order = one_hot(block_owner(dp_rank, dp_steps, "dp"), D // dp_count)
    inputs_across = dot(width_order, inputs, NT).astype(HALF)
    qkv_span = 3 * local_width
    qkv_lanes = -(-qkv_span // 128) * 128
    w_qkv_own = jnp.pad(
        jnp.concatenate([qkv_weight[i].astype(HALF) for i in range(3)], axis=1),
        ((0, 0), (0, qkv_lanes - qkv_span)),
    )
    unit_own, inverse_own = standardise(rel_table)
    vec_rows = vectors.shape[0]
    table_part = rel_table.shape[0]
    vec_high = vectors.astype(HALF)
    vec_low = (vectors - vec_high.astype(FULL)).astype(HALF)
    vec_lanes = -(-2 * vec_rows // table_part // 128) * 128
    vec_pack = jnp.pad(
        jnp.concatenate([vec_high, vec_low]), (0, table_part * vec_lanes - 2 * vec_rows)
    ).reshape(table_part, vec_lanes)
    small = jnp.concatenate([unit_own.astype(HALF), vec_pack], axis=1)
    small_steps = dp_steps + head_steps
    both_first = gather_rows(w_qkv_own, dp_steps[:1])
    small = gather_rows(small, small_steps)
    inputs_own, cotangent_own = (
        lax.dynamic_slice_in_dim(values, head_rank * quarter, quarter, 0)
        for values in (inputs, cotangent)
    )
    both_first = after(both_first, inputs_across, inputs_own, cotangent_own)
    both_more = gather_rows(both_first, dp_steps[1:-1])
    both_last = swap(both_more, dp_steps[-1])
    w_qkv_turned = jnp.concatenate([both_more, both_last])[:, :qkv_span]
    owner = block_owner(dp_rank, small_steps, "dp") * head_count + block_owner(
        head_rank, small_steps, "head"
    )
    unit_table = small[:, :D]
    vec_used = -(-2 * vec_rows // vec_lanes)
    vec_all = (
        small[:, D:]
        .reshape(device_count, table_part, vec_lanes)[:, :vec_used]
        .reshape(device_count, vec_used * vec_lanes)
    )
    vec_all = dot(one_hot(owner, 1), vec_all, TN)
    vector_full = (vec_all[:, :vec_rows] + vec_all[:, vec_rows : 2 * vec_rows]).reshape(-1)
    vector_rows = vector_full[: 11 * D].reshape(11, D)

    far, core, low, mid = head_steps[0], head_steps[1], dp_steps[-1], dp_steps[-2]
    half = D // 2
    wide_lanes = -(-(up_local + local_width) // 256) * 256
    up_out_own = jnp.pad(
        jnp.concatenate([up_weight, out_weight.T], axis=1).astype(HALF),
        ((0, 0), (0, wide_lanes - up_local - local_width)),
    )
    up_near = gather_rows(up_out_own, dp_steps[:-1])
    up_blocks = [up_near, swap(up_near, low), swap(up_near, far), swap_both(up_near, low, far)]
    up_near_core = swap(up_near, core)
    down_one = gather_rows(after(down_weight.T.astype(HALF), both_first), dp_steps[:-2])
    down_near = jnp.stack(
        [down_one, swap(down_one, low), swap(down_one, far), swap_both(down_one, low, far)]
    )
    down_far = swap(down_near, mid)
    down_near_core = swap(down_near, core)
    differences = list(range(head_count))

    table_order = one_hot(owner, table_part)
    w_qkv = dot(width_order, w_qkv_turned, TN).astype(HALF)

    def head_part(row_values):
        return lax.dynamic_slice_in_dim(row_values, head_rank * local_width, local_width)

    bias_qkv = jnp.concatenate([head_part(vector_rows[8 + i]) for i in range(3)])
    normed = (unit_table.astype(FULL) * vector_rows[4] + vector_rows[5]).astype(HALF)
    normed_across = dot(width_order, normed, NT).astype(HALF)
    tables = (dot(normed, w_qkv[:, : 2 * local_width]) + bias_qkv[: 2 * local_width]).astype(HALF)
    tables = dot(table_order, tables, TN).astype(HALF)
    selector = offset_selector()[::-1]
    by_offset = dot(jnp.asarray(selector, dtype=HALF), tables).astype(HALF)
    qkv = (dot(inputs, w_qkv) + bias_qkv).astype(HALF)
    info = jnp.concatenate([seg_lengths[0], head_rank[None].astype(jnp.int32)])
    context, probs = attention_forward(info, qkv, by_offset, head_count, (up_near, down_near, unit_table))
    context, up_near_core, down_near_core = lax.optimization_barrier(
        (context, up_near_core, down_near_core)
    )
    def exchange(blocks):
        return {
            o: swap(block, ("head", o)) if o else block for o, block in blocks.items()
        }

    context_low = exchange({o: context[o * quarter : (o + 1) * quarter] for o in differences})
    *up_rest, down_far, _ = lax.optimization_barrier((*up_blocks[1:], down_far, tuple(context_low.values())))
    up_blocks = [up_near] + up_rest + [up_near_core] + [swap(block, core) for block in up_rest]
    down_blocks = [down_near, down_far, down_near_core, swap(down_far, core)]

    vec = jnp.concatenate([vector_rows[:4], vector_rows[6:8], vector_rows[:2]], axis=0)
    bias_up = vector_full[11 * D :].reshape(head_count, up_local)
    output, grad_pre_first, norm_sums, grad_bias_up, grad_context, *weight_grads = middle(
        info,
        inputs_own,
        cotangent_own,
        width_order,
        vec,
        bias_up,
        [context_low[o] for o in differences],
        up_blocks,
        down_blocks,
        (normed_across, table_order),
    )

    def fold(blocks, step):
        bit = step[1]
        return {
            o: (block.astype(FULL) + swap(blocks[o ^ bit], step).astype(FULL)).astype(HALF)
            for o, block in blocks.items()
            if not o & bit
        }

    up_keep, up_send, down_keep, down_send = weight_grads
    grad_context = exchange(dict(zip(differences, grad_context)))
    grad_context = jnp.concatenate([grad_context[o] for o in differences], axis=0)
    up_got, down_got, _ = lax.optimization_barrier(
        (swap(up_send, core), swap(down_send, core), grad_context)
    )
    lower, upper = slice(0, half), slice(half, D)
    up_stays, up_low, up_far, up_both = (
        (up_keep[i, rows], up_got[i, rows])
        for i, rows in ((0, lower), (0, upper), (1, lower), (1, upper))
    )
    up_low, up_far, up_both = add(*up_low), add(*up_far), add(*up_both)
    down_keep, down_got = (
        values.reshape(2, 2, 2, D // 4, up_local) for values in (down_keep, down_got)
    )
    down_leaves = add(down_keep[:, :, 1], down_got[:, :, 1])
    grad_qkv_low, grad_offsets = attention_backward(
        info,
        qkv,
        by_offset,
        probs,
        grad_context,
        head_count,
        (up_low, up_far, up_both, down_leaves),
    )
    *up_got, down_got_mid, _ = lax.optimization_barrier(
        (
            swap(up_low, low),
            swap(up_far, far),
            swap_both(up_both, low, far),
            swap(down_leaves, mid),
            grad_qkv_low,
        )
    )
    up_next = add(*up_stays, *up_got)
    down_stays, down_low, down_far, down_both = (
        add(down_keep[i, j, 0], down_got[i, j, 0], down_got_mid[i, j])
        for i, j in ((0, 0), (0, 1), (1, 0), (1, 1))
    )
    qkv_keep, qkv_send, input_parts, grad_normed, grad_vector = tail(
        info,
        grad_qkv_low,
        grad_offsets,
        w_qkv,
        inputs_across,
        normed_across,
        unit_table,
        jnp.asarray(selector.T, dtype=HALF),
        table_order,
        norm_sums,
        grad_bias_up,
        head_count,
        qkv_lanes,
        (up_next, down_low, down_far, down_both),
    )
    up_next = scatter_rows(up_next, dp_steps[1:-1][::-1]).astype(HALF)
    down_next = add(
        down_stays, swap(down_low, low), swap(down_far, far), swap_both(down_both, low, far)
    )
    down_next = scatter_rows(down_next, dp_steps[1:-2][::-1]).astype(HALF)
    qkv_first = add(qkv_keep, swap(qkv_send, low))
    qkv_shard = scatter_rows(qkv_first, dp_steps[:-1][::-1])
    input_both = scatter_rows(input_parts, head_steps[-1:]).astype(HALF)
    input_grad = grad_pre_first + scatter_rows(input_both, head_steps[:-1][::-1])[0]

    vec_lanes = -(-vec_rows // 128) * 128
    grad_vector = jnp.pad(
        grad_vector.reshape(-1)[: device_count * vec_rows].reshape(device_count, vec_rows),
        ((0, 0), (0, vec_lanes - vec_rows)),
    )
    grad_vector = dot(one_hot(owner, 1), grad_vector.astype(HALF)).astype(HALF)
    spare = -(-vec_lanes // table_part // 128) * 128 * table_part
    grad_vector = jnp.pad(grad_vector, ((0, 0), (0, spare - vec_lanes)))
    grad_vector = grad_vector.reshape(device_count * table_part, -1)
    small = jnp.concatenate([grad_normed, grad_vector], axis=1)
    small = scatter_rows(small, small_steps[:2:-1]).astype(HALF)
    small_shard = scatter_rows(small, small_steps[2::-1])
    part = up_next.shape[0] // 2
    up_got, down_got, _, _ = lax.optimization_barrier(
        (
            swap(up_next[part:], dp_steps[0]),
            swap(down_next[D // dp_count :], dp_steps[0]),
            small,
            qkv_first,
        )
    )
    up_out_shard = up_next[:part].astype(FULL) + up_got.astype(FULL)
    down_shard = (down_next[: D // dp_count].astype(FULL) + down_got.astype(FULL)).T
    up_shard = up_out_shard[:, :up_local]
    out_shard = up_out_shard[:, up_local : up_local + local_width].T
    table_shard = standardise_back(small_shard[:, :D] * vector_rows[4], unit_own, inverse_own)
    vector_shard = small_shard[:, D:].reshape(-1)[:vec_rows]

    qkv_grad_shard = jnp.stack(
        [qkv_shard[:, i * local_width : (i + 1) * local_width] for i in range(3)]
    )
    new_qkv = nesterov(
        qkv_weight, qkv_moment, qkv_average, qkv_grad_shard, 0.75 / math.sqrt(D * total_tokens)
    )
    new_out = nesterov(
        out_weight,
        out_moment,
        out_average,
        out_shard,
        0.125 * MAXLEN / math.sqrt(D * total_tokens),
    )
    new_up = nesterov(up_weight, up_moment, up_average, up_shard, 1.1 / math.sqrt(D * total_tokens))
    new_down = nesterov(
        down_weight, down_moment, down_average, down_shard, 1.0 / math.sqrt(FF * total_tokens)
    )
    new_table = nesterov(
        rel_table,
        table_moment,
        table_average,
        table_shard,
        0.55 * math.sqrt(MAXLEN / total_tokens),
    )
    new_vector = nesterov(
        vectors, vector_moment, vector_average, vector_shard, 0.3 / math.sqrt(total_tokens)
    )
    return (output, input_grad) + new_qkv + new_out + new_up + new_down + new_table + new_vector


def solution(mesh):
    rows = P("dp", None)
    owned = P(("dp", "head"), None)
    qkv = P(None, "dp", "head")
    out = P("head", "dp")
    up = P("dp", "head")
    vector = P(("dp", "head"))
    return jax.shard_map(
        per_device,
        mesh=mesh,
        in_specs=(rows,) * 3 + (qkv,) * 3 + (out,) * 3 + (up,) * 3 + (out,) * 3 + (owned,) * 3 + (vector,) * 3,
        out_specs=(owned,) * 2 + (qkv,) * 3 + (out,) * 3 + (up,) * 3 + (out,) * 3 + (owned,) * 3 + (vector,) * 3,
        check_vma=False,
    )
```

```python
import functools
import math

import jax
import jax.numpy as jnp
import numpy as np
from jax import lax
from jax.experimental import pallas as pl
from jax.experimental.pallas import tpu as pltpu
from jax.sharding import PartitionSpec as P

D = 768
HEADS = 12
HD = 64
FF = 3072
BUCKETS = 256
MAXLEN = 512

EPSILON = 1e-07
MOMENTUM = 0.9
DECAY = 0.01
AVERAGE = 0.7
MASKED = -1e30

TILE = 128
NARROW = 5
SCALE = (3.0 * HD) ** -0.5
LOG2E = math.log2(math.e)
HALF = jnp.bfloat16
FULL = jnp.float32
NN = (((1,), (0,)), ((), ()))
NT = (((1,), (1,)), ((), ()))
TN = (((0,), (0,)), ((), ()))


def dot(left, right, dims=NN):
    return lax.dot_general(left, right, dims, preferred_element_type=FULL)


def shear(values, count, low):
    rolled = [
        pltpu.roll(values[:, m * TILE : (m + 1) * TILE], 0, 1, stride=1, stride_axis=0)
        for m in range(count + 1)
    ]
    return jnp.concatenate(
        [jnp.where(low, rolled[m], rolled[m + 1]) for m in range(count)], axis=1
    )


def unshear(values, count, after, shift):
    rolled = [
        pltpu.roll(values[:, m * TILE : (m + 1) * TILE], shift, 1, stride=1, stride_axis=0)
        for m in range(count)
    ]
    zero = jnp.zeros((TILE, TILE), values.dtype)
    return jnp.concatenate(
        [
            jnp.where(
                after, rolled[m] if m < count else zero, rolled[m - 1] if m > 0 else zero
            ).astype(HALF)
            for m in range(count + 1)
        ],
        axis=1,
    )


def flip_matrix():
    across = lax.broadcasted_iota(jnp.int32, (TILE, TILE), 1)
    down = lax.broadcasted_iota(jnp.int32, (TILE, TILE), 0)
    return (across + down == TILE - 1).astype(FULL).astype(HALF)


def tiles_of(block, count=1):
    return pl.ds(pl.multiple_of(block * TILE, TILE), count * TILE)


def sequence_bounds(ends, first, last):
    start, stop = jnp.int32(0), jnp.int32(0)
    begin = jnp.int32(0)
    for end in ends:
        start = jnp.where((begin <= first) & (first < end), begin, start)
        stop = jnp.where((begin <= last) & (last < end), end, stop)
        begin = end
    return start, stop


def by_window(ends, block, tiles, body):
    start, stop = sequence_bounds(ends, block * TILE, block * TILE + TILE - 1)
    first = start // TILE
    narrow = min(NARROW, tiles)
    fits = (stop + TILE - 1) // TILE - first <= narrow

    @pl.when(fits)
    def _():
        body(narrow, jnp.minimum(first, tiles - narrow))

    @pl.when(jnp.logical_not(fits))
    def _():
        body(tiles, jnp.int32(0))


def sequence_ends(info, count):
    ends, total = [], jnp.int32(0)
    for s in range(count):
        total = total + info[s]
        ends.append(total)
    return ends


def sequence_of(places, ends):
    return sum((places >= end).astype(jnp.int32) for end in ends[:-1])


def turned(block, rank, per_owner):
    return ((block // per_owner) ^ rank) * per_owner + block % per_owner


def probs_copy(source, target, sems, block):
    rows = tiles_of(block)
    return pltpu.make_async_copy(source.at[:, rows], target.at[:, rows], sems.at[block])


def forward_kernel(info, qkv_ref, tab_ref, *refs, owners):
    ctx_ref, p_far, q_ref, k_ref, v_ref, qb_ref, kb_ref, p2c_ref, p_ref, sems = refs[-10:]
    heads, tiles = q_ref.shape[0], q_ref.shape[1] // TILE
    segments = info.shape[0] - 1
    rank, per_owner = info[segments], tiles // owners
    ends = sequence_ends(info, segments)
    across = lax.broadcasted_iota(jnp.int32, (TILE, TILE), 1)
    down = lax.broadcasted_iota(jnp.int32, (TILE, TILE), 0)
    low = across < down
    flip = flip_matrix()
    for h in range(heads):
        for i, ref in enumerate((q_ref, k_ref, v_ref)):
            ref[h] = qkv_ref[:, (i * heads + h) * HD : (i * heads + h + 1) * HD]
        for i, ref in enumerate((qb_ref, kb_ref)):
            ref[h] = tab_ref[:, (i * heads + h) * HD : (i * heads + h + 1) * HD]

    def p2c_block(block, carried):
        rows = tiles_of(block)

        def body(count, first):
            offsets = tiles_of(first - block + tiles - 1, count + 1)
            for h in range(heads):
                sheared = shear(dot(k_ref[h, rows, :], qb_ref[h, offsets, :], NT), count, low)
                for m in range(count):
                    p2c_ref[h, tiles_of(first + m), rows] = sheared[
                        :, m * TILE : (m + 1) * TILE
                    ].T

        by_window(ends, block, tiles, body)
        return carried

    lax.fori_loop(0, tiles, p2c_block, 0)

    def score_block(block, carried):
        rows = tiles_of(block)
        row_sequence = sequence_of(down + block * TILE, ends)

        def body(count, first):
            cols = tiles_of(first, count)
            offsets = tiles_of(first - block + tiles - 1, count + 1)
            same = [
                row_sequence == sequence_of(across + (first + m) * TILE, ends) for m in range(count)
            ]
            same = jnp.concatenate(same, axis=1)
            contexts = []
            for h in range(heads):
                query = q_ref[h, rows, :]
                c2p = shear(dot(query, kb_ref[h, offsets, :], NT), count, low)
                raw = dot(query, k_ref[h, cols, :], NT) + c2p + p2c_ref[h, rows, cols]
                scores = jnp.where(same, (SCALE * LOG2E) * raw, MASKED)
                powers = jnp.exp2(scores - jnp.max(scores, axis=1, keepdims=True))
                probs = (powers * (1.0 / jnp.sum(powers, axis=1, keepdims=True))).astype(HALF)
                for m in range(count):
                    p_ref[h, rows, tiles_of(tiles - 1 - first - m)] = dot(
                        probs[:, m * TILE : (m + 1) * TILE], flip
                    ).astype(HALF)
                contexts.append(dot(probs, v_ref[h, cols, :]).astype(HALF))
            ctx_ref[tiles_of(turned(block, rank, per_owner)), :] = jnp.concatenate(contexts, axis=1)

        by_window(ends, block, tiles, body)
        probs_copy(p_ref, p_far, sems, block).start()
        return carried

    lax.fori_loop(0, tiles, score_block, 0)

    def finish(block, carried):
        probs_copy(p_ref, p_far, sems, block).wait()
        return carried

    lax.fori_loop(0, tiles, finish, 0)


def backward_kernel(
    info,
    qkv_ref,
    tab_ref,
    p_far,
    g_ref,
    *refs,
    owners,
):
    dqkv_ref, gtab_ref, q_ref, k_ref, krev_ref, vrev_ref, qbs_ref, kbs_ref = refs[-14:-6]
    grad_ref, dst_ref, dvt_ref, gsum_ref, p_ref, sems = refs[-6:]
    heads, tiles = q_ref.shape[0], q_ref.shape[1] // TILE
    width = heads * HD
    segments = info.shape[0] - 1
    rank, per_owner = info[segments], tiles // owners
    ends = sequence_ends(info, segments)
    across = lax.broadcasted_iota(jnp.int32, (TILE, TILE), 1)
    down = lax.broadcasted_iota(jnp.int32, (TILE, TILE), 0)
    flip = flip_matrix()

    def begin(block, carried):
        probs_copy(p_far, p_ref, sems, block).start()
        return carried

    lax.fori_loop(0, tiles, begin, 0)
    dst_ref[...] = jnp.zeros_like(dst_ref)
    dvt_ref[...] = jnp.zeros_like(dvt_ref)
    gsum_ref[...] = jnp.zeros_like(gsum_ref)
    for h in range(heads):
        q_ref[h] = qkv_ref[:, h * HD : (h + 1) * HD]
        k_ref[h] = qkv_ref[:, width + h * HD : width + (h + 1) * HD]
        qbs_ref[h] = tab_ref[:, h * HD : (h + 1) * HD]
        grad_ref[h] = g_ref[:, h * HD : (h + 1) * HD]
    for m in range(tiles):
        here, there = slice(m * TILE, (m + 1) * TILE), slice((tiles - 1 - m) * TILE, (tiles - m) * TILE)
        turned_rows = dot(flip, qkv_ref[here, width:]).astype(HALF)
        for h in range(heads):
            krev_ref[h, there, :] = turned_rows[:, h * HD : (h + 1) * HD]
            vrev_ref[h, there, :] = turned_rows[:, width + h * HD : width + (h + 1) * HD]
    for m in range(2 * tiles):
        here = slice(m * TILE, (m + 1) * TILE)
        there = slice((2 * tiles - 1 - m) * TILE, (2 * tiles - m) * TILE)
        turned_rows = dot(flip, tab_ref[here, width:]).astype(HALF)
        for h in range(heads):
            kbs_ref[h, there, :] = turned_rows[:, h * HD : (h + 1) * HD]

    def query_block(block, carried):
        rows = tiles_of(block)
        probs_copy(p_far, p_ref, sems, block).wait()

        def body(count, first):
            start = tiles - first - count
            cols = tiles_of(start, count)
            offsets = tiles_of(block + start, count + 1)
            grads = []
            for h in range(heads):
                grad = grad_ref[h, tiles_of(turned(block, rank, per_owner)), :]
                probs_low = p_ref[h, rows, cols]
                probs = probs_low.astype(FULL)
                grad_probs = dot(grad, vrev_ref[h, cols, :], NT)
                inner = jnp.sum(probs * grad_probs, axis=1, keepdims=True)
                grad_raw = (probs * (grad_probs - inner)) * SCALE
                by_offset = unshear(grad_raw, count, across >= down, 0)
                grads.append(
                    (
                        dot(grad_raw.astype(HALF), krev_ref[h, cols, :])
                        + dot(by_offset, kbs_ref[h, offsets, :])
                    ).astype(HALF)
                )
                gsum_ref[heads + h, :, offsets] += dot(
                    q_ref[h, rows, :].astype(FULL).T.astype(HALF), by_offset
                )
                dvt_ref[h, :, cols] += dot(grad.astype(FULL).T.astype(HALF), probs_low)
                for m in range(count):
                    dst_ref[h, tiles_of(start + m), rows] = grad_raw[
                        :, m * TILE : (m + 1) * TILE
                    ].T
            dqkv_ref[rows, :width] = jnp.concatenate(grads, axis=1)

        by_window(ends, block, tiles, body)
        return carried

    lax.fori_loop(0, tiles, query_block, 0)

    def key_block(block, carried):
        rows, back = tiles_of(block), tiles_of(tiles - 1 - block)

        def body(count, first):
            cols = tiles_of(first, count)
            offsets = tiles_of(tiles - 1 - block + first, count + 1)
            grads = []
            for h in range(heads):
                grad_raw = dst_ref[h, back, cols]
                by_offset = unshear(grad_raw, count, across > down, 1)
                grads.append(
                    (
                        dot(grad_raw.astype(HALF), q_ref[h, cols, :])
                        + dot(by_offset, qbs_ref[h, offsets, :])
                    ).astype(HALF)
                )
                gsum_ref[h, :, offsets] += dot(
                    krev_ref[h, back, :].astype(FULL).T.astype(HALF), by_offset
                )
            grads += [dvt_ref[h, :, back].T.astype(HALF) for h in range(heads)]
            dqkv_ref[rows, width:] = dot(flip, jnp.concatenate(grads, axis=1)).astype(HALF)

        by_window(ends, block, tiles, body)
        return carried

    lax.fori_loop(0, tiles, key_block, 0)
    for i in range(heads):
        gtab_ref[i * HD : (i + 1) * HD, :] = gsum_ref[i].astype(HALF)
        for m in range(2 * tiles):
            there = slice((2 * tiles - 1 - m) * TILE, (2 * tiles - m) * TILE)
            gtab_ref[width + i * HD : width + (i + 1) * HD, there] = dot(
                gsum_ref[heads + i, :, m * TILE : (m + 1) * TILE].astype(HALF), flip
            ).astype(HALF)


SMEM_SPEC = pl.BlockSpec(memory_space=pltpu.SMEM)
VMEM_SPEC = pl.BlockSpec(memory_space=pltpu.VMEM)
ANY_SPEC = pl.BlockSpec(memory_space=pl.ANY)


def kernel_cost(microseconds):
    return pl.CostEstimate(
        flops=int(microseconds * 1e9), bytes_accessed=int(microseconds * 1e6), transcendentals=0
    )


def attention_forward(info, qkv, tables, owners, before):
    rows, heads = qkv.shape[0], qkv.shape[1] // (3 * HD)
    small, wide = pltpu.VMEM((heads, rows, HD), HALF), pltpu.VMEM((heads, 2 * rows, HD), HALF)
    return pl.pallas_call(
        functools.partial(forward_kernel, owners=owners),
        out_shape=(
            jax.ShapeDtypeStruct((rows, heads * HD), HALF),
            jax.ShapeDtypeStruct((heads, rows, rows), HALF),
        ),
        in_specs=[SMEM_SPEC] + [VMEM_SPEC] * 2 + [ANY_SPEC] * len(before),
        out_specs=(VMEM_SPEC, ANY_SPEC),
        scratch_shapes=[small] * 3
        + [wide] * 2
        + [
            pltpu.VMEM((heads, rows, rows), FULL),
            pltpu.VMEM((heads, rows, rows), HALF),
            pltpu.SemaphoreType.DMA((rows // TILE,)),
        ],
        compiler_params=pltpu.CompilerParams(vmem_limit_bytes=48 * 2**20),
        cost_estimate=kernel_cost(60),
    )(info, qkv, tables, *before)


def attention_backward(info, qkv, tables, probs, grad, owners, before):
    rows, heads = qkv.shape[0], qkv.shape[1] // (3 * HD)
    shape = jax.ShapeDtypeStruct
    small, wide = pltpu.VMEM((heads, rows, HD), HALF), pltpu.VMEM((heads, 2 * rows, HD), HALF)
    return pl.pallas_call(
        functools.partial(backward_kernel, owners=owners),
        out_shape=(shape(qkv.shape, HALF), shape((2 * heads * HD, 2 * rows), HALF)),
        in_specs=[SMEM_SPEC] + [VMEM_SPEC] * 2
        + [ANY_SPEC, VMEM_SPEC]
        + [ANY_SPEC] * len(before),
        out_specs=(VMEM_SPEC,) * 2,
        scratch_shapes=[small] * 4
        + [wide] * 2
        + [
            small,
            pltpu.VMEM((heads, rows, rows), FULL),
            pltpu.VMEM((heads, HD, rows), FULL),
            pltpu.VMEM((2 * heads, HD, 2 * rows), FULL),
            pltpu.VMEM((heads, rows, rows), HALF),
            pltpu.SemaphoreType.DMA((rows // TILE,)),
        ],
        compiler_params=pltpu.CompilerParams(vmem_limit_bytes=52 * 2**20),
        cost_estimate=kernel_cost(60),
    )(info, qkv, tables, probs, grad, *before)


def standardise(values):
    center = values - jnp.mean(values, axis=-1, keepdims=True)
    spread = jnp.mean(center * center, axis=-1, keepdims=True)
    inverse = lax.rsqrt(spread + EPSILON)
    return center * inverse, inverse


def standardise_back(grad, unit, inverse):
    return inverse * (
        grad
        - jnp.mean(grad, axis=-1, keepdims=True)
        - unit * jnp.mean(grad * unit, axis=-1, keepdims=True)
    )


def exact_dot(values, order, dims):
    high = values.astype(HALF)
    rest = values - high.astype(FULL)
    middle = rest.astype(HALF)
    last = (rest - middle.astype(FULL)).astype(HALF)
    return dot(high, order, dims) + dot(middle, order, dims) + dot(last, order, dims)


def turn(values):
    return values.astype(FULL).T.astype(HALF)


def middle_kernel(info, x_ref, cot_ref, order_ref, vec_ref, bias_ref, *refs):
    heads = bias_ref.shape[0]
    ctx, up_far, down_far = refs[:heads], refs[heads : heads + 8], refs[heads + 8 : heads + 12]
    half, chunk = up_far[0].shape[0], down_far[0].shape[1]
    refs = refs[len(refs) - heads - 16 :]
    out_ref, pre_ref, sums_ref, grad_bias_ref = refs[:4]
    grad_ctx = refs[4 : heads + 4]
    up_keep, up_send, down_keep, down_send = refs[heads + 4 : heads + 8]
    slope_ref, hidden_ref, up, down, grad_up, grad_down, sems_in, sems_out = refs[heads + 8 :]
    wide = bias_ref.shape[1]
    arrivals = [
        [
            pltpu.make_async_copy(
                up_far[4 * (o % 2) + 2 * (o // 2) + i].at[:, lanes],
                up.at[o, i * half : (i + 1) * half, lanes],
                sems_in.at[2 * j + i, o],
            )
            for o in range(heads)
        ]
        for j, lanes in enumerate((slice(wide, up.shape[2]), slice(0, wide)))
        for i in range(2)
    ]
    arrivals += [
        [
            pltpu.make_async_copy(
                down_far[2 * (o % 2) + i % 2].at[2 * (o // 2) + i // 2],
                down.at[o, i * chunk : (i + 1) * chunk],
                sems_in.at[4 + i, o],
            )
            for o in range(heads)
        ]
        for i in range(4)
    ]
    for copies in arrivals[:2]:
        for copy in copies:
            copy.start()
    for o in range(heads):
        for copies in arrivals[2:]:
            copies[o].start()
    departures = []

    def depart(i, o):
        near, keep, send = ((grad_up, up_keep, up_send), (grad_down, down_keep, down_send))[i > 1]
        lanes = (slice(0, wide), slice(wide, grad_up.shape[2]), slice(0, wide))[i]
        copy = pltpu.make_async_copy(
            near.at[o, :, lanes],
            (send if o % 2 else keep).at[o // 2, :, lanes],
            sems_out.at[i, o],
        )
        copy.start()
        departures.append(copy)

    rank = info[info.shape[0] - 1]
    wide = bias_ref.shape[1]
    span = ctx[0].shape[1]
    order = order_ref[...]
    vec = exact_dot(vec_ref[...], order, NT)
    gain1, bias1, gain2, bias2, bias_out, bias_down = (vec[i : i + 1] for i in range(6))

    pre_first = dot(x_ref[...], order, NT) + bias_out
    for o in range(heads):
        arrivals[0][o].wait()
        arrivals[1][o].wait()
        pre_first = pre_first + dot(ctx[o][...], up[o, :, wide : wide + span], NT)
    unit_first, inverse_first = standardise(pre_first)
    first = unit_first * gain1 + bias1
    first_low = first.astype(HALF)
    total = first + bias_down
    for o in range(heads):
        arrivals[2][o].wait()
        arrivals[3][o].wait()
        values = dot(first_low, up[o, :, :wide]) + bias_ref[pl.ds(rank ^ o, 1), :]
        below = 0.5 + 0.5 * lax.erf(values * math.sqrt(0.5))
        hidden = (values * below).astype(HALF)
        hidden_ref[o] = hidden
        slope_ref[o] = below + values * (
            jnp.exp2(values * values * (-0.5 * LOG2E)) * (1.0 / math.sqrt(2.0 * math.pi))
        )
        for copies in arrivals[4:]:
            copies[o].wait()
        total = total + dot(hidden, down[o], NT)
    unit_second, inverse_second = standardise(total)
    out_ref[...] = dot((unit_second * gain2 + bias2).astype(HALF), order).astype(HALF)

    grad_out = dot(cot_ref[...], order, NT)
    grad_second = standardise_back(grad_out * gain2, unit_second, inverse_second)
    grad_down_low = grad_second.astype(HALF)
    grad_down_turned, first_turned = turn(grad_down_low), turn(first_low)
    grad_first = grad_second
    for o in range(heads):
        grad_down[o] = dot(grad_down_turned, hidden_ref[o]).astype(HALF)
        depart(2, o)
        grad_values = (slope_ref[o] * dot(grad_down_low, down[o])).astype(HALF)
        grad_bias_ref[pl.ds(rank ^ o, 1), :] = jnp.sum(
            grad_values.astype(FULL), axis=0, keepdims=True
        )
        grad_up[o, :, :wide] = dot(first_turned, grad_values).astype(HALF)
        depart(0, o)
        grad_first = grad_first + dot(grad_values, up[o, :, :wide], NT)
    grad_pre = standardise_back(grad_first * gain1, unit_first, inverse_first)
    grad_low = grad_pre.astype(HALF)
    grad_turned = turn(grad_low)
    for o in range(heads):
        grad_ctx[o][...] = dot(grad_low, up[o, :, wide : wide + span]).astype(HALF)
        grad_up[o, :, wide : wide + span] = dot(grad_turned, ctx[o][...]).astype(HALF)
        if wide + span < up.shape[2]:
            grad_up[o, :, wide + span :] = jnp.zeros((up.shape[1], up.shape[2] - wide - span), HALF)
        depart(1, o)
    pre_ref[...] = exact_dot(grad_pre, order, NN)
    sums = [
        jnp.sum(part, axis=0, keepdims=True)
        for part in (
            grad_first * unit_first,
            grad_first,
            grad_out * unit_second,
            grad_out,
            grad_pre,
            grad_second,
        )
    ]
    sums_ref[...] = exact_dot(jnp.concatenate(sums + [jnp.zeros_like(sums[0])] * 2, axis=0), order, NN)
    for copy in departures:
        copy.wait()


def middle(info, x, cot, order, vec, bias, ctx, up, down, before):
    heads, (rows, width), wide = len(ctx), x.shape, bias.shape[1]
    up_shape, down_shape = (width, up[0].shape[1]), (width, wide)
    shape = jax.ShapeDtypeStruct
    results = pl.pallas_call(
        middle_kernel,
        out_shape=(
            shape((rows, width), HALF),
            shape((rows, width), FULL),
            shape(vec.shape, FULL),
            shape(bias.shape, FULL),
        )
        + tuple(shape(c.shape, HALF) for c in ctx)
        + tuple(shape((heads // 2,) + w, HALF) for w in (up_shape, up_shape, down_shape, down_shape)),
        in_specs=[SMEM_SPEC] + [VMEM_SPEC] * (5 + heads) + [ANY_SPEC] * (12 + len(before)),
        out_specs=(VMEM_SPEC,) * (4 + heads) + (ANY_SPEC,) * 4,
        scratch_shapes=[pltpu.VMEM((heads, rows, wide), FULL), pltpu.VMEM((heads, rows, wide), HALF)]
        + [pltpu.VMEM((heads,) + w, HALF) for w in (up_shape, down_shape, up_shape, down_shape)]
        + [pltpu.SemaphoreType.DMA((8, heads))] * 2,
        compiler_params=pltpu.CompilerParams(vmem_limit_bytes=48 * 2**20),
        cost_estimate=kernel_cost(20),
    )(info, x, cot, order, vec, bias, *ctx, *up, *down, *before)
    return results[:4] + (results[4 : 4 + heads],) + results[4 + heads :]


def by_row(parts, count):
    row = lax.broadcasted_iota(jnp.int32, (count, parts[0].shape[1]), 0)
    total = jnp.zeros(row.shape, FULL)
    for i, part in enumerate(parts):
        total = jnp.where(row == i, part, total)
    return total


def tail_kernel(
    info,
    dqkv_ref,
    offsets_ref,
    w_ref,
    inputs_ref,
    normed_ref,
    unit_ref,
    selector_ref,
    order_ref,
    norm_sums_ref,
    bias_up_ref,
    *refs,
):
    qkv_keep, qkv_send, parts_ref, normed_grad_ref, vector_ref = refs[-5:]
    rank = info[info.shape[0] - 1]
    width = dqkv_ref.shape[1] // 3
    owners, quarter = parts_ref.shape[:2]
    tables = dot(selector_ref[...], offsets_ref[...], NT).astype(HALF)
    turned_tables = dot(order_ref[...], tables).astype(HALF)
    weights = w_ref[...]
    grad_normed = dot(turned_tables, weights[:, : 2 * width], NT)
    normed_grad_ref[...] = grad_normed.astype(HALF)
    grads = dqkv_ref[...]
    grad_qkv = dot(inputs_ref[...], grads)
    grad_qkv = jnp.concatenate(
        [
            grad_qkv[:, : 2 * width] + dot(normed_ref[...], turned_tables),
            grad_qkv[:, 2 * width :],
        ],
        axis=1,
    ).astype(HALF)
    half = qkv_keep.shape[0]
    for i, ref in enumerate((qkv_keep, qkv_send)):
        ref[:, : 3 * width] = grad_qkv[i * half : (i + 1) * half]
        if 3 * width < ref.shape[1]:
            ref[:, 3 * width :] = jnp.zeros((half, ref.shape[1] - 3 * width), HALF)
    for o in range(owners):
        apart = rank ^ o
        parts_ref[(apart % 2) * (owners // 2) + apart // 2] = dot(
            dqkv_ref[o * quarter : (o + 1) * quarter, :], weights, NT
        ).astype(HALF)
    sums = jnp.sum(grads.astype(FULL), axis=0, keepdims=True)
    table_sums = jnp.sum(turned_tables.astype(FULL), axis=0, keepdims=True)
    sums = jnp.concatenate([sums[:, : 2 * width] + table_sums, sums[:, 2 * width :]], axis=1)
    sums = by_row([sums[:, i * width : (i + 1) * width] for i in range(3)], 8)
    places = (
        lax.broadcasted_iota(jnp.int32, (width, D), 1)
        == lax.broadcasted_iota(jnp.int32, (width, D), 0) + rank * width
    ).astype(FULL).astype(HALF)
    placed = exact_dot(sums, places, NN)
    norm_sums, bias_up = norm_sums_ref[...], bias_up_ref[...]
    parts = [norm_sums[i : i + 1] for i in range(4)]
    parts.append(jnp.sum(grad_normed * unit_ref[...].astype(FULL), axis=0, keepdims=True))
    parts.append(jnp.sum(grad_normed, axis=0, keepdims=True))
    parts += [norm_sums[i : i + 1] for i in range(4, 6)]
    parts += [placed[i : i + 1] for i in range(3)]
    parts += [bias_up[i : i + 1] for i in range(bias_up.shape[0])]
    vector_ref[...] = by_row(parts, vector_ref.shape[0])


def tail(
    info, dqkv, offsets, weights, inputs, normed, unit, selector, order, norm_sums, bias_up,
    owners, lanes, before,
):
    rows, shape = dqkv.shape[0], jax.ShapeDtypeStruct
    return pl.pallas_call(
        tail_kernel,
        out_shape=(
            shape((D // 2, lanes), HALF),
            shape((D // 2, lanes), HALF),
            shape((owners, rows // owners, D), HALF),
            shape(normed.shape[::-1], HALF),
            shape((-(-(11 + bias_up.shape[0]) // 8) * 8, D), FULL),
        ),
        in_specs=[SMEM_SPEC] + [VMEM_SPEC] * 10 + [ANY_SPEC] * len(before),
        out_specs=(VMEM_SPEC,) * 5,
        compiler_params=pltpu.CompilerParams(vmem_limit_bytes=40 * 2**20),
        cost_estimate=kernel_cost(0.1),
    )(info, dqkv, offsets, weights, inputs, normed, unit, selector, order, norm_sums, bias_up, *before)


def index_steps(axis):
    size = lax.axis_size(axis)
    steps, bit = [], size // 2
    while bit >= 1:
        steps.append((axis, bit))
        bit //= 2
    return steps


def swap(values, step):
    axis, bit = step
    return lax.ppermute(values, axis, [(i, i ^ bit) for i in range(lax.axis_size(axis))])


def after(values, *others):
    return lax.optimization_barrier((values,) + others)[0]


def swap_both(values, one, other):
    (axis, bit), (along, place) = one, other
    width = lax.axis_size(along)
    count = lax.axis_size(axis) * width
    return lax.ppermute(
        values, (axis, along), [(i, i ^ (bit * width) ^ place) for i in range(count)]
    )


def gather_blocks(values, steps, layout):
    taken = []
    for step in steps:
        place = sum(1 for other in taken if layout.index(other) < layout.index(step))
        taken.append(step)
        other = swap(values, step)
        values = jnp.concatenate(
            [jnp.expand_dims(values, place), jnp.expand_dims(other, place)], axis=place
        )
    return values


def gather_rows(values, steps):
    for step in steps:
        values = jnp.concatenate([values, swap(values, step)], axis=0)
    return values


def scatter_rows(values, steps):
    kind = values.dtype
    for i, step in enumerate(steps):
        half = values.shape[0] // 2
        values = values[:half].astype(FULL) + swap(values[half:], step).astype(FULL)
        if i < len(steps) - 1:
            values = values.astype(kind)
    return values


def add(*parts):
    return sum(part.astype(FULL) for part in parts).astype(HALF)


def block_owner(rank, steps, axis):
    places = np.arange(2 ** len(steps))
    offsets = sum(
        ((places >> i) & 1) * bit for i, (along, bit) in enumerate(steps) if along == axis
    )
    return jnp.asarray(offsets, jnp.int32) ^ rank


def one_hot(owners, per_block):
    own = (owners[:, None] * per_block + jnp.arange(per_block, dtype=jnp.int32)[None, :]).reshape(-1)
    return (own[:, None] == jnp.arange(own.shape[0], dtype=jnp.int32)[None, :]).astype(HALF)


def bucket_of(offset, buckets, longest):
    middle = buckets // 2
    distance = middle - 1 if abs(offset) < middle else abs(offset)
    sign_of = 1 if offset > 0 else -1 if offset < 0 else 0
    far_bucket = (
        math.ceil(math.log(distance / middle) / math.log((longest - 1) / middle) * (middle - 1))
        + middle
    )
    bucket = offset if distance <= middle else sign_of * far_bucket
    return min(max(bucket + buckets, 0), 2 * buckets - 1)


def offset_selector():
    selector = np.zeros((4 * MAXLEN, 2 * BUCKETS), dtype=np.float32)
    for offset in range(1 - MAXLEN, MAXLEN):
        selector[offset + 2 * MAXLEN - 1, bucket_of(offset, BUCKETS, MAXLEN)] = 1.0
    return selector


def nesterov(weight, moment, average, gradient, step_rate):
    decayed = gradient + DECAY * weight
    moment_new = MOMENTUM * moment + decayed
    weight_new = weight - step_rate * (decayed + MOMENTUM * moment_new)
    average_new = AVERAGE * average + (1.0 - AVERAGE) * weight_new
    return (weight_new, moment_new, average_new)


def column_sums(matrix):
    return jnp.sum(matrix, axis=0, dtype=FULL)


def per_device(
    inputs,
    seg_lengths,
    cotangent,
    qkv_weight,
    qkv_moment,
    qkv_average,
    out_weight,
    out_moment,
    out_average,
    up_weight,
    up_moment,
    up_average,
    down_weight,
    down_moment,
    down_average,
    rel_table,
    table_moment,
    table_average,
    vectors,
    vector_moment,
    vector_average,
):
    tok_rows = inputs.shape[0]
    head_count = lax.axis_size("head")
    dp_count = lax.axis_size("dp")
    head_rank = lax.axis_index("head")
    dp_rank = lax.axis_index("dp")
    local_heads = HEADS // head_count
    local_width = local_heads * HD
    quarter = tok_rows // head_count
    total_tokens = tok_rows * dp_count
    up_local = up_weight.shape[1]
    dp_steps, head_steps = index_steps("dp"), index_steps("head")
    device_count = dp_count * head_count

    width_order = one_hot(block_owner(dp_rank, dp_steps, "dp"), D // dp_count)
    inputs_across = dot(width_order, inputs, NT).astype(HALF)
    qkv_span = 3 * local_width
    qkv_lanes = -(-qkv_span // 128) * 128
    w_qkv_own = jnp.pad(
        jnp.concatenate([qkv_weight[i].astype(HALF) for i in range(3)], axis=1),
        ((0, 0), (0, qkv_lanes - qkv_span)),
    )
    unit_own, inverse_own = standardise(rel_table)
    vec_rows = vectors.shape[0]
    table_part = rel_table.shape[0]
    vec_high = vectors.astype(HALF)
    vec_low = (vectors - vec_high.astype(FULL)).astype(HALF)
    vec_lanes = -(-2 * vec_rows // table_part // 128) * 128
    vec_pack = jnp.pad(
        jnp.concatenate([vec_high, vec_low]), (0, table_part * vec_lanes - 2 * vec_rows)
    ).reshape(table_part, vec_lanes)
    small = jnp.concatenate([unit_own.astype(HALF), vec_pack], axis=1)
    small_steps = dp_steps + head_steps
    both_first = gather_rows(w_qkv_own, dp_steps[:1])
    small = gather_rows(small, small_steps)
    inputs_own, cotangent_own = (
        lax.dynamic_slice_in_dim(values, head_rank * quarter, quarter, 0)
        for values in (inputs, cotangent)
    )
    both_more = gather_rows(both_first, dp_steps[1:-1])
    both_last = swap(both_more, dp_steps[-1])
    w_qkv_turned = jnp.concatenate([both_more, both_last])[:, :qkv_span]
    owner = block_owner(dp_rank, small_steps, "dp") * head_count + block_owner(
        head_rank, small_steps, "head"
    )
    unit_table = small[:, :D]
    vec_used = -(-2 * vec_rows // vec_lanes)
    vec_all = (
        small[:, D:]
        .reshape(device_count, table_part, vec_lanes)[:, :vec_used]
        .reshape(device_count, vec_used * vec_lanes)
    )
    vec_all = dot(one_hot(owner, 1), vec_all, TN)
    vector_full = (vec_all[:, :vec_rows] + vec_all[:, vec_rows : 2 * vec_rows]).reshape(-1)
    vector_rows = vector_full[: 11 * D].reshape(11, D)

    far, core, low, mid = head_steps[0], head_steps[1], dp_steps[-1], dp_steps[-2]
    half = D // 2
    wide_lanes = -(-(up_local + local_width) // 256) * 256
    up_out_own = jnp.pad(
        jnp.concatenate([up_weight, out_weight.T], axis=1).astype(HALF),
        ((0, 0), (0, wide_lanes - up_local - local_width)),
    )
    up_near = gather_rows(up_out_own, dp_steps[:-1])
    up_blocks = [up_near, swap(up_near, low), swap(up_near, far), swap_both(up_near, low, far)]
    up_near_core = swap(up_near, core)
    down_one = gather_rows(after(down_weight.T.astype(HALF), both_more), dp_steps[:-2])
    down_rest = (swap(down_one, low), swap(down_one, far), swap_both(down_one, low, far))
    down_rest, *_ = lax.optimization_barrier((down_rest, both_last, up_near, inputs_across, inputs_own, cotangent_own))
    down_near = jnp.stack([down_one, *down_rest])
    down_far = swap(down_near, mid)
    down_near_core = swap(down_near, core)
    differences = list(range(head_count))

    table_order = one_hot(owner, table_part)
    w_qkv = dot(width_order, w_qkv_turned, TN).astype(HALF)

    def head_part(row_values):
        return lax.dynamic_slice_in_dim(row_values, head_rank * local_width, local_width)

    bias_qkv = jnp.concatenate([head_part(vector_rows[8 + i]) for i in range(3)])
    normed = (unit_table.astype(FULL) * vector_rows[4] + vector_rows[5]).astype(HALF)
    normed_across = dot(width_order, normed, NT).astype(HALF)
    tables = (dot(normed, w_qkv[:, : 2 * local_width]) + bias_qkv[: 2 * local_width]).astype(HALF)
    tables = dot(table_order, tables, TN).astype(HALF)
    selector = offset_selector()[::-1]
    by_offset = dot(jnp.asarray(selector, dtype=HALF), tables).astype(HALF)
    qkv = (dot(inputs, w_qkv) + bias_qkv).astype(HALF)
    info = jnp.concatenate([seg_lengths[0], head_rank[None].astype(jnp.int32)])
    context, probs = attention_forward(info, qkv, by_offset, head_count, (up_near, down_near, unit_table))
    context, up_near_core, down_near_core = lax.optimization_barrier(
        (context, up_near_core, down_near_core)
    )
    def exchange(blocks):
        return {
            o: swap(block, ("head", o)) if o else block for o, block in blocks.items()
        }

    context_low = exchange({o: context[o * quarter : (o + 1) * quarter] for o in differences})
    *up_rest, down_far, _ = lax.optimization_barrier((*up_blocks[1:], down_far, tuple(context_low.values())))
    up_blocks = [up_near] + up_rest + [up_near_core] + [swap(block, core) for block in up_rest]
    down_blocks = [down_near, down_far, down_near_core, swap(down_far, core)]

    vec = jnp.concatenate([vector_rows[:4], vector_rows[6:8], vector_rows[:2]], axis=0)
    bias_up = vector_full[11 * D :].reshape(head_count, up_local)
    output, grad_pre_first, norm_sums, grad_bias_up, grad_context, *weight_grads = middle(
        info,
        inputs_own,
        cotangent_own,
        width_order,
        vec,
        bias_up,
        [context_low[o] for o in differences],
        up_blocks,
        down_blocks,
        (normed_across, table_order),
    )

    def fold(blocks, step):
        bit = step[1]
        return {
            o: (block.astype(FULL) + swap(blocks[o ^ bit], step).astype(FULL)).astype(HALF)
            for o, block in blocks.items()
            if not o & bit
        }

    up_keep, up_send, down_keep, down_send = weight_grads
    grad_context = exchange(dict(zip(differences, grad_context)))
    grad_context = jnp.concatenate([grad_context[o] for o in differences], axis=0)
    up_got, down_got, _ = lax.optimization_barrier(
        (swap(up_send, core), swap(down_send, core), grad_context)
    )
    lower, upper = slice(0, half), slice(half, D)
    up_stays, up_low, up_far, up_both = (
        (up_keep[i, rows], up_got[i, rows])
        for i, rows in ((0, lower), (0, upper), (1, lower), (1, upper))
    )
    up_low, up_far, up_both = add(*up_low), add(*up_far), add(*up_both)
    down_keep, down_got = (
        values.reshape(2, 2, 2, D // 4, up_local) for values in (down_keep, down_got)
    )
    down_leaves = add(down_keep[:, :, 1], down_got[:, :, 1])
    grad_qkv_low, grad_offsets = attention_backward(
        info,
        qkv,
        by_offset,
        probs,
        grad_context,
        head_count,
        (up_low, up_far, up_both, down_leaves),
    )
    *up_got, down_got_mid, _ = lax.optimization_barrier(
        (
            swap(up_low, low),
            swap(up_far, far),
            swap_both(up_both, low, far),
            swap(down_leaves, mid),
            grad_qkv_low,
        )
    )
    up_next = add(*up_stays, *up_got)
    down_stays, down_low, down_far, down_both = (
        add(down_keep[i, j, 0], down_got[i, j, 0], down_got_mid[i, j])
        for i, j in ((0, 0), (0, 1), (1, 0), (1, 1))
    )
    qkv_keep, qkv_send, input_parts, grad_normed, grad_vector = tail(
        info,
        grad_qkv_low,
        grad_offsets,
        w_qkv,
        inputs_across,
        normed_across,
        unit_table,
        jnp.asarray(selector.T, dtype=HALF),
        table_order,
        norm_sums,
        grad_bias_up,
        head_count,
        qkv_lanes,
        (up_next, down_low, down_far, down_both),
    )
    up_next = scatter_rows(up_next, dp_steps[1:-1][::-1]).astype(HALF)
    down_next = add(
        down_stays, swap(down_low, low), swap(down_far, far), swap_both(down_both, low, far)
    )
    down_next = scatter_rows(down_next, dp_steps[1:-2][::-1]).astype(HALF)
    qkv_first = add(qkv_keep, swap(qkv_send, low))
    qkv_shard = scatter_rows(qkv_first, dp_steps[:-1][::-1])
    input_both = scatter_rows(input_parts, head_steps[-1:]).astype(HALF)
    input_grad = grad_pre_first + scatter_rows(input_both, head_steps[:-1][::-1])[0]

    vec_lanes = -(-vec_rows // 128) * 128
    grad_vector = jnp.pad(
        grad_vector.reshape(-1)[: device_count * vec_rows].reshape(device_count, vec_rows),
        ((0, 0), (0, vec_lanes - vec_rows)),
    )
    grad_vector = dot(one_hot(owner, 1), grad_vector.astype(HALF)).astype(HALF)
    spare = -(-vec_lanes // table_part // 128) * 128 * table_part
    grad_vector = jnp.pad(grad_vector, ((0, 0), (0, spare - vec_lanes)))
    grad_vector = grad_vector.reshape(device_count * table_part, -1)
    small = jnp.concatenate([grad_normed, grad_vector], axis=1)
    small = scatter_rows(small, small_steps[:2:-1]).astype(HALF)
    small_shard = scatter_rows(small, small_steps[2::-1])
    part = up_next.shape[0] // 2
    up_got, down_got, _, _ = lax.optimization_barrier(
        (
            swap(up_next[part:], dp_steps[0]),
            swap(down_next[D // dp_count :], dp_steps[0]),
            small,
            qkv_first,
        )
    )
    up_out_shard = up_next[:part].astype(FULL) + up_got.astype(FULL)
    down_shard = (down_next[: D // dp_count].astype(FULL) + down_got.astype(FULL)).T
    up_shard = up_out_shard[:, :up_local]
    out_shard = up_out_shard[:, up_local : up_local + local_width].T
    table_shard = standardise_back(small_shard[:, :D] * vector_rows[4], unit_own, inverse_own)
    vector_shard = small_shard[:, D:].reshape(-1)[:vec_rows]

    qkv_grad_shard = jnp.stack(
        [qkv_shard[:, i * local_width : (i + 1) * local_width] for i in range(3)]
    )
    new_qkv = nesterov(
        qkv_weight, qkv_moment, qkv_average, qkv_grad_shard, 0.75 / math.sqrt(D * total_tokens)
    )
    new_out = nesterov(
        out_weight,
        out_moment,
        out_average,
        out_shard,
        0.125 * MAXLEN / math.sqrt(D * total_tokens),
    )
    new_up = nesterov(up_weight, up_moment, up_average, up_shard, 1.1 / math.sqrt(D * total_tokens))
    new_down = nesterov(
        down_weight, down_moment, down_average, down_shard, 1.0 / math.sqrt(FF * total_tokens)
    )
    new_table = nesterov(
        rel_table,
        table_moment,
        table_average,
        table_shard,
        0.55 * math.sqrt(MAXLEN / total_tokens),
    )
    new_vector = nesterov(
        vectors, vector_moment, vector_average, vector_shard, 0.3 / math.sqrt(total_tokens)
    )
    return (output, input_grad) + new_qkv + new_out + new_up + new_down + new_table + new_vector


def solution(mesh):
    rows = P("dp", None)
    owned = P(("dp", "head"), None)
    qkv = P(None, "dp", "head")
    out = P("head", "dp")
    up = P("dp", "head")
    vector = P(("dp", "head"))
    return jax.shard_map(
        per_device,
        mesh=mesh,
        in_specs=(rows,) * 3 + (qkv,) * 3 + (out,) * 3 + (up,) * 3 + (out,) * 3 + (owned,) * 3 + (vector,) * 3,
        out_specs=(owned,) * 2 + (qkv,) * 3 + (out,) * 3 + (up,) * 3 + (out,) * 3 + (owned,) * 3 + (vector,) * 3,
        check_vma=False,
    )
```

```python
import functools
import math

import jax
import jax.numpy as jnp
import numpy as np
from jax import lax
from jax.experimental import pallas as pl
from jax.experimental.pallas import tpu as pltpu
from jax.sharding import PartitionSpec as P

D = 768
HEADS = 12
HD = 64
FF = 3072
BUCKETS = 256
MAXLEN = 512

EPSILON = 1e-07
MOMENTUM = 0.9
DECAY = 0.01
AVERAGE = 0.7
MASKED = -1e30

TILE = 128
NARROW = 5
SCALE = (3.0 * HD) ** -0.5
LOG2E = math.log2(math.e)
HALF = jnp.bfloat16
FULL = jnp.float32
NN = (((1,), (0,)), ((), ()))
NT = (((1,), (1,)), ((), ()))
TN = (((0,), (0,)), ((), ()))


def dot(left, right, dims=NN):
    return lax.dot_general(left, right, dims, preferred_element_type=FULL)


def shear(values, count, low):
    rolled = [
        pltpu.roll(values[:, m * TILE : (m + 1) * TILE], 0, 1, stride=1, stride_axis=0)
        for m in range(count + 1)
    ]
    return jnp.concatenate(
        [jnp.where(low, rolled[m], rolled[m + 1]) for m in range(count)], axis=1
    )


def unshear(values, count, after, shift):
    rolled = [
        pltpu.roll(values[:, m * TILE : (m + 1) * TILE], shift, 1, stride=1, stride_axis=0)
        for m in range(count)
    ]
    zero = jnp.zeros((TILE, TILE), values.dtype)
    return jnp.concatenate(
        [
            jnp.where(
                after, rolled[m] if m < count else zero, rolled[m - 1] if m > 0 else zero
            ).astype(HALF)
            for m in range(count + 1)
        ],
        axis=1,
    )


def flip_matrix():
    across = lax.broadcasted_iota(jnp.int32, (TILE, TILE), 1)
    down = lax.broadcasted_iota(jnp.int32, (TILE, TILE), 0)
    return (across + down == TILE - 1).astype(FULL).astype(HALF)


def tiles_of(block, count=1):
    return pl.ds(pl.multiple_of(block * TILE, TILE), count * TILE)


def sequence_bounds(ends, first, last):
    start, stop = jnp.int32(0), jnp.int32(0)
    begin = jnp.int32(0)
    for end in ends:
        start = jnp.where((begin <= first) & (first < end), begin, start)
        stop = jnp.where((begin <= last) & (last < end), end, stop)
        begin = end
    return start, stop


def by_window(ends, block, tiles, body):
    start, stop = sequence_bounds(ends, block * TILE, block * TILE + TILE - 1)
    first = start // TILE
    narrow = min(NARROW, tiles)
    fits = (stop + TILE - 1) // TILE - first <= narrow

    @pl.when(fits)
    def _():
        body(narrow, jnp.minimum(first, tiles - narrow))

    @pl.when(jnp.logical_not(fits))
    def _():
        body(tiles, jnp.int32(0))


def sequence_ends(info, count):
    ends, total = [], jnp.int32(0)
    for s in range(count):
        total = total + info[s]
        ends.append(total)
    return ends


def sequence_of(places, ends):
    return sum((places >= end).astype(jnp.int32) for end in ends[:-1])


def turned(block, rank, per_owner):
    return ((block // per_owner) ^ rank) * per_owner + block % per_owner


def probs_copy(source, target, sems, block):
    rows = tiles_of(block)
    return pltpu.make_async_copy(source.at[:, rows], target.at[:, rows], sems.at[block])


def forward_kernel(info, qkv_ref, tab_ref, *refs, owners):
    ctx_ref, p_far, q_ref, k_ref, v_ref, qb_ref, kb_ref, p2c_ref, p_ref, sems = refs[-10:]
    heads, tiles = q_ref.shape[0], q_ref.shape[1] // TILE
    segments = info.shape[0] - 1
    rank, per_owner = info[segments], tiles // owners
    ends = sequence_ends(info, segments)
    across = lax.broadcasted_iota(jnp.int32, (TILE, TILE), 1)
    down = lax.broadcasted_iota(jnp.int32, (TILE, TILE), 0)
    low = across < down
    flip = flip_matrix()
    for h in range(heads):
        for i, ref in enumerate((q_ref, k_ref, v_ref)):
            ref[h] = qkv_ref[:, (i * heads + h) * HD : (i * heads + h + 1) * HD]
        for i, ref in enumerate((qb_ref, kb_ref)):
            ref[h] = tab_ref[:, (i * heads + h) * HD : (i * heads + h + 1) * HD]

    def p2c_block(block, carried):
        rows = tiles_of(block)

        def body(count, first):
            offsets = tiles_of(first - block + tiles - 1, count + 1)
            for h in range(heads):
                sheared = shear(dot(k_ref[h, rows, :], qb_ref[h, offsets, :], NT), count, low)
                for m in range(count):
                    p2c_ref[h, tiles_of(first + m), rows] = sheared[
                        :, m * TILE : (m + 1) * TILE
                    ].T

        by_window(ends, block, tiles, body)
        return carried

    lax.fori_loop(0, tiles, p2c_block, 0)

    def score_block(block, carried):
        rows = tiles_of(block)
        row_sequence = sequence_of(down + block * TILE, ends)

        def body(count, first):
            cols = tiles_of(first, count)
            offsets = tiles_of(first - block + tiles - 1, count + 1)
            same = [
                row_sequence == sequence_of(across + (first + m) * TILE, ends) for m in range(count)
            ]
            same = jnp.concatenate(same, axis=1)
            contexts = []
            for h in range(heads):
                query = q_ref[h, rows, :]
                c2p = shear(dot(query, kb_ref[h, offsets, :], NT), count, low)
                raw = dot(query, k_ref[h, cols, :], NT) + c2p + p2c_ref[h, rows, cols]
                scores = jnp.where(same, (SCALE * LOG2E) * raw, MASKED)
                powers = jnp.exp2(scores - jnp.max(scores, axis=1, keepdims=True))
                probs = (powers * (1.0 / jnp.sum(powers, axis=1, keepdims=True))).astype(HALF)
                for m in range(count):
                    p_ref[h, rows, tiles_of(tiles - 1 - first - m)] = dot(
                        probs[:, m * TILE : (m + 1) * TILE], flip
                    ).astype(HALF)
                contexts.append(dot(probs, v_ref[h, cols, :]).astype(HALF))
            ctx_ref[tiles_of(turned(block, rank, per_owner)), :] = jnp.concatenate(contexts, axis=1)

        by_window(ends, block, tiles, body)
        probs_copy(p_ref, p_far, sems, block).start()
        return carried

    lax.fori_loop(0, tiles, score_block, 0)

    def finish(block, carried):
        probs_copy(p_ref, p_far, sems, block).wait()
        return carried

    lax.fori_loop(0, tiles, finish, 0)


def backward_kernel(
    info,
    qkv_ref,
    tab_ref,
    p_far,
    g_ref,
    *refs,
    owners,
):
    dqkv_ref, gtab_ref, q_ref, k_ref, krev_ref, vrev_ref, qbs_ref, kbs_ref = refs[-14:-6]
    grad_ref, dst_ref, dvt_ref, gsum_ref, p_ref, sems = refs[-6:]
    heads, tiles = q_ref.shape[0], q_ref.shape[1] // TILE
    width = heads * HD
    segments = info.shape[0] - 1
    rank, per_owner = info[segments], tiles // owners
    ends = sequence_ends(info, segments)
    across = lax.broadcasted_iota(jnp.int32, (TILE, TILE), 1)
    down = lax.broadcasted_iota(jnp.int32, (TILE, TILE), 0)
    flip = flip_matrix()

    def begin(block, carried):
        probs_copy(p_far, p_ref, sems, block).start()
        return carried

    lax.fori_loop(0, tiles, begin, 0)
    dst_ref[...] = jnp.zeros_like(dst_ref)
    dvt_ref[...] = jnp.zeros_like(dvt_ref)
    gsum_ref[...] = jnp.zeros_like(gsum_ref)
    for h in range(heads):
        q_ref[h] = qkv_ref[:, h * HD : (h + 1) * HD]
        k_ref[h] = qkv_ref[:, width + h * HD : width + (h + 1) * HD]
        qbs_ref[h] = tab_ref[:, h * HD : (h + 1) * HD]
        grad_ref[h] = g_ref[:, h * HD : (h + 1) * HD]
    for m in range(tiles):
        here, there = slice(m * TILE, (m + 1) * TILE), slice((tiles - 1 - m) * TILE, (tiles - m) * TILE)
        turned_rows = dot(flip, qkv_ref[here, width:]).astype(HALF)
        for h in range(heads):
            krev_ref[h, there, :] = turned_rows[:, h * HD : (h + 1) * HD]
            vrev_ref[h, there, :] = turned_rows[:, width + h * HD : width + (h + 1) * HD]
    for m in range(2 * tiles):
        here = slice(m * TILE, (m + 1) * TILE)
        there = slice((2 * tiles - 1 - m) * TILE, (2 * tiles - m) * TILE)
        turned_rows = dot(flip, tab_ref[here, width:]).astype(HALF)
        for h in range(heads):
            kbs_ref[h, there, :] = turned_rows[:, h * HD : (h + 1) * HD]

    def query_block(block, carried):
        rows = tiles_of(block)
        probs_copy(p_far, p_ref, sems, block).wait()

        def body(count, first):
            start = tiles - first - count
            cols = tiles_of(start, count)
            offsets = tiles_of(block + start, count + 1)
            grads = []
            for h in range(heads):
                grad = grad_ref[h, tiles_of(turned(block, rank, per_owner)), :]
                probs_low = p_ref[h, rows, cols]
                probs = probs_low.astype(FULL)
                grad_probs = dot(grad, vrev_ref[h, cols, :], NT)
                inner = jnp.sum(probs * grad_probs, axis=1, keepdims=True)
                grad_raw = (probs * (grad_probs - inner)) * SCALE
                by_offset = unshear(grad_raw, count, across >= down, 0)
                grads.append(
                    (
                        dot(grad_raw.astype(HALF), krev_ref[h, cols, :])
                        + dot(by_offset, kbs_ref[h, offsets, :])
                    ).astype(HALF)
                )
                gsum_ref[heads + h, :, offsets] += dot(
                    q_ref[h, rows, :].astype(FULL).T.astype(HALF), by_offset
                )
                dvt_ref[h, :, cols] += dot(grad.astype(FULL).T.astype(HALF), probs_low)
                for m in range(count):
                    dst_ref[h, tiles_of(start + m), rows] = grad_raw[
                        :, m * TILE : (m + 1) * TILE
                    ].T
            dqkv_ref[rows, :width] = jnp.concatenate(grads, axis=1)

        by_window(ends, block, tiles, body)
        return carried

    lax.fori_loop(0, tiles, query_block, 0)

    def key_block(block, carried):
        rows, back = tiles_of(block), tiles_of(tiles - 1 - block)

        def body(count, first):
            cols = tiles_of(first, count)
            offsets = tiles_of(tiles - 1 - block + first, count + 1)
            grads = []
            for h in range(heads):
                grad_raw = dst_ref[h, back, cols]
                by_offset = unshear(grad_raw, count, across > down, 1)
                grads.append(
                    (
                        dot(grad_raw.astype(HALF), q_ref[h, cols, :])
                        + dot(by_offset, qbs_ref[h, offsets, :])
                    ).astype(HALF)
                )
                gsum_ref[h, :, offsets] += dot(
                    krev_ref[h, back, :].astype(FULL).T.astype(HALF), by_offset
                )
            grads += [dvt_ref[h, :, back].T.astype(HALF) for h in range(heads)]
            dqkv_ref[rows, width:] = dot(flip, jnp.concatenate(grads, axis=1)).astype(HALF)

        by_window(ends, block, tiles, body)
        return carried

    lax.fori_loop(0, tiles, key_block, 0)
    for i in range(heads):
        gtab_ref[i * HD : (i + 1) * HD, :] = gsum_ref[i].astype(HALF)
        for m in range(2 * tiles):
            there = slice((2 * tiles - 1 - m) * TILE, (2 * tiles - m) * TILE)
            gtab_ref[width + i * HD : width + (i + 1) * HD, there] = dot(
                gsum_ref[heads + i, :, m * TILE : (m + 1) * TILE].astype(HALF), flip
            ).astype(HALF)


SMEM_SPEC = pl.BlockSpec(memory_space=pltpu.SMEM)
VMEM_SPEC = pl.BlockSpec(memory_space=pltpu.VMEM)
ANY_SPEC = pl.BlockSpec(memory_space=pl.ANY)


def kernel_cost(microseconds):
    return pl.CostEstimate(
        flops=int(microseconds * 1e9), bytes_accessed=int(microseconds * 1e6), transcendentals=0
    )


def attention_forward(info, qkv, tables, owners, before):
    rows, heads = qkv.shape[0], qkv.shape[1] // (3 * HD)
    small, wide = pltpu.VMEM((heads, rows, HD), HALF), pltpu.VMEM((heads, 2 * rows, HD), HALF)
    return pl.pallas_call(
        functools.partial(forward_kernel, owners=owners),
        out_shape=(
            jax.ShapeDtypeStruct((rows, heads * HD), HALF),
            jax.ShapeDtypeStruct((heads, rows, rows), HALF),
        ),
        in_specs=[SMEM_SPEC] + [VMEM_SPEC] * 2 + [ANY_SPEC] * len(before),
        out_specs=(VMEM_SPEC, ANY_SPEC),
        scratch_shapes=[small] * 3
        + [wide] * 2
        + [
            pltpu.VMEM((heads, rows, rows), FULL),
            pltpu.VMEM((heads, rows, rows), HALF),
            pltpu.SemaphoreType.DMA((rows // TILE,)),
        ],
        compiler_params=pltpu.CompilerParams(vmem_limit_bytes=48 * 2**20),
        cost_estimate=kernel_cost(60),
    )(info, qkv, tables, *before)


def attention_backward(info, qkv, tables, probs, grad, owners, before):
    rows, heads = qkv.shape[0], qkv.shape[1] // (3 * HD)
    shape = jax.ShapeDtypeStruct
    small, wide = pltpu.VMEM((heads, rows, HD), HALF), pltpu.VMEM((heads, 2 * rows, HD), HALF)
    return pl.pallas_call(
        functools.partial(backward_kernel, owners=owners),
        out_shape=(shape(qkv.shape, HALF), shape((2 * heads * HD, 2 * rows), HALF)),
        in_specs=[SMEM_SPEC] + [VMEM_SPEC] * 2
        + [ANY_SPEC, VMEM_SPEC]
        + [ANY_SPEC] * len(before),
        out_specs=(VMEM_SPEC,) * 2,
        scratch_shapes=[small] * 4
        + [wide] * 2
        + [
            small,
            pltpu.VMEM((heads, rows, rows), FULL),
            pltpu.VMEM((heads, HD, rows), FULL),
            pltpu.VMEM((2 * heads, HD, 2 * rows), FULL),
            pltpu.VMEM((heads, rows, rows), HALF),
            pltpu.SemaphoreType.DMA((rows // TILE,)),
        ],
        compiler_params=pltpu.CompilerParams(vmem_limit_bytes=52 * 2**20),
        cost_estimate=kernel_cost(60),
    )(info, qkv, tables, probs, grad, *before)


def standardise(values):
    center = values - jnp.mean(values, axis=-1, keepdims=True)
    spread = jnp.mean(center * center, axis=-1, keepdims=True)
    inverse = lax.rsqrt(spread + EPSILON)
    return center * inverse, inverse


def standardise_back(grad, unit, inverse):
    return inverse * (
        grad
        - jnp.mean(grad, axis=-1, keepdims=True)
        - unit * jnp.mean(grad * unit, axis=-1, keepdims=True)
    )


def exact_dot(values, order, dims):
    high = values.astype(HALF)
    rest = values - high.astype(FULL)
    middle = rest.astype(HALF)
    last = (rest - middle.astype(FULL)).astype(HALF)
    return dot(high, order, dims) + dot(middle, order, dims) + dot(last, order, dims)


def turn(values):
    return values.astype(FULL).T.astype(HALF)


def middle_kernel(info, x_ref, cot_ref, order_ref, vec_ref, bias_ref, *refs):
    heads = bias_ref.shape[0]
    ctx, up_far, down_far = refs[:heads], refs[heads : heads + 8], refs[heads + 8 : heads + 12]
    half, chunk = up_far[0].shape[0], down_far[0].shape[1]
    refs = refs[len(refs) - heads - 16 :]
    out_ref, pre_ref, sums_ref, grad_bias_ref = refs[:4]
    grad_ctx = refs[4 : heads + 4]
    up_keep, up_send, down_keep, down_send = refs[heads + 4 : heads + 8]
    slope_ref, hidden_ref, up, down, grad_up, grad_down, sems_in, sems_out = refs[heads + 8 :]
    wide = bias_ref.shape[1]
    arrivals = [
        [
            pltpu.make_async_copy(
                up_far[4 * (o % 2) + 2 * (o // 2) + i].at[:, lanes],
                up.at[o, i * half : (i + 1) * half, lanes],
                sems_in.at[2 * j + i, o],
            )
            for o in range(heads)
        ]
        for j, lanes in enumerate((slice(wide, up.shape[2]), slice(0, wide)))
        for i in range(2)
    ]
    arrivals += [
        [
            pltpu.make_async_copy(
                down_far[2 * (o % 2) + i % 2].at[2 * (o // 2) + i // 2],
                down.at[o, i * chunk : (i + 1) * chunk],
                sems_in.at[4 + i, o],
            )
            for o in range(heads)
        ]
        for i in range(4)
    ]
    for copies in arrivals[:2]:
        for copy in copies:
            copy.start()
    for o in range(heads):
        for copies in arrivals[2:]:
            copies[o].start()
    departures = []

    def depart(i, o):
        near, keep, send = ((grad_up, up_keep, up_send), (grad_down, down_keep, down_send))[i > 1]
        lanes = (slice(0, wide), slice(wide, grad_up.shape[2]), slice(0, wide))[i]
        copy = pltpu.make_async_copy(
            near.at[o, :, lanes],
            (send if o % 2 else keep).at[o // 2, :, lanes],
            sems_out.at[i, o],
        )
        copy.start()
        departures.append(copy)

    rank = info[info.shape[0] - 1]
    wide = bias_ref.shape[1]
    span = ctx[0].shape[1]
    order = order_ref[...]
    vec = exact_dot(vec_ref[...], order, NT)
    gain1, bias1, gain2, bias2, bias_out, bias_down = (vec[i : i + 1] for i in range(6))

    pre_first = dot(x_ref[...], order, NT) + bias_out
    for o in range(heads):
        arrivals[0][o].wait()
        arrivals[1][o].wait()
        pre_first = pre_first + dot(ctx[o][...], up[o, :, wide : wide + span], NT)
    unit_first, inverse_first = standardise(pre_first)
    first = unit_first * gain1 + bias1
    first_low = first.astype(HALF)
    total = first + bias_down
    for o in range(heads):
        arrivals[2][o].wait()
        arrivals[3][o].wait()
        values = dot(first_low, up[o, :, :wide]) + bias_ref[pl.ds(rank ^ o, 1), :]
        below = 0.5 + 0.5 * lax.erf(values * math.sqrt(0.5))
        hidden = (values * below).astype(HALF)
        hidden_ref[o] = hidden
        slope_ref[o] = below + values * (
            jnp.exp2(values * values * (-0.5 * LOG2E)) * (1.0 / math.sqrt(2.0 * math.pi))
        )
        for copies in arrivals[4:]:
            copies[o].wait()
        total = total + dot(hidden, down[o], NT)
    unit_second, inverse_second = standardise(total)
    out_ref[...] = dot((unit_second * gain2 + bias2).astype(HALF), order).astype(HALF)

    grad_out = dot(cot_ref[...], order, NT)
    grad_second = standardise_back(grad_out * gain2, unit_second, inverse_second)
    grad_down_low = grad_second.astype(HALF)
    grad_down_turned, first_turned = turn(grad_down_low), turn(first_low)
    grad_first = grad_second
    for o in range(heads):
        grad_down[o] = dot(grad_down_turned, hidden_ref[o]).astype(HALF)
        depart(2, o)
        grad_values = (slope_ref[o] * dot(grad_down_low, down[o])).astype(HALF)
        grad_bias_ref[pl.ds(rank ^ o, 1), :] = jnp.sum(
            grad_values.astype(FULL), axis=0, keepdims=True
        )
        grad_up[o, :, :wide] = dot(first_turned, grad_values).astype(HALF)
        depart(0, o)
        grad_first = grad_first + dot(grad_values, up[o, :, :wide], NT)
    grad_pre = standardise_back(grad_first * gain1, unit_first, inverse_first)
    grad_low = grad_pre.astype(HALF)
    grad_turned = turn(grad_low)
    for o in range(heads):
        grad_ctx[o][...] = dot(grad_low, up[o, :, wide : wide + span]).astype(HALF)
        grad_up[o, :, wide : wide + span] = dot(grad_turned, ctx[o][...]).astype(HALF)
        if wide + span < up.shape[2]:
            grad_up[o, :, wide + span :] = jnp.zeros((up.shape[1], up.shape[2] - wide - span), HALF)
        depart(1, o)
    pre_ref[...] = exact_dot(grad_pre, order, NN)
    sums = [
        jnp.sum(part, axis=0, keepdims=True)
        for part in (
            grad_first * unit_first,
            grad_first,
            grad_out * unit_second,
            grad_out,
            grad_pre,
            grad_second,
        )
    ]
    sums_ref[...] = exact_dot(jnp.concatenate(sums + [jnp.zeros_like(sums[0])] * 2, axis=0), order, NN)
    for copy in departures:
        copy.wait()


def middle(info, x, cot, order, vec, bias, ctx, up, down, before):
    heads, (rows, width), wide = len(ctx), x.shape, bias.shape[1]
    up_shape, down_shape = (width, up[0].shape[1]), (width, wide)
    shape = jax.ShapeDtypeStruct
    results = pl.pallas_call(
        middle_kernel,
        out_shape=(
            shape((rows, width), HALF),
            shape((rows, width), FULL),
            shape(vec.shape, FULL),
            shape(bias.shape, FULL),
        )
        + tuple(shape(c.shape, HALF) for c in ctx)
        + tuple(shape((heads // 2,) + w, HALF) for w in (up_shape, up_shape, down_shape, down_shape)),
        in_specs=[SMEM_SPEC] + [VMEM_SPEC] * (5 + heads) + [ANY_SPEC] * (12 + len(before)),
        out_specs=(VMEM_SPEC,) * (4 + heads) + (ANY_SPEC,) * 4,
        scratch_shapes=[pltpu.VMEM((heads, rows, wide), FULL), pltpu.VMEM((heads, rows, wide), HALF)]
        + [pltpu.VMEM((heads,) + w, HALF) for w in (up_shape, down_shape, up_shape, down_shape)]
        + [pltpu.SemaphoreType.DMA((8, heads))] * 2,
        compiler_params=pltpu.CompilerParams(vmem_limit_bytes=48 * 2**20),
        cost_estimate=kernel_cost(20),
    )(info, x, cot, order, vec, bias, *ctx, *up, *down, *before)
    return results[:4] + (results[4 : 4 + heads],) + results[4 + heads :]


def by_row(parts, count):
    row = lax.broadcasted_iota(jnp.int32, (count, parts[0].shape[1]), 0)
    total = jnp.zeros(row.shape, FULL)
    for i, part in enumerate(parts):
        total = jnp.where(row == i, part, total)
    return total


def tail_kernel(
    info,
    dqkv_ref,
    offsets_ref,
    w_ref,
    inputs_ref,
    normed_ref,
    unit_ref,
    selector_ref,
    order_ref,
    norm_sums_ref,
    bias_up_ref,
    *refs,
):
    qkv_keep, qkv_send, parts_ref, normed_grad_ref, vector_ref = refs[-5:]
    rank = info[info.shape[0] - 1]
    width = dqkv_ref.shape[1] // 3
    owners, quarter = parts_ref.shape[:2]
    tables = dot(selector_ref[...], offsets_ref[...], NT).astype(HALF)
    turned_tables = dot(order_ref[...], tables).astype(HALF)
    weights = w_ref[...]
    grad_normed = dot(turned_tables, weights[:, : 2 * width], NT)
    normed_grad_ref[...] = grad_normed.astype(HALF)
    grads = dqkv_ref[...]
    grad_qkv = dot(inputs_ref[...], grads)
    grad_qkv = jnp.concatenate(
        [
            grad_qkv[:, : 2 * width] + dot(normed_ref[...], turned_tables),
            grad_qkv[:, 2 * width :],
        ],
        axis=1,
    ).astype(HALF)
    half = qkv_keep.shape[0]
    for i, ref in enumerate((qkv_keep, qkv_send)):
        ref[:, : 3 * width] = grad_qkv[i * half : (i + 1) * half]
        if 3 * width < ref.shape[1]:
            ref[:, 3 * width :] = jnp.zeros((half, ref.shape[1] - 3 * width), HALF)
    for o in range(owners):
        apart = rank ^ o
        parts_ref[(apart % 2) * (owners // 2) + apart // 2] = dot(
            dqkv_ref[o * quarter : (o + 1) * quarter, :], weights, NT
        ).astype(HALF)
    sums = jnp.sum(grads.astype(FULL), axis=0, keepdims=True)
    table_sums = jnp.sum(turned_tables.astype(FULL), axis=0, keepdims=True)
    sums = jnp.concatenate([sums[:, : 2 * width] + table_sums, sums[:, 2 * width :]], axis=1)
    sums = by_row([sums[:, i * width : (i + 1) * width] for i in range(3)], 8)
    places = (
        lax.broadcasted_iota(jnp.int32, (width, D), 1)
        == lax.broadcasted_iota(jnp.int32, (width, D), 0) + rank * width
    ).astype(FULL).astype(HALF)
    placed = exact_dot(sums, places, NN)
    norm_sums, bias_up = norm_sums_ref[...], bias_up_ref[...]
    parts = [norm_sums[i : i + 1] for i in range(4)]
    parts.append(jnp.sum(grad_normed * unit_ref[...].astype(FULL), axis=0, keepdims=True))
    parts.append(jnp.sum(grad_normed, axis=0, keepdims=True))
    parts += [norm_sums[i : i + 1] for i in range(4, 6)]
    parts += [placed[i : i + 1] for i in range(3)]
    parts += [bias_up[i : i + 1] for i in range(bias_up.shape[0])]
    vector_ref[...] = by_row(parts, vector_ref.shape[0])


def tail(
    info, dqkv, offsets, weights, inputs, normed, unit, selector, order, norm_sums, bias_up,
    owners, lanes, before,
):
    rows, shape = dqkv.shape[0], jax.ShapeDtypeStruct
    return pl.pallas_call(
        tail_kernel,
        out_shape=(
            shape((D // 2, lanes), HALF),
            shape((D // 2, lanes), HALF),
            shape((owners, rows // owners, D), HALF),
            shape(normed.shape[::-1], HALF),
            shape((-(-(11 + bias_up.shape[0]) // 8) * 8, D), FULL),
        ),
        in_specs=[SMEM_SPEC] + [VMEM_SPEC] * 10 + [ANY_SPEC] * len(before),
        out_specs=(VMEM_SPEC,) * 5,
        compiler_params=pltpu.CompilerParams(vmem_limit_bytes=40 * 2**20),
        cost_estimate=kernel_cost(0.1),
    )(info, dqkv, offsets, weights, inputs, normed, unit, selector, order, norm_sums, bias_up, *before)


def index_steps(axis):
    size = lax.axis_size(axis)
    steps, bit = [], size // 2
    while bit >= 1:
        steps.append((axis, bit))
        bit //= 2
    return steps


def swap(values, step):
    axis, bit = step
    return lax.ppermute(values, axis, [(i, i ^ bit) for i in range(lax.axis_size(axis))])


def after(values, *others):
    return lax.optimization_barrier((values,) + others)[0]


def swap_both(values, one, other):
    (axis, bit), (along, place) = one, other
    width = lax.axis_size(along)
    count = lax.axis_size(axis) * width
    return lax.ppermute(
        values, (axis, along), [(i, i ^ (bit * width) ^ place) for i in range(count)]
    )


def gather_blocks(values, steps, layout):
    taken = []
    for step in steps:
        place = sum(1 for other in taken if layout.index(other) < layout.index(step))
        taken.append(step)
        other = swap(values, step)
        values = jnp.concatenate(
            [jnp.expand_dims(values, place), jnp.expand_dims(other, place)], axis=place
        )
    return values


def gather_rows(values, steps):
    for step in steps:
        values = jnp.concatenate([values, swap(values, step)], axis=0)
    return values


def scatter_rows(values, steps):
    kind = values.dtype
    for i, step in enumerate(steps):
        half = values.shape[0] // 2
        values = values[:half].astype(FULL) + swap(values[half:], step).astype(FULL)
        if i < len(steps) - 1:
            values = values.astype(kind)
    return values


def add(*parts):
    return sum(part.astype(FULL) for part in parts).astype(HALF)


def block_owner(rank, steps, axis):
    places = np.arange(2 ** len(steps))
    offsets = sum(
        ((places >> i) & 1) * bit for i, (along, bit) in enumerate(steps) if along == axis
    )
    return jnp.asarray(offsets, jnp.int32) ^ rank


def one_hot(owners, per_block):
    own = (owners[:, None] * per_block + jnp.arange(per_block, dtype=jnp.int32)[None, :]).reshape(-1)
    return (own[:, None] == jnp.arange(own.shape[0], dtype=jnp.int32)[None, :]).astype(HALF)


def bucket_of(offset, buckets, longest):
    middle = buckets // 2
    distance = middle - 1 if abs(offset) < middle else abs(offset)
    sign_of = 1 if offset > 0 else -1 if offset < 0 else 0
    far_bucket = (
        math.ceil(math.log(distance / middle) / math.log((longest - 1) / middle) * (middle - 1))
        + middle
    )
    bucket = offset if distance <= middle else sign_of * far_bucket
    return min(max(bucket + buckets, 0), 2 * buckets - 1)


def offset_selector():
    selector = np.zeros((4 * MAXLEN, 2 * BUCKETS), dtype=np.float32)
    for offset in range(1 - MAXLEN, MAXLEN):
        selector[offset + 2 * MAXLEN - 1, bucket_of(offset, BUCKETS, MAXLEN)] = 1.0
    return selector


def nesterov(weight, moment, average, gradient, step_rate):
    decayed = gradient + DECAY * weight
    moment_new = MOMENTUM * moment + decayed
    weight_new = weight - step_rate * (decayed + MOMENTUM * moment_new)
    average_new = AVERAGE * average + (1.0 - AVERAGE) * weight_new
    return (weight_new, moment_new, average_new)


def column_sums(matrix):
    return jnp.sum(matrix, axis=0, dtype=FULL)


def per_device(
    inputs,
    seg_lengths,
    cotangent,
    qkv_weight,
    qkv_moment,
    qkv_average,
    out_weight,
    out_moment,
    out_average,
    up_weight,
    up_moment,
    up_average,
    down_weight,
    down_moment,
    down_average,
    rel_table,
    table_moment,
    table_average,
    vectors,
    vector_moment,
    vector_average,
):
    tok_rows = inputs.shape[0]
    head_count = lax.axis_size("head")
    dp_count = lax.axis_size("dp")
    head_rank = lax.axis_index("head")
    dp_rank = lax.axis_index("dp")
    local_heads = HEADS // head_count
    local_width = local_heads * HD
    quarter = tok_rows // head_count
    total_tokens = tok_rows * dp_count
    up_local = up_weight.shape[1]
    dp_steps, head_steps = index_steps("dp"), index_steps("head")
    device_count = dp_count * head_count

    width_order = one_hot(block_owner(dp_rank, dp_steps, "dp"), D // dp_count)
    inputs_across = dot(width_order, inputs, NT).astype(HALF)
    qkv_span = 3 * local_width
    qkv_lanes = -(-qkv_span // 128) * 128
    w_qkv_own = jnp.pad(
        jnp.concatenate([qkv_weight[i].astype(HALF) for i in range(3)], axis=1),
        ((0, 0), (0, qkv_lanes - qkv_span)),
    )
    unit_own, inverse_own = standardise(rel_table)
    vec_rows = vectors.shape[0]
    table_part = rel_table.shape[0]
    vec_high = vectors.astype(HALF)
    vec_low = (vectors - vec_high.astype(FULL)).astype(HALF)
    vec_lanes = -(-2 * vec_rows // table_part // 128) * 128
    vec_pack = jnp.pad(
        jnp.concatenate([vec_high, vec_low]), (0, table_part * vec_lanes - 2 * vec_rows)
    ).reshape(table_part, vec_lanes)
    small = jnp.concatenate([unit_own.astype(HALF), vec_pack], axis=1)
    small_steps = dp_steps + head_steps
    both_first = gather_rows(w_qkv_own, dp_steps[:1])
    small = gather_rows(small, small_steps)
    inputs_own, cotangent_own = (
        lax.dynamic_slice_in_dim(values, head_rank * quarter, quarter, 0)
        for values in (inputs, cotangent)
    )
    both_more = gather_rows(both_first, dp_steps[1:-1])
    both_last = swap(both_more, dp_steps[-1])
    w_qkv_turned = jnp.concatenate([both_more, both_last])[:, :qkv_span]
    owner = block_owner(dp_rank, small_steps, "dp") * head_count + block_owner(
        head_rank, small_steps, "head"
    )
    unit_table = small[:, :D]
    vec_used = -(-2 * vec_rows // vec_lanes)
    vec_all = (
        small[:, D:]
        .reshape(device_count, table_part, vec_lanes)[:, :vec_used]
        .reshape(device_count, vec_used * vec_lanes)
    )
    vec_all = dot(one_hot(owner, 1), vec_all, TN)
    vector_full = (vec_all[:, :vec_rows] + vec_all[:, vec_rows : 2 * vec_rows]).reshape(-1)
    vector_rows = vector_full[: 11 * D].reshape(11, D)

    far, core, low, mid = head_steps[0], head_steps[1], dp_steps[-1], dp_steps[-2]
    half = D // 2
    wide_lanes = -(-(up_local + local_width) // 256) * 256
    up_out_own = jnp.pad(
        jnp.concatenate([up_weight, out_weight.T], axis=1).astype(HALF),
        ((0, 0), (0, wide_lanes - up_local - local_width)),
    )
    up_near = gather_rows(up_out_own, dp_steps[:-1])
    up_blocks = [up_near, swap(up_near, low), swap(up_near, far), swap_both(up_near, low, far)]
    up_near_core = swap(up_near, core)
    down_one = gather_rows(after(down_weight.T.astype(HALF), both_more), dp_steps[:-2])
    down_rest = (swap(down_one, low), swap(down_one, far), swap_both(down_one, low, far))
    down_rest, *_ = lax.optimization_barrier((down_rest, both_last, up_near, inputs_across, inputs_own, cotangent_own))
    down_near = jnp.stack([down_one, *down_rest])
    down_far = swap(down_near, mid)
    down_near_core = swap(down_near, core)
    differences = list(range(head_count))

    table_order = one_hot(owner, table_part)
    w_qkv = dot(width_order, w_qkv_turned, TN).astype(HALF)

    def head_part(row_values):
        return lax.dynamic_slice_in_dim(row_values, head_rank * local_width, local_width)

    bias_qkv = jnp.concatenate([head_part(vector_rows[8 + i]) for i in range(3)])
    normed = (unit_table.astype(FULL) * vector_rows[4] + vector_rows[5]).astype(HALF)
    normed_across = dot(width_order, normed, NT).astype(HALF)
    tables = (dot(normed, w_qkv[:, : 2 * local_width]) + bias_qkv[: 2 * local_width]).astype(HALF)
    tables = dot(table_order, tables, TN).astype(HALF)
    selector = offset_selector()[::-1]
    by_offset = dot(jnp.asarray(selector, dtype=HALF), tables).astype(HALF)
    qkv = (dot(inputs, w_qkv) + bias_qkv).astype(HALF)
    info = jnp.concatenate([seg_lengths[0], head_rank[None].astype(jnp.int32)])
    context, probs = attention_forward(info, qkv, by_offset, head_count, (up_near, down_near, unit_table))
    context, up_near_core, down_near_core = lax.optimization_barrier(
        (context, up_near_core, down_near_core)
    )
    def exchange(blocks):
        return {
            o: swap(block, ("head", o)) if o else block for o, block in blocks.items()
        }

    context_low = exchange({o: context[o * quarter : (o + 1) * quarter] for o in differences})
    *up_rest, down_far, _ = lax.optimization_barrier((*up_blocks[1:], down_far, tuple(context_low.values())))
    up_blocks = [up_near] + up_rest + [up_near_core] + [swap(block, core) for block in up_rest]
    down_blocks = [down_near, down_far, down_near_core, swap(down_far, core)]

    vec = jnp.concatenate([vector_rows[:4], vector_rows[6:8], vector_rows[:2]], axis=0)
    bias_up = vector_full[11 * D :].reshape(head_count, up_local)
    output, grad_pre_first, norm_sums, grad_bias_up, grad_context, *weight_grads = middle(
        info,
        inputs_own,
        cotangent_own,
        width_order,
        vec,
        bias_up,
        [context_low[o] for o in differences],
        up_blocks,
        down_blocks,
        (normed_across, table_order),
    )

    def fold(blocks, step):
        bit = step[1]
        return {
            o: (block.astype(FULL) + swap(blocks[o ^ bit], step).astype(FULL)).astype(HALF)
            for o, block in blocks.items()
            if not o & bit
        }

    up_keep, up_send, down_keep, down_send = weight_grads
    grad_context = exchange(dict(zip(differences, grad_context)))
    grad_context = jnp.concatenate([grad_context[o] for o in differences], axis=0)
    up_got, down_got, _ = lax.optimization_barrier(
        (swap(up_send, core), swap(down_send, core), grad_context[:quarter])
    )
    lower, upper = slice(0, half), slice(half, D)
    up_stays, up_low, up_far, up_both = (
        (up_keep[i, rows], up_got[i, rows])
        for i, rows in ((0, lower), (0, upper), (1, lower), (1, upper))
    )
    up_low, up_far, up_both = add(*up_low), add(*up_far), add(*up_both)
    down_keep, down_got = (
        values.reshape(2, 2, 2, D // 4, up_local) for values in (down_keep, down_got)
    )
    down_leaves = add(down_keep[:, :, 1], down_got[:, :, 1])
    grad_qkv_low, grad_offsets = attention_backward(
        info,
        qkv,
        by_offset,
        probs,
        grad_context,
        head_count,
        (up_low, up_far, up_both, down_leaves),
    )
    *up_got, down_got_mid, _ = lax.optimization_barrier(
        (
            swap(up_low, low),
            swap(up_far, far),
            swap_both(up_both, low, far),
            swap(down_leaves, mid),
            grad_qkv_low,
        )
    )
    up_next = add(*up_stays, *up_got)
    down_stays, down_low, down_far, down_both = (
        add(down_keep[i, j, 0], down_got[i, j, 0], down_got_mid[i, j])
        for i, j in ((0, 0), (0, 1), (1, 0), (1, 1))
    )
    qkv_keep, qkv_send, input_parts, grad_normed, grad_vector = tail(
        info,
        grad_qkv_low,
        grad_offsets,
        w_qkv,
        inputs_across,
        normed_across,
        unit_table,
        jnp.asarray(selector.T, dtype=HALF),
        table_order,
        norm_sums,
        grad_bias_up,
        head_count,
        qkv_lanes,
        (up_next, down_low, down_far, down_both),
    )
    up_next = scatter_rows(up_next, dp_steps[1:-1][::-1]).astype(HALF)
    down_next = add(
        down_stays, swap(down_low, low), swap(down_far, far), swap_both(down_both, low, far)
    )
    down_next = scatter_rows(down_next, dp_steps[1:-2][::-1]).astype(HALF)
    qkv_first = add(qkv_keep, swap(qkv_send, low))
    qkv_shard = scatter_rows(qkv_first, dp_steps[:-1][::-1])
    input_both = scatter_rows(input_parts, head_steps[-1:]).astype(HALF)
    input_grad = grad_pre_first + scatter_rows(input_both, head_steps[:-1][::-1])[0]

    vec_lanes = -(-vec_rows // 128) * 128
    grad_vector = jnp.pad(
        grad_vector.reshape(-1)[: device_count * vec_rows].reshape(device_count, vec_rows),
        ((0, 0), (0, vec_lanes - vec_rows)),
    )
    grad_vector = dot(one_hot(owner, 1), grad_vector.astype(HALF)).astype(HALF)
    spare = -(-vec_lanes // table_part // 128) * 128 * table_part
    grad_vector = jnp.pad(grad_vector, ((0, 0), (0, spare - vec_lanes)))
    grad_vector = grad_vector.reshape(device_count * table_part, -1)
    small = jnp.concatenate([grad_normed, grad_vector], axis=1)
    small = scatter_rows(small, small_steps[:2:-1]).astype(HALF)
    small_shard = scatter_rows(small, small_steps[2::-1])
    part = up_next.shape[0] // 2
    up_got, down_got, _, _ = lax.optimization_barrier(
        (
            swap(up_next[part:], dp_steps[0]),
            swap(down_next[D // dp_count :], dp_steps[0]),
            small,
            qkv_first,
        )
    )
    up_out_shard = up_next[:part].astype(FULL) + up_got.astype(FULL)
    down_shard = (down_next[: D // dp_count].astype(FULL) + down_got.astype(FULL)).T
    up_shard = up_out_shard[:, :up_local]
    out_shard = up_out_shard[:, up_local : up_local + local_width].T
    table_shard = standardise_back(small_shard[:, :D] * vector_rows[4], unit_own, inverse_own)
    vector_shard = small_shard[:, D:].reshape(-1)[:vec_rows]

    qkv_grad_shard = jnp.stack(
        [qkv_shard[:, i * local_width : (i + 1) * local_width] for i in range(3)]
    )
    new_qkv = nesterov(
        qkv_weight, qkv_moment, qkv_average, qkv_grad_shard, 0.75 / math.sqrt(D * total_tokens)
    )
    new_out = nesterov(
        out_weight,
        out_moment,
        out_average,
        out_shard,
        0.125 * MAXLEN / math.sqrt(D * total_tokens),
    )
    new_up = nesterov(up_weight, up_moment, up_average, up_shard, 1.1 / math.sqrt(D * total_tokens))
    new_down = nesterov(
        down_weight, down_moment, down_average, down_shard, 1.0 / math.sqrt(FF * total_tokens)
    )
    new_table = nesterov(
        rel_table,
        table_moment,
        table_average,
        table_shard,
        0.55 * math.sqrt(MAXLEN / total_tokens),
    )
    new_vector = nesterov(
        vectors, vector_moment, vector_average, vector_shard, 0.3 / math.sqrt(total_tokens)
    )
    return (output, input_grad) + new_qkv + new_out + new_up + new_down + new_table + new_vector


def solution(mesh):
    rows = P("dp", None)
    owned = P(("dp", "head"), None)
    qkv = P(None, "dp", "head")
    out = P("head", "dp")
    up = P("dp", "head")
    vector = P(("dp", "head"))
    return jax.shard_map(
        per_device,
        mesh=mesh,
        in_specs=(rows,) * 3 + (qkv,) * 3 + (out,) * 3 + (up,) * 3 + (out,) * 3 + (owned,) * 3 + (vector,) * 3,
        out_specs=(owned,) * 2 + (qkv,) * 3 + (out,) * 3 + (up,) * 3 + (out,) * 3 + (owned,) * 3 + (vector,) * 3,
        check_vma=False,
    )
```
